512 devices in a mesh: freq: 16 (over z, core), src: 32 (over x, y).
Axes of the slice: x: 4, y: 8, z: 8, core: 2. Of those that a mesh axis runs over, the one named last changes fastest.
Arguments:
- data: bfloat16 [2, 16, 128, 98304], P(None, 'freq', None, 'src'), may hold values from -6 to 6
- recip: bfloat16 [2, 16, 128, 512], P(None, 'freq', None, 'src'), may hold values from -6 to 6
- gap: int32 [128, 512], P(None, 'src'), may hold values 0 or 1
- owner: int32 [32], replicated, may hold values from 0 to 31, as said below
- weights: bfloat16 [2, 16, 98304, 256], P(None, 'freq', 'src'), may hold values from -0.02734375 to 0.02734375
- start_row: int32 [16], P('freq'), may hold values from 0 to 480, as said below
- end_row: int32 [16], P('freq'), may hold values from 32 to 512, as said below
- recorded: bfloat16 [768, 256, 128], P('freq', 'src'), may hold values from -6 to 6
Outputs:
- primaries: bfloat16 [768, 256, 128], P('freq', 'src')
- filters: float32 [16, 27], P('freq')
The draws below stay inside these ranges and needn't reach their ends.
Inputs may be any that keep to these rules, and one draw needn't show every extreme that they name: `owner`: a permutation: each block is named by exactly one src index. `start_row`: start of window i lies between i * 32 - 8 and i * 32, never before 0; window 1 starts exactly 8 early. `end_row`: end of window i lies between (i + 1) * 32 and (i + 1) * 32 + 8, never after 512; window 1 ends exactly 8 late.
All inputs are finite; a program needn't handle non-finite values. No bound on the sum of `gap` on one device may be relied on, other than what follows from the above.
Results may differ from the reference program's by a relative error of at most 0.001.
Values may be sent and summed in bfloat16 or wider, within the bound.
No kernel may reach another device: no remote copies, remote signals or barrier semaphores. Data moves between devices by JAX's collectives and lax.ppermute only.
A program may use at most 64 MiB of HBM per device.

```python
import math
import jax
import jax.numpy as jnp
from jax import lax

RECV = 128
NFFT = 512
F_LOW = 40
K_DEV = 3072
T_DEV = 32
NEAR = 16
HALO = 8
LAGS_T = 9
LAGS_X = 3
NF = 16
KTOT = 98304
SOUT = 256
NT = 512
WROWS = 48
NU = 27
N_FREQ = 16
N_SRC = 32


def window_bounds(key):
    early = jax.random.randint(jax.random.fold_in(key, 11), (N_FREQ,), 0, HALO + 1)
    late = jax.random.randint(jax.random.fold_in(key, 12), (N_FREQ,), 0, HALO + 1)
    index = jnp.arange(N_FREQ, dtype=jnp.int32)
    early = jnp.where(index == 1, HALO, early)
    late = jnp.where(index == 1, HALO, late)
    first = jnp.maximum(index * T_DEV - early, 0)
    last = jnp.minimum((index + 1) * T_DEV + late, T_DEV * N_FREQ)
    return (first.astype(jnp.int32), last.astype(jnp.int32))


def draw_start_row(key, part):
    first, last = window_bounds(key)
    return first


def draw_end_row(key, part):
    first, last = window_bounds(key)
    return last


def draw_owner(key, part):
    key = jax.random.fold_in(key, 21)
    anchor = jax.random.randint(jax.random.fold_in(key, 1), (), 0, N_SRC).astype(jnp.int32)
    ranks = jax.random.permutation(jax.random.fold_in(key, 2), N_SRC).astype(jnp.int32) + 3
    index = jnp.arange(N_SRC, dtype=jnp.int32)
    second = (anchor + 1) % N_SRC
    third = (anchor + 1 + N_SRC // 2) % N_SRC
    ranks = jnp.where(index == anchor, 0, ranks)
    ranks = jnp.where(index == second, 1, ranks)
    ranks = jnp.where(index == third, 2, ranks)
    order = jnp.argsort(ranks, stable=True).astype(jnp.int32)
    after = jnp.roll(order, -1)
    return jnp.zeros((N_SRC,), jnp.int32).at[order].set(after)


def place_ends(result, stream_key, least, high):
    index_at = [jax.random.randint(jax.random.fold_in(stream_key, axis), (), 0, length) for axis, length in enumerate(result.shape)]
    main_axis = result.shape.index(max(result.shape))
    neighbour = index_at[:main_axis] + [(index_at[main_axis] + 1) % result.shape[main_axis]] + index_at[main_axis + 1:]
    return result.at[tuple(index_at)].set(least).at[tuple(neighbour)].set(high)


def raised(array, rng, source, target, blocks, factor):
    def block_of(axis_at):
        return (jnp.arange(array.shape[axis_at]) // (array.shape[axis_at] // blocks)).reshape((-1,) + (1,) * (array.ndim - 1 - axis_at))

    first = jax.random.permutation(rng, blocks)[block_of(target)]
    second = (block_of(target) + blocks // 2) % blocks
    return jnp.where((block_of(source) == first) | (block_of(source) == second), factor * array, array)


def block_scale(key, extent, split, smallest, high):
    loudness, own = 1.0, jax.random.fold_in(key, 6)
    for axis_at, parts in split:
        draws = jnp.exp(jax.random.uniform(jax.random.fold_in(own, axis_at), (parts,), jnp.float32, smallest / len(split), high / len(split)))
        loudness = loudness * jnp.repeat(draws, extent[axis_at] // parts).reshape([-1 if axis == axis_at else 1 for axis in range(len(extent))])
    return loudness


def centred(rng, dims, spread, limit, cuts=(), kind=jnp.bfloat16):
    values = spread * jax.random.normal(rng, dims, jnp.float32)
    if cuts:
        values = values * block_scale(rng, dims, cuts, -0.22, 0.18)
    return jnp.clip(values, -limit, limit).astype(kind)


def noise_with(stream_key, extent, spread, reach, cuts, heavy, held_as=jnp.bfloat16):
    result = spread * jax.random.normal(stream_key, extent, jnp.float32)
    if cuts:
        result = result * block_scale(stream_key, extent, cuts, -0.22, 0.18)
    return jnp.clip(raised(result, jax.random.fold_in(stream_key, 3), *heavy), -reach, reach).astype(held_as)


def setup_inputs(seed: int = 0) -> dict:
    seeds = jax.random.split(jax.random.key(seed), 9)
    return {
        "data": centred(seeds[0], (2, NF, RECV, KTOT), 1.0, 6.0, ((1, 16), (3, 32))),
        "recip": centred(seeds[1], (2, NF, RECV, NEAR * N_SRC), 1.0, 6.0, ((1, 16), (3, 32))),
        "gap": place_ends((jax.random.randint(seeds[2], (RECV, NEAR * N_SRC), 0, 2) < 1).astype(jnp.int32), jax.random.fold_in(seeds[2], 1), 0, 1),
        "owner": draw_owner(jax.random.fold_in(seeds[8], 71), 0),
        "weights": noise_with(seeds[4], (2, NF, KTOT, SOUT), (2 * KTOT) ** -0.5, 0.02734375, ((1, 16), (2, 32)), (2, 3, 32, 2.75)),
        "start_row": draw_start_row(jax.random.fold_in(seeds[8], 71), 0),
        "end_row": draw_end_row(jax.random.fold_in(seeds[8], 71), 0),
        "recorded": centred(seeds[7], (N_FREQ * WROWS, SOUT, RECV), 1.0, 6.0, ((0, 16), (1, 32))),
    }


def phase_tables(times, freqs):
    turns = (F_LOW + freqs)[None, :] * times[:, None] % NFFT
    angle = turns.astype(jnp.float32) * (2.0 * math.pi / NFFT)
    return (jnp.cos(angle), jnp.sin(angle))

def shifted_stack(masked, keep):
    lead = LAGS_T // 2
    side = LAGS_X // 2
    padded = jnp.pad(masked, ((lead, lead), (0, 0), (side, side)))
    height = masked.shape[0]
    width = masked.shape[2]
    pieces = [padded[LAGS_T - 1 - a:LAGS_T - 1 - a + height, :, LAGS_X - 1 - b:LAGS_X - 1 - b + width] for a in range(LAGS_T) for b in range(LAGS_X)]
    return jnp.stack(pieces) * keep[None, :, None, None]

def solve_filter(gram, rhs, damping):
    count = gram.shape[0]
    centre = LAGS_T // 2 * LAGS_X + LAGS_X // 2
    unit = (jnp.arange(count) == centre).astype(jnp.float32)
    eye = jnp.eye(count, dtype=jnp.float32)
    factor = jnp.linalg.cholesky(gram + damping * eye)
    return jax.scipy.linalg.cho_solve((factor, True), rhs + damping * unit)

def fill_panel(data, recip, gap, owner):
    blocks = data.reshape(2, NF, RECV, N_SRC, K_DEV)
    pieces = recip.reshape(2, NF, RECV, N_SRC, NEAR)
    filled = jnp.zeros_like(pieces).at[:, :, :, owner, :].set(pieces)
    missing = (gap.reshape(RECV, N_SRC, NEAR) == 1)[None, None]
    near = jnp.where(missing, filled, blocks[..., :NEAR])
    blocks = jnp.concatenate([near, blocks[..., NEAR:]], axis=4)
    return blocks.reshape(2, NF, RECV, KTOT)

def reference(data, recip, gap, owner, weights, start_row, end_row, recorded):
    panel = fill_panel(data, recip, gap, owner)

    def one_freq(pair):
        left, right = pair
        real = jnp.dot(left[0].astype(jnp.float32), right[0].astype(jnp.float32), preferred_element_type=jnp.float32) - jnp.dot(left[1].astype(jnp.float32), right[1].astype(jnp.float32), preferred_element_type=jnp.float32)
        imag = jnp.dot(left[0].astype(jnp.float32), right[1].astype(jnp.float32), preferred_element_type=jnp.float32) + jnp.dot(left[1].astype(jnp.float32), right[0].astype(jnp.float32), preferred_element_type=jnp.float32)
        return (real, imag)
    real, imag = lax.map(one_freq, (jnp.moveaxis(panel, 1, 0), jnp.moveaxis(weights, 1, 0)))
    cosine, sine = phase_tables(jnp.arange(NT, dtype=jnp.int32), jnp.arange(NF, dtype=jnp.int32))
    hp = lax.Precision.HIGHEST
    trace = (jnp.einsum('tf,frs->tsr', cosine, real, precision=hp) - jnp.einsum('tf,frs->tsr', sine, imag, precision=hp)) * (1.0 / math.sqrt(NF))
    padded = jnp.pad(trace, ((HALO, HALO), (0, 0), (0, 0)))
    damping = float(WROWS * SOUT * RECV)

    def one_window(index):
        ext = lax.dynamic_slice_in_dim(padded, index * T_DEV, WROWS, 0)
        rows = index * T_DEV - HALO + jnp.arange(WROWS, dtype=jnp.int32)
        keep = ((rows >= start_row[index]) & (rows < end_row[index])).astype(jnp.float32)
        target = lax.dynamic_slice_in_dim(recorded, index * WROWS, WROWS, 0).astype(jnp.float32) * keep[:, None, None]
        stack = shifted_stack(ext * keep[:, None, None], keep)
        flat = stack.reshape(NU, -1)
        gram = jnp.dot(flat, flat.T, precision=hp)
        rhs = jnp.dot(flat, target.reshape(-1), precision=hp)
        filt = solve_filter(gram, rhs, damping)
        matched = jnp.einsum('u,uwsr->wsr', filt, stack, precision=hp)
        return (target - matched, filt)
    prim, filters = lax.map(one_window, jnp.arange(N_FREQ, dtype=jnp.int32))
    primaries = prim.reshape(N_FREQ * WROWS, SOUT, RECV).astype(jnp.bfloat16)
    return (primaries, filters)
```

```python
import functools
import math

import jax
import jax.numpy as jnp
import ml_dtypes
import numpy as np
from jax import lax
from jax.experimental import pallas as pl
from jax.experimental.pallas import tpu as pltpu
from jax.sharding import PartitionSpec as P

RECV = 128
NFFT = 512
F_LOW = 40
NEAR = 16
HALO = 8
LAGS_T = 9
LAGS_X = 3
LEAD = LAGS_T // 2
T_DEV = 32
WROWS = T_DEV + 2 * HALO
NF = 16
GROUP = 4
GROWS = 256
SIDE = 40
TARGET_COL = GROUP * LEAD + 3
CENTRE_ROW = GROUP * LEAD + 1
PACK_AT = (0, 40, 72, 96, 112)
VMEM = pl.BlockSpec(memory_space=pltpu.VMEM)
SMEM = pl.BlockSpec(memory_space=pltpu.SMEM)
F32 = jnp.float32
BF16 = jnp.bfloat16


def split3(x):
    high = x.astype(ml_dtypes.bfloat16)
    rest = x - high.astype(np.float32)
    mid = rest.astype(ml_dtypes.bfloat16)
    low = (rest - mid.astype(np.float32)).astype(ml_dtypes.bfloat16)
    return high, mid, low


@functools.cache
def phase_rows():
    table = np.zeros((NF, GROWS, 256), ml_dtypes.bfloat16)
    freqs = np.arange(NF)
    scale = 1.0 / math.sqrt(NF)
    for window in range(NF):
        for row in range(WROWS):
            time = window * T_DEV - HALO + row
            if not 0 <= time < NFFT:
                continue
            turns = (F_LOW + freqs) * time % NFFT
            angle = turns * (2.0 * math.pi / NFFT)
            phase = np.stack([np.cos(angle), -np.sin(angle)], axis=1).reshape(-1) * scale
            high, mid, low = split3(phase.astype(np.float32))
            at = GROUP * (row + LEAD)
            table[window, at : at + 3, :192] = np.concatenate([high, high, mid, high, low, mid])
            table[window, at + 3, 192 + row] = 1
    return table


def main_product(mask_ref, data_ref, weights_ref, out_ref, acc_ref):
    step = pl.program_id(0)
    depth = data_ref.shape[3]

    @pl.when(step == 0)
    def _():
        acc_ref[...] = jnp.zeros_like(acc_ref)

    panel = data_ref[...].reshape(2 * RECV, depth)
    mask = jnp.where(step == 0, mask_ref[...], jnp.ones_like(mask_ref))
    near = panel[:, :RECV] * jnp.concatenate([mask, mask], axis=0)
    panel = jnp.concatenate([near, panel[:, RECV:]], axis=1)
    both = jnp.concatenate([weights_ref[0, 0], weights_ref[1, 0]], axis=1)
    product = jnp.dot(panel, both, preferred_element_type=F32)
    half = product.shape[1] // 2
    acc_ref[0] += product[:RECV, :half] - product[RECV:, half:]
    acc_ref[1] += product[:RECV, half:] + product[RECV:, :half]

    @pl.when(step == pl.num_programs(0) - 1)
    def _():
        out_ref[0] = acc_ref[0].T
        out_ref[1] = acc_ref[1].T


def add_fill(pred_ref, recip_ref, gap_ref, near_ref, out_ref):
    slots = out_ref.shape[0]
    piece = jnp.sum(recip_ref[...].astype(F32), axis=0).astype(BF16)
    fill = jnp.dot(near_ref[...], piece * gap_ref[...], preferred_element_type=F32)
    total = pred_ref[...].reshape(fill.shape) + fill
    half = slots * 8
    out_ref[:, :8, :] = total[:half].reshape(slots, 8, RECV)
    out_ref[:, 8:, :] = total[half:].reshape(slots, 8, RECV)


def sum_slots(part_ref, out_ref):
    total = jnp.sum(part_ref[...], axis=0)
    out_ref[...] = jnp.broadcast_to(total[None], out_ref.shape)


def two_parts(x):
    high = x.astype(BF16)
    return high, (x - high.astype(F32)).astype(BF16)


def trace_and_gram(lohi_ref, x_ref, rows_ref, target_ref, gram_ref, trace_ref, a_ref, g_ref):
    sources = 8
    x = jnp.concatenate([x_ref[pl.ds(s, 2 * NF, stride=sources), :] for s in range(sources)], axis=1)
    high, rest = x.astype(BF16), x
    rest = rest - high.astype(F32)
    mid = rest.astype(BF16)
    low = (rest - mid.astype(F32)).astype(BF16)
    stack = jnp.concatenate([high, mid, high, low, high, mid, target_ref[...]], axis=0)
    base = jnp.dot(rows_ref[...], stack, preferred_element_type=F32)
    lag = lax.rem(lax.broadcasted_iota(jnp.int32, (GROWS, RECV), 0), GROUP)
    recv = lax.broadcasted_iota(jnp.int32, (GROWS, RECV), 1)
    ahead = (lag == 0) & (recv < RECV - 1)
    behind = (lag == 2) & (recv > 0)
    same = (lag == 1) | (lag == 3)
    for s in range(sources):
        at = slice(s * RECV, (s + 1) * RECV)
        here = base[:, at]
        shifted = jnp.where(
            same,
            here,
            jnp.where(
                ahead,
                pltpu.roll(here, RECV - 1, 1),
                jnp.where(behind, pltpu.roll(here, 1, 1), 0.0),
            ),
        )
        a_ref[s * GROWS : (s + 1) * GROWS, :] = shifted
    for s in range(sources):
        mine = a_ref[pl.ds(s * GROWS + 1, WROWS + 2 * LEAD, stride=GROUP), :]
        trace_ref[pl.ds(s, WROWS + 2 * LEAD, stride=sources), :] = mine
    high, low = two_parts(jnp.concatenate([a_ref[s * GROWS : (s + 1) * GROWS, :] for s in range(sources)], axis=1))
    dims = (((1,), (1,)), ((), ()))
    g_ref[...] = lax.dot_general(high, high, dims, preferred_element_type=F32) + 2.0 * lax.dot_general(
        high, low, dims, preferred_element_type=F32
    )
    first, last = lohi_ref[0], lohi_ref[1]
    total = jnp.zeros((SIDE, RECV), F32)
    for u in range(WROWS):
        at = GROUP * u
        if at + SIDE <= RECV:
            part = g_ref[at : at + SIDE, :RECV]
            part = pltpu.roll(part, (RECV - at) % RECV, 1)
        elif at >= RECV:
            part = g_ref[at : at + SIDE, RECV:]
            part = pltpu.roll(part, (2 * RECV - at) % RECV, 1)
        else:
            part = pltpu.roll(g_ref[at : at + SIDE, :], 2 * RECV - at, 1)[:, :RECV]
        kept = jnp.where((u >= first) & (u < last), 1.0, 0.0)
        total = total + part * kept
    full = jnp.concatenate([total, jnp.zeros((RECV - SIDE, RECV), F32)], axis=0)
    total = 0.5 * (total + full.T[:SIDE])
    lanes = lax.broadcasted_iota(jnp.int32, (8, RECV), 1)
    packed = jnp.zeros((8, RECV), F32)
    for g, at in enumerate(PACK_AT):
        piece = total[8 * g : 8 * g + 8]
        piece = jnp.where((lanes >= 8 * g) & (lanes < SIDE), piece, 0.0)
        packed = packed + pltpu.roll(piece, at - 8 * g, 1)
    gram_ref[...] = jnp.broadcast_to(packed[None], gram_ref.shape)


def solve_and_filter(damping, lohi_ref, gram_ref, trace_ref, recorded_ref, out_ref, filters_ref, h_ref):
    packed = jnp.sum(gram_ref[...], axis=0)
    lanes = lax.broadcasted_iota(jnp.int32, (8, RECV), 1)
    pieces = []
    for g, at in enumerate(PACK_AT):
        piece = pltpu.roll(packed, (RECV + 8 * g - at) % RECV, 1)
        pieces.append(jnp.where((lanes >= 8 * g) & (lanes < SIDE), piece, 0.0))
    upper = jnp.concatenate(pieces, axis=0)
    full = jnp.concatenate([upper, jnp.zeros((RECV - SIDE, RECV), F32)], axis=0)
    row = lax.broadcasted_iota(jnp.int32, (SIDE, RECV), 0)
    lane = lax.broadcasted_iota(jnp.int32, (SIDE, RECV), 1)
    system = jnp.where(lane // 8 < row // 8, full.T[:SIDE], upper)
    unknown = lax.rem(row, GROUP) < LAGS_X
    system = system + jnp.where((row == lane) & unknown, damping, 0.0)
    system = system + jnp.where((row == CENTRE_ROW) & (lane == TARGET_COL), damping, 0.0)
    for k in range(GROUP * LAGS_T):
        if k % GROUP >= LAGS_X:
            continue
        pivot_row = system[k : k + 1, :]
        column = jnp.broadcast_to(system[:, k : k + 1], (SIDE, RECV))
        scaled = pivot_row / jnp.broadcast_to(system[k : k + 1, k : k + 1], (1, RECV))
        system = jnp.where(row == k, scaled, system - column * scaled)
    h_ref[...] = jnp.broadcast_to(system[:, TARGET_COL : TARGET_COL + 1], (SIDE, RECV))
    filters_ref[...] = h_ref[...]
    first, last = lohi_ref[0], lohi_ref[1]
    recv = lax.broadcasted_iota(jnp.int32, (8, RECV), 1)
    taps = [[jnp.broadcast_to(h_ref[GROUP * p + c : GROUP * p + c + 1, :], (8, RECV)) for c in range(LAGS_X)] for p in range(LAGS_T)]
    for u in range(WROWS):
        sums = [None] * LAGS_X
        for p in range(LAGS_T):
            value = trace_ref[8 * (u + p) : 8 * (u + p) + 8, :]
            for c in range(LAGS_X):
                term = taps[p][c] * value
                sums[c] = term if sums[c] is None else sums[c] + term
        ahead = jnp.where(recv < RECV - 1, pltpu.roll(sums[0], RECV - 1, 1), 0.0)
        behind = jnp.where(recv > 0, pltpu.roll(sums[2], 1, 1), 0.0)
        kept = jnp.where((u >= first) & (u < last), 1.0, 0.0)
        value = recorded_ref[u].astype(F32) - (sums[1] + ahead + behind)
        out_ref[u] = (value * kept).astype(BF16)


def call(kernel, out_shape, args, specs, scratch=(), flops=1000000):
    return pl.pallas_call(
        kernel,
        out_shape=out_shape,
        in_specs=specs,
        out_specs=jax.tree.map(lambda _: VMEM, out_shape),
        scratch_shapes=list(scratch),
        compiler_params=pltpu.CompilerParams(vmem_limit_bytes=32 * 2**20),
        cost_estimate=pl.CostEstimate(flops=flops, bytes_accessed=1000000, transcendentals=0),
    )(*args)


def body(data, recip, gap, owner, weights, start_row, end_row, recorded):
    src_here = lax.axis_index("src")
    freq_here = lax.axis_index("freq")
    src_count = lax.axis_size("src")
    total_out = weights.shape[3]
    points = data.shape[3]

    mine = jnp.swapaxes(recip[:, 0], 1, 2).reshape(2 * NEAR, RECV)
    slots = jnp.arange(src_count, dtype=jnp.int32)
    send = jnp.where((slots == owner[src_here])[:, None, None], mine[None], jnp.zeros_like(mine)[None])
    arrived = lax.all_to_all(send, "src", 0, 0, tiled=True)

    missing = gap == 1
    mask = jnp.pad((~missing).astype(BF16), ((0, 0), (0, RECV - NEAR)), constant_values=1)
    depth = 768
    pred = pl.pallas_call(
        main_product,
        grid=(points // depth,),
        out_shape=jax.ShapeDtypeStruct((2, total_out, RECV), F32),
        in_specs=[
            pl.BlockSpec((RECV, RECV), lambda k: (0, 0)),
            pl.BlockSpec((2, 1, RECV, depth), lambda k: (0, 0, 0, k)),
            pl.BlockSpec((2, 1, depth, total_out), lambda k: (0, 0, k, 0)),
        ],
        out_specs=pl.BlockSpec((2, total_out, RECV), lambda k: (0, 0, 0)),
        scratch_shapes=[pltpu.VMEM((2, RECV, total_out), F32)],
        compiler_params=pltpu.CompilerParams(vmem_limit_bytes=32 * 2**20),
        cost_estimate=pl.CostEstimate(flops=8 * RECV * points * total_out, bytes_accessed=5000000, transcendentals=0),
    )(mask, data, weights)

    near = weights[:, 0, :NEAR, :]
    near_rows = jnp.concatenate(
        [jnp.concatenate([near[0], -near[1]], axis=0), jnp.concatenate([near[1], near[0]], axis=0)], axis=1
    ).T
    gap_rows = missing.T.astype(BF16)
    gap_rows = jnp.concatenate([gap_rows, gap_rows], axis=0)
    parts = call(
        add_fill,
        jax.ShapeDtypeStruct((src_count, 16, RECV), F32),
        (pred, arrived, gap_rows, near_rows),
        [VMEM] * 4,
    )
    parts = lax.all_to_all(parts, "src", 0, 0, tiled=True)
    copies = call(sum_slots, jax.ShapeDtypeStruct((NF, 16, RECV), F32), (parts,), [VMEM])
    spread = lax.all_to_all(copies, "freq", 0, 0, tiled=True).reshape(NF * 16, RECV)

    begin = freq_here * T_DEV - HALO
    lohi = jnp.stack([start_row[0] - begin, end_row[0] - begin]).astype(jnp.int32)
    row = jnp.arange(GROWS, dtype=jnp.int32) // GROUP - LEAD
    keep = (row >= lohi[0]) & (row < lohi[1])
    rows = lax.dynamic_index_in_dim(jnp.asarray(phase_rows()), freq_here, 0, keepdims=False)
    rows = jnp.where(keep[:, None], rows, jnp.zeros_like(rows))
    target = jnp.pad(recorded.reshape(WROWS, -1), ((0, 16), (0, 0)))
    trace_rows = 8 * (WROWS + 2 * LEAD)
    gram, trace = call(
        trace_and_gram,
        (jax.ShapeDtypeStruct((src_count, 8, RECV), F32), jax.ShapeDtypeStruct((trace_rows, RECV), F32)),
        (lohi, spread, rows, target),
        [SMEM, VMEM, VMEM, VMEM],
        [pltpu.VMEM((8 * GROWS, RECV), F32), pltpu.VMEM((GROWS, GROWS), F32)],
    )
    gram = lax.all_to_all(gram, "src", 0, 0, tiled=True)
    damping = float(WROWS * total_out * RECV)
    primaries, filters = call(
        functools.partial(solve_and_filter, damping),
        (jax.ShapeDtypeStruct(recorded.shape, BF16), jax.ShapeDtypeStruct((SIDE, RECV), F32)),
        (lohi, gram, trace, recorded),
        [SMEM, VMEM, VMEM, VMEM],
        [pltpu.VMEM((SIDE, RECV), F32)],
    )
    taps = filters[: GROUP * LAGS_T, 0].reshape(LAGS_T, GROUP)[::-1, :LAGS_X]
    return primaries, taps.reshape(1, -1)


def solution(mesh):
    placed = (
        P(None, "freq", None, "src"),
        P(None, "freq", None, "src"),
        P(None, "src"),
        P(),
        P(None, "freq", "src", None),
        P("freq"),
        P("freq"),
        P("freq", "src", None),
    )
    return jax.shard_map(
        body,
        mesh=mesh,
        in_specs=placed,
        out_specs=(P("freq", "src", None), P("freq", None)),
        check_vma=False,
    )
```

```python
import functools
import math

import jax
import jax.numpy as jnp
import ml_dtypes
import numpy as np
from jax import lax
from jax.experimental import pallas as pl
from jax.experimental.pallas import tpu as pltpu
from jax.sharding import PartitionSpec as P

RECV = 128
NFFT = 512
F_LOW = 40
NEAR = 16
HALO = 8
LAGS_T = 9
LAGS_X = 3
LEAD = LAGS_T // 2
T_DEV = 32
WROWS = T_DEV + 2 * HALO
NF = 16
GROUP = 4
GROWS = 256
SIDE = 40
UNKNOWNS = LAGS_T * LAGS_X
TARGET_COL = GROUP * LEAD + 3
CENTRE_ROW = GROUP * LEAD + 1
PACK_AT = (0, 40, 72, 96, 112)
LOW_AT, RECIP_AT, GAP_AT, NEAR_AT, SLOT_ROWS = 16, 32, 64, 80, 96
VMEM = pl.BlockSpec(memory_space=pltpu.VMEM)
SMEM = pl.BlockSpec(memory_space=pltpu.SMEM)
F32 = jnp.float32
BF16 = jnp.bfloat16


def split3(x):
    high = x.astype(ml_dtypes.bfloat16)
    rest = x - high.astype(np.float32)
    mid = rest.astype(ml_dtypes.bfloat16)
    low = (rest - mid.astype(np.float32)).astype(ml_dtypes.bfloat16)
    return high, mid, low


@functools.cache
def phase_rows():
    table = np.zeros((NF, GROWS, 256), ml_dtypes.bfloat16)
    freqs = np.arange(NF)
    scale = 1.0 / math.sqrt(NF)
    for window in range(NF):
        for row in range(WROWS):
            time = window * T_DEV - HALO + row
            if not 0 <= time < NFFT:
                continue
            turns = (F_LOW + freqs) * time % NFFT
            angle = turns * (2.0 * math.pi / NFFT)
            phase = np.stack([np.cos(angle), -np.sin(angle)], axis=1).reshape(-1) * scale
            high, mid, low = split3(phase.astype(np.float32))
            at = GROUP * (row + LEAD)
            table[window, at : at + 3, :192] = np.concatenate([high, high, mid, high, low, mid])
            table[window, at + 3, 192 + row] = 1
    return table


def main_product(gap_ref, recip_ref, data_ref, weights_ref, out_ref, acc_ref, mask_ref):
    step = pl.program_id(0)
    depth = data_ref.shape[3]
    slots = out_ref.shape[0]

    @pl.when(step == 0)
    def _():
        acc_ref[...] = jnp.zeros_like(acc_ref)
        gap = jnp.where(gap_ref[...] == 1, 1.0, 0.0)
        full = jnp.concatenate([gap, jnp.zeros((RECV - NEAR, RECV), F32)], axis=0)
        mask_ref[...] = (1.0 - full.T).astype(BF16)
        out_ref[:, RECIP_AT:GAP_AT] = jnp.broadcast_to(recip_ref[...][None], (slots, 2 * NEAR, RECV))
        out_ref[:, GAP_AT:NEAR_AT] = jnp.broadcast_to(gap.astype(BF16)[None], (slots, NEAR, RECV))
        lanes = lax.broadcasted_iota(jnp.int32, (NEAR, RECV), 1)
        for group in range(slots * 8 // 64):
            at = RECV * (group // 2)
            real = weights_ref[0, 0, :NEAR, at : at + RECV].astype(F32)
            imag = weights_ref[1, 0, :NEAR, at : at + RECV].astype(F32)
            if group % 2:
                real = pltpu.roll(real, 64, 1)
            else:
                imag = pltpu.roll(imag, 64, 1)
            near = jnp.where(lanes < 64, real, imag).astype(BF16)
            out_ref[8 * group : 8 * group + 8, NEAR_AT:] = jnp.broadcast_to(near[None], (8, NEAR, RECV))

    @pl.when(step == 1)
    def _():
        mask_ref[...] = jnp.ones_like(mask_ref)

    panel = data_ref[...].reshape(2 * RECV, depth)
    mask = mask_ref[...]
    near = panel[:, :RECV] * jnp.concatenate([mask, mask], axis=0)
    panel = jnp.concatenate([near, panel[:, RECV:]], axis=1)
    both = jnp.concatenate([weights_ref[0, 0], weights_ref[1, 0]], axis=1)
    product = jnp.dot(panel, both, preferred_element_type=F32)
    half = product.shape[1] // 2
    acc_ref[0] += product[:RECV, :half] - product[RECV:, half:]
    acc_ref[1] += product[:RECV, half:] + product[RECV:, :half]

    @pl.when(step == pl.num_programs(0) - 1)
    def _():
        real = acc_ref[0].T.reshape(slots, 8, RECV)
        imag = acc_ref[1].T.reshape(slots, 8, RECV)
        high, low = two_parts(jnp.concatenate([real, imag], axis=1))
        out_ref[:, :LOW_AT] = high
        out_ref[:, LOW_AT:RECIP_AT] = low


def sum_and_fill(owner_ref, place_ref, part_ref, out_ref, z_ref, w_ref, f_ref):
    slots = part_ref.shape[0]
    total = jnp.zeros((16, RECV), F32)
    for j in range(slots):
        total = total + part_ref[j, :LOW_AT].astype(F32) + part_ref[j, LOW_AT:RECIP_AT].astype(F32)
        block = owner_ref[j]
        gap = part_ref[block, GAP_AT:NEAR_AT]
        at = slice(NEAR * j, NEAR * j + NEAR)
        z_ref[at, :RECV] = part_ref[j, RECIP_AT : RECIP_AT + NEAR] * gap
        z_ref[at, RECV:] = part_ref[j, RECIP_AT + NEAR : GAP_AT] * gap
        w_ref[at, :] = part_ref[block, NEAR_AT:]
    f_ref[...] = lax.dot_general(
        w_ref[...], z_ref[...], (((0,), (0,)), ((), ())), preferred_element_type=F32
    )
    at = pl.multiple_of(place_ref[0] * 8, 8)
    by_real = f_ref[pl.ds(at, 8), :]
    by_imag = f_ref[pl.ds(at + 64, 8), :]
    real = total[:8] + by_real[:, :RECV] - by_imag[:, RECV:]
    imag = total[8:] + by_imag[:, :RECV] + by_real[:, RECV:]
    out_ref[:, :8] = jnp.broadcast_to(real[None], (out_ref.shape[0], 8, RECV))
    out_ref[:, 8:] = jnp.broadcast_to(imag[None], (out_ref.shape[0], 8, RECV))


def two_parts(x):
    high = x.astype(BF16)
    return high, (x - high.astype(F32)).astype(BF16)


def trace_and_gram(lohi_ref, x_ref, rows_ref, target_ref, gram_ref, trace_ref, a_ref, g_ref):
    sources = 8
    x = jnp.concatenate([x_ref[pl.ds(s, 2 * NF, stride=sources), :] for s in range(sources)], axis=1)
    high, rest = x.astype(BF16), x
    rest = rest - high.astype(F32)
    mid = rest.astype(BF16)
    low = (rest - mid.astype(F32)).astype(BF16)
    stack = jnp.concatenate([high, mid, high, low, high, mid, target_ref[...]], axis=0)
    base = jnp.dot(rows_ref[...], stack, preferred_element_type=F32)
    lag = lax.rem(lax.broadcasted_iota(jnp.int32, (GROWS, RECV), 0), GROUP)
    recv = lax.broadcasted_iota(jnp.int32, (GROWS, RECV), 1)
    ahead = (lag == 0) & (recv < RECV - 1)
    behind = (lag == 2) & (recv > 0)
    same = (lag == 1) | (lag == 3)
    for s in range(sources):
        at = slice(s * RECV, (s + 1) * RECV)
        here = base[:, at]
        shifted = jnp.where(
            same,
            here,
            jnp.where(
                ahead,
                pltpu.roll(here, RECV - 1, 1),
                jnp.where(behind, pltpu.roll(here, 1, 1), 0.0),
            ),
        )
        a_ref[s * GROWS : (s + 1) * GROWS, :] = shifted
    for s in range(sources):
        mine = a_ref[pl.ds(s * GROWS + 1, WROWS + 2 * LEAD, stride=GROUP), :]
        trace_ref[pl.ds(s, WROWS + 2 * LEAD, stride=sources), :] = mine
    high, low = two_parts(jnp.concatenate([a_ref[s * GROWS : (s + 1) * GROWS, :] for s in range(sources)], axis=1))
    dims = (((1,), (1,)), ((), ()))
    g_ref[...] = lax.dot_general(high, high, dims, preferred_element_type=F32) + 2.0 * lax.dot_general(
        high, low, dims, preferred_element_type=F32
    )
    first, last = lohi_ref[0], lohi_ref[1]
    total = jnp.zeros((SIDE, RECV), F32)
    for u in range(WROWS):
        at = GROUP * u
        if at + SIDE <= RECV:
            part = g_ref[at : at + SIDE, :RECV]
            part = pltpu.roll(part, (RECV - at) % RECV, 1)
        elif at >= RECV:
            part = g_ref[at : at + SIDE, RECV:]
            part = pltpu.roll(part, (2 * RECV - at) % RECV, 1)
        else:
            part = pltpu.roll(g_ref[at : at + SIDE, :], 2 * RECV - at, 1)[:, :RECV]
        kept = jnp.where((u >= first) & (u < last), 1.0, 0.0)
        total = total + part * kept
    full = jnp.concatenate([total, jnp.zeros((RECV - SIDE, RECV), F32)], axis=0)
    total = 0.5 * (total + full.T[:SIDE])
    lanes = lax.broadcasted_iota(jnp.int32, (8, RECV), 1)
    packed = jnp.zeros((8, RECV), F32)
    for g, at in enumerate(PACK_AT):
        piece = total[8 * g : 8 * g + 8]
        piece = jnp.where((lanes >= 8 * g) & (lanes < SIDE), piece, 0.0)
        packed = packed + pltpu.roll(piece, at - 8 * g, 1)
    gram_ref[...] = jnp.broadcast_to(packed[None], gram_ref.shape)


def solve_and_filter(damping, lohi_ref, gram_ref, trace_ref, recorded_ref, out_ref, filters_ref, h_ref):
    packed = jnp.sum(gram_ref[...], axis=0)
    lanes = lax.broadcasted_iota(jnp.int32, (8, RECV), 1)
    pieces = []
    for g, at in enumerate(PACK_AT):
        piece = pltpu.roll(packed, (RECV + 8 * g - at) % RECV, 1)
        pieces.append(jnp.where((lanes >= 8 * g) & (lanes < SIDE), piece, 0.0))
    upper = jnp.concatenate(pieces, axis=0)
    full = jnp.concatenate([upper, jnp.zeros((RECV - SIDE, RECV), F32)], axis=0)
    row = lax.broadcasted_iota(jnp.int32, (SIDE, RECV), 0)
    lane = lax.broadcasted_iota(jnp.int32, (SIDE, RECV), 1)
    system = jnp.where(lane // 8 < row // 8, full.T[:SIDE], upper)
    unknown = lax.rem(row, GROUP) < LAGS_X
    system = system + jnp.where((row == lane) & unknown, damping, 0.0)
    system = system + jnp.where((row == CENTRE_ROW) & (lane == TARGET_COL), damping, 0.0)
    for k in range(GROUP * LAGS_T):
        if k % GROUP >= LAGS_X:
            continue
        pivot_row = system[k : k + 1, :]
        column = jnp.broadcast_to(system[:, k : k + 1], (SIDE, RECV))
        scaled = pivot_row / jnp.broadcast_to(system[k : k + 1, k : k + 1], (1, RECV))
        system = jnp.where(row == k, scaled, system - column * scaled)
    chosen = (lane < UNKNOWNS) & (row == GROUP * (LAGS_T - 1 - lane // LAGS_X) + lane % LAGS_X)
    h_ref[...] = jnp.broadcast_to(system[:, TARGET_COL : TARGET_COL + 1], (SIDE, RECV))
    filters_ref[...] = jnp.sum(jnp.where(chosen, h_ref[...], 0.0), axis=0, keepdims=True)[:, :UNKNOWNS]
    first, last = lohi_ref[0], lohi_ref[1]
    recv = lax.broadcasted_iota(jnp.int32, (8, RECV), 1)
    taps = [[jnp.broadcast_to(h_ref[GROUP * p + c : GROUP * p + c + 1, :], (8, RECV)) for c in range(LAGS_X)] for p in range(LAGS_T)]
    for u in range(WROWS):
        sums = [None] * LAGS_X
        for p in range(LAGS_T):
            value = trace_ref[8 * (u + p) : 8 * (u + p) + 8, :]
            for c in range(LAGS_X):
                term = taps[p][c] * value
                sums[c] = term if sums[c] is None else sums[c] + term
        ahead = jnp.where(recv < RECV - 1, pltpu.roll(sums[0], RECV - 1, 1), 0.0)
        behind = jnp.where(recv > 0, pltpu.roll(sums[2], 1, 1), 0.0)
        kept = jnp.where((u >= first) & (u < last), 1.0, 0.0)
        value = recorded_ref[u].astype(F32) - (sums[1] + ahead + behind)
        out_ref[u] = (value * kept).astype(BF16)


def call(kernel, out_shape, args, specs, scratch=(), flops=1000000):
    return pl.pallas_call(
        kernel,
        out_shape=out_shape,
        in_specs=specs,
        out_specs=jax.tree.map(lambda _: VMEM, out_shape),
        scratch_shapes=list(scratch),
        compiler_params=pltpu.CompilerParams(vmem_limit_bytes=32 * 2**20),
        cost_estimate=pl.CostEstimate(flops=flops, bytes_accessed=1000000, transcendentals=0),
    )(*args)


def body(data, recip, gap, owner, weights, start_row, end_row, recorded):
    src_here = lax.axis_index("src")
    freq_here = lax.axis_index("freq")
    src_count = lax.axis_size("src")
    total_out = weights.shape[3]
    points = data.shape[3]

    recip_rows = jnp.swapaxes(recip[:, 0], 1, 2).reshape(2 * NEAR, RECV)
    depth = 768
    parts = pl.pallas_call(
        main_product,
        grid=(points // depth,),
        out_shape=jax.ShapeDtypeStruct((src_count, SLOT_ROWS, RECV), BF16),
        in_specs=[
            pl.BlockSpec((NEAR, RECV), lambda k: (0, 0)),
            pl.BlockSpec((2 * NEAR, RECV), lambda k: (0, 0)),
            pl.BlockSpec((2, 1, RECV, depth), lambda k: (0, 0, 0, k)),
            pl.BlockSpec((2, 1, depth, total_out), lambda k: (0, 0, k, 0)),
        ],
        out_specs=pl.BlockSpec((src_count, SLOT_ROWS, RECV), lambda k: (0, 0, 0)),
        scratch_shapes=[pltpu.VMEM((2, RECV, total_out), F32), pltpu.VMEM((RECV, RECV), BF16)],
        cost_estimate=pl.CostEstimate(flops=8 * RECV * points * total_out, bytes_accessed=5000000, transcendentals=0),
    )(gap.T, recip_rows, data, weights)
    parts = lax.all_to_all(parts, "src", 0, 0, tiled=True)
    place = jnp.reshape(src_here % 8, (1,)).astype(jnp.int32)
    copies = call(
        sum_and_fill,
        jax.ShapeDtypeStruct((NF, 16, RECV), F32),
        (owner, place, parts),
        [SMEM, SMEM, VMEM],
        [
            pltpu.VMEM((NEAR * src_count, 2 * RECV), BF16),
            pltpu.VMEM((NEAR * src_count, RECV), BF16),
            pltpu.VMEM((RECV, 2 * RECV), F32),
        ],
    )
    spread = lax.all_to_all(copies, "freq", 0, 0, tiled=True).reshape(NF * 16, RECV)

    begin = freq_here * T_DEV - HALO
    lohi = jnp.stack([start_row[0] - begin, end_row[0] - begin]).astype(jnp.int32)
    row = jnp.arange(GROWS, dtype=jnp.int32) // GROUP - LEAD
    keep = (row >= lohi[0]) & (row < lohi[1])
    rows = lax.dynamic_index_in_dim(jnp.asarray(phase_rows()), freq_here, 0, keepdims=False)
    rows = jnp.where(keep[:, None], rows, jnp.zeros_like(rows))
    target = jnp.pad(recorded.reshape(WROWS, -1), ((0, 16), (0, 0)))
    trace_rows = 8 * (WROWS + 2 * LEAD)
    gram, trace = call(
        trace_and_gram,
        (jax.ShapeDtypeStruct((src_count, 8, RECV), F32), jax.ShapeDtypeStruct((trace_rows, RECV), F32)),
        (lohi, spread, rows, target),
        [SMEM, VMEM, VMEM, VMEM],
        [pltpu.VMEM((8 * GROWS, RECV), F32), pltpu.VMEM((GROWS, GROWS), F32)],
    )
    gram = lax.all_to_all(gram, "src", 0, 0, tiled=True)
    damping = float(WROWS * total_out * RECV)
    primaries, filters = call(
        functools.partial(solve_and_filter, damping),
        (jax.ShapeDtypeStruct(recorded.shape, BF16), jax.ShapeDtypeStruct((1, UNKNOWNS), F32)),
        (lohi, gram, trace, recorded),
        [SMEM, VMEM, VMEM, VMEM],
        [pltpu.VMEM((SIDE, RECV), F32)],
    )
    return primaries, filters


def solution(mesh):
    placed = (
        P(None, "freq", None, "src"),
        P(None, "freq", None, "src"),
        P(None, "src"),
        P(),
        P(None, "freq", "src", None),
        P("freq"),
        P("freq"),
        P("freq", "src", None),
    )
    return jax.shard_map(
        body,
        mesh=mesh,
        in_specs=placed,
        out_specs=(P("freq", "src", None), P("freq", None)),
        check_vma=False,
    )
```

```python
import functools
import math

import jax
import jax.numpy as jnp
import ml_dtypes
import numpy as np
from jax import lax
from jax.experimental import pallas as pl
from jax.experimental.pallas import tpu as pltpu
from jax.sharding import PartitionSpec as P

RECV = 128
NFFT = 512
F_LOW = 40
NEAR = 16
HALO = 8
LAGS_T = 9
LAGS_X = 3
LEAD = LAGS_T // 2
T_DEV = 32
WROWS = T_DEV + 2 * HALO
NF = 16
GROUP = 4
GROWS = 256
SIDE = 40
UNKNOWNS = LAGS_T * LAGS_X
TARGET_COL = GROUP * LEAD + 3
CENTRE_ROW = GROUP * LEAD + 1
PACK_AT = (0, 40, 72, 96, 112)
LOW_AT, RECIP_AT, GAP_AT, NEAR_AT, SLOT_ROWS = 16, 32, 64, 80, 96
VMEM = pl.BlockSpec(memory_space=pltpu.VMEM)
F32 = jnp.float32
BF16 = jnp.bfloat16


def split3(x):
    high = x.astype(ml_dtypes.bfloat16)
    rest = x - high.astype(np.float32)
    mid = rest.astype(ml_dtypes.bfloat16)
    low = (rest - mid.astype(np.float32)).astype(ml_dtypes.bfloat16)
    return high, mid, low


@functools.cache
def phase_rows():
    table = np.zeros((NF, GROWS, 256), ml_dtypes.bfloat16)
    freqs = np.arange(NF)
    scale = 1.0 / math.sqrt(NF)
    for window in range(NF):
        for row in range(WROWS):
            time = window * T_DEV - HALO + row
            if not 0 <= time < NFFT:
                continue
            turns = (F_LOW + freqs) * time % NFFT
            angle = turns * (2.0 * math.pi / NFFT)
            phase = np.stack([np.cos(angle), -np.sin(angle)], axis=1).reshape(-1) * scale
            high, mid, low = split3(phase.astype(np.float32))
            at = GROUP * (row + LEAD)
            table[window, at : at + 3, :192] = np.concatenate([high, high, mid, high, low, mid])
            table[window, at + 3, 192 + row] = 1
    return table


def main_product(gap_ref, recip_ref, data_ref, weights_ref, out_ref, acc_ref, mask_ref):
    step = pl.program_id(0)
    depth = data_ref.shape[3]
    slots = out_ref.shape[0]

    @pl.when(step == 0)
    def _():
        acc_ref[...] = jnp.zeros_like(acc_ref)
        gap = jnp.where(gap_ref[...] == 1, 1.0, 0.0)
        full = jnp.concatenate([gap, jnp.zeros((RECV - NEAR, RECV), F32)], axis=0)
        mask_ref[...] = (1.0 - full.T).astype(BF16)
        out_ref[:, RECIP_AT:GAP_AT] = jnp.broadcast_to(recip_ref[...][None], (slots, 2 * NEAR, RECV))
        out_ref[:, GAP_AT:NEAR_AT] = jnp.broadcast_to(gap.astype(BF16)[None], (slots, NEAR, RECV))
        lanes = lax.broadcasted_iota(jnp.int32, (NEAR, RECV), 1)
        for group in range(slots * 8 // 64):
            at = RECV * (group // 2)
            real = weights_ref[0, 0, :NEAR, at : at + RECV].astype(F32)
            imag = weights_ref[1, 0, :NEAR, at : at + RECV].astype(F32)
            if group % 2:
                real = pltpu.roll(real, 64, 1)
            else:
                imag = pltpu.roll(imag, 64, 1)
            near = jnp.where(lanes < 64, real, imag).astype(BF16)
            out_ref[8 * group : 8 * group + 8, NEAR_AT:] = jnp.broadcast_to(near[None], (8, NEAR, RECV))

    @pl.when(step == 1)
    def _():
        mask_ref[...] = jnp.ones_like(mask_ref)

    panel = data_ref[...].reshape(2 * RECV, depth)
    mask = mask_ref[...]
    near = panel[:, :RECV] * jnp.concatenate([mask, mask], axis=0)
    panel = jnp.concatenate([near, panel[:, RECV:]], axis=1)
    both = jnp.concatenate([weights_ref[0, 0], weights_ref[1, 0]], axis=1)
    product = jnp.dot(panel, both, preferred_element_type=F32)
    half = product.shape[1] // 2
    acc_ref[0] += product[:RECV, :half] - product[RECV:, half:]
    acc_ref[1] += product[:RECV, half:] + product[RECV:, :half]

    @pl.when(step == pl.num_programs(0) - 1)
    def _():
        real = acc_ref[0].T.reshape(slots, 8, RECV)
        imag = acc_ref[1].T.reshape(slots, 8, RECV)
        high, low = two_parts(jnp.concatenate([real, imag], axis=1))
        out_ref[:, :LOW_AT] = high
        out_ref[:, LOW_AT:RECIP_AT] = low


def sum_and_fill(owner_ref, part_ref, out_ref, z_ref, w_ref, f_ref, block_ref, sem):
    slots = part_ref.shape[0]
    copy = pltpu.make_async_copy(owner_ref, block_ref, sem)
    copy.start()
    place = lax.rem(lax.axis_index("src"), 8)
    total = jnp.zeros((16, RECV), F32)
    for j in range(slots):
        total = total + part_ref[j, :LOW_AT].astype(F32) + part_ref[j, LOW_AT:RECIP_AT].astype(F32)
    copy.wait()
    for j in range(slots):
        block = block_ref[j]
        gap = part_ref[block, GAP_AT:NEAR_AT]
        at = slice(NEAR * j, NEAR * j + NEAR)
        z_ref[at, :RECV] = part_ref[j, RECIP_AT : RECIP_AT + NEAR] * gap
        z_ref[at, RECV:] = part_ref[j, RECIP_AT + NEAR : GAP_AT] * gap
        w_ref[at, :] = part_ref[block, NEAR_AT:]
    f_ref[...] = lax.dot_general(
        w_ref[...], z_ref[...], (((0,), (0,)), ((), ())), preferred_element_type=F32
    )
    at = pl.multiple_of(place * 8, 8)
    by_real = f_ref[pl.ds(at, 8), :]
    by_imag = f_ref[pl.ds(at + 64, 8), :]
    real = total[:8] + by_real[:, :RECV] - by_imag[:, RECV:]
    imag = total[8:] + by_imag[:, :RECV] + by_real[:, RECV:]
    out_ref[:, :8] = jnp.broadcast_to(real[None], (out_ref.shape[0], 8, RECV))
    out_ref[:, 8:] = jnp.broadcast_to(imag[None], (out_ref.shape[0], 8, RECV))


def two_parts(x):
    high = x.astype(BF16)
    return high, (x - high.astype(F32)).astype(BF16)


def trace_and_gram(keep_ref, x_ref, rows_ref, target_ref, gram_ref, trace_ref, a_ref, g_ref):
    sources = 8
    x = jnp.concatenate([x_ref[pl.ds(s, 2 * NF, stride=sources), :] for s in range(sources)], axis=1)
    high, rest = x.astype(BF16), x
    rest = rest - high.astype(F32)
    mid = rest.astype(BF16)
    low = (rest - mid.astype(F32)).astype(BF16)
    stack = jnp.concatenate([high, mid, high, low, high, mid, target_ref[...]], axis=0)
    base = jnp.dot(rows_ref[...], stack, preferred_element_type=F32)
    lag = lax.rem(lax.broadcasted_iota(jnp.int32, (GROWS, RECV), 0), GROUP)
    recv = lax.broadcasted_iota(jnp.int32, (GROWS, RECV), 1)
    ahead = (lag == 0) & (recv < RECV - 1)
    behind = (lag == 2) & (recv > 0)
    same = (lag == 1) | (lag == 3)
    for s in range(sources):
        at = slice(s * RECV, (s + 1) * RECV)
        here = base[:, at]
        shifted = jnp.where(
            same,
            here,
            jnp.where(
                ahead,
                pltpu.roll(here, RECV - 1, 1),
                jnp.where(behind, pltpu.roll(here, 1, 1), 0.0),
            ),
        )
        a_ref[s * GROWS : (s + 1) * GROWS, :] = shifted
    for s in range(sources):
        mine = a_ref[pl.ds(s * GROWS + 1, WROWS + 2 * LEAD, stride=GROUP), :]
        trace_ref[pl.ds(s, WROWS + 2 * LEAD, stride=sources), :] = mine
    high, low = two_parts(jnp.concatenate([a_ref[s * GROWS : (s + 1) * GROWS, :] for s in range(sources)], axis=1))
    dims = (((1,), (1,)), ((), ()))
    g_ref[...] = lax.dot_general(high, high, dims, preferred_element_type=F32) + 2.0 * lax.dot_general(
        high, low, dims, preferred_element_type=F32
    )
    total = jnp.zeros((SIDE, RECV), F32)
    for u in range(WROWS):
        at = GROUP * u
        if at + SIDE <= RECV:
            part = g_ref[at : at + SIDE, :RECV]
            part = pltpu.roll(part, (RECV - at) % RECV, 1)
        elif at >= RECV:
            part = g_ref[at : at + SIDE, RECV:]
            part = pltpu.roll(part, (2 * RECV - at) % RECV, 1)
        else:
            part = pltpu.roll(g_ref[at : at + SIDE, :], 2 * RECV - at, 1)[:, :RECV]
        total = total + part * keep_ref[u : u + 1, :]
    full = jnp.concatenate([total, jnp.zeros((RECV - SIDE, RECV), F32)], axis=0)
    total = 0.5 * (total + full.T[:SIDE])
    lanes = lax.broadcasted_iota(jnp.int32, (8, RECV), 1)
    packed = jnp.zeros((8, RECV), F32)
    for g, at in enumerate(PACK_AT):
        piece = total[8 * g : 8 * g + 8]
        piece = jnp.where((lanes >= 8 * g) & (lanes < SIDE), piece, 0.0)
        packed = packed + pltpu.roll(piece, at - 8 * g, 1)
    gram_ref[...] = jnp.broadcast_to(packed[None], gram_ref.shape)


def solve_and_filter(damping, keep_ref, gram_ref, trace_ref, recorded_ref, out_ref, filters_ref, h_ref):
    packed = jnp.sum(gram_ref[...], axis=0)
    lanes = lax.broadcasted_iota(jnp.int32, (8, RECV), 1)
    pieces = []
    for g, at in enumerate(PACK_AT):
        piece = pltpu.roll(packed, (RECV + 8 * g - at) % RECV, 1)
        pieces.append(jnp.where((lanes >= 8 * g) & (lanes < SIDE), piece, 0.0))
    upper = jnp.concatenate(pieces, axis=0)
    full = jnp.concatenate([upper, jnp.zeros((RECV - SIDE, RECV), F32)], axis=0)
    row = lax.broadcasted_iota(jnp.int32, (SIDE, RECV), 0)
    lane = lax.broadcasted_iota(jnp.int32, (SIDE, RECV), 1)
    system = jnp.where(lane // 8 < row // 8, full.T[:SIDE], upper)
    unknown = lax.rem(row, GROUP) < LAGS_X
    system = system + jnp.where((row == lane) & unknown, damping, 0.0)
    system = system + jnp.where((row == CENTRE_ROW) & (lane == TARGET_COL), damping, 0.0)
    order = [k for k in range(GROUP * LAGS_T) if k % GROUP < LAGS_X]
    for one, two in zip(order[:-1:2], order[1::2]):
        first = jnp.broadcast_to(system[:, one : one + 1], (SIDE, RECV))
        second = jnp.broadcast_to(system[:, two : two + 1], (SIDE, RECV))
        top, bottom = system[one : one + 1, :], system[two : two + 1, :]
        a, b, d = first[one : one + 1], second[one : one + 1], second[two : two + 1]
        scale = 1.0 / (a * d - b * b)
        top, bottom = (d * top - b * bottom) * scale, (a * bottom - b * top) * scale
        rest = system - first * top - second * bottom
        system = jnp.where(row == one, top, jnp.where(row == two, bottom, rest))
    last = order[-1]
    column = jnp.broadcast_to(system[:, last : last + 1], (SIDE, RECV))
    pivot_row = system[last : last + 1, :] / column[last : last + 1]
    system = jnp.where(row == last, pivot_row, system - column * pivot_row)
    chosen = (lane < UNKNOWNS) & (row == GROUP * (LAGS_T - 1 - lane // LAGS_X) + lane % LAGS_X)
    h_ref[...] = jnp.broadcast_to(system[:, TARGET_COL : TARGET_COL + 1], (SIDE, RECV))
    filters_ref[...] = jnp.sum(jnp.where(chosen, h_ref[...], 0.0), axis=0, keepdims=True)[:, :UNKNOWNS]
    recv = lax.broadcasted_iota(jnp.int32, (8, RECV), 1)
    taps = [[jnp.broadcast_to(h_ref[GROUP * p + c : GROUP * p + c + 1, :], (8, RECV)) for c in range(LAGS_X)] for p in range(LAGS_T)]
    for u in range(WROWS):
        sums = [None] * LAGS_X
        for p in range(LAGS_T):
            value = trace_ref[8 * (u + p) : 8 * (u + p) + 8, :]
            for c in range(LAGS_X):
                term = taps[p][c] * value
                sums[c] = term if sums[c] is None else sums[c] + term
        ahead = jnp.where(recv < RECV - 1, pltpu.roll(sums[0], RECV - 1, 1), 0.0)
        behind = jnp.where(recv > 0, pltpu.roll(sums[2], 1, 1), 0.0)
        value = recorded_ref[u].astype(F32) - (sums[1] + ahead + behind)
        out_ref[u] = (value * keep_ref[u : u + 1, :]).astype(BF16)


def call(kernel, out_shape, args, specs, scratch=(), flops=1000000):
    return pl.pallas_call(
        kernel,
        out_shape=out_shape,
        in_specs=specs,
        out_specs=jax.tree.map(lambda _: VMEM, out_shape),
        scratch_shapes=list(scratch),
        compiler_params=pltpu.CompilerParams(vmem_limit_bytes=32 * 2**20),
        cost_estimate=pl.CostEstimate(flops=flops, bytes_accessed=1000000, transcendentals=0),
    )(*args)


def body(data, recip, gap, owner, weights, start_row, end_row, recorded):
    freq_here = lax.axis_index("freq")
    src_count = lax.axis_size("src")
    total_out = weights.shape[3]
    points = data.shape[3]

    recip_rows = jnp.swapaxes(recip[:, 0], 1, 2).reshape(2 * NEAR, RECV)
    depth = points // 2
    parts = pl.pallas_call(
        main_product,
        grid=(points // depth,),
        out_shape=jax.ShapeDtypeStruct((src_count, SLOT_ROWS, RECV), BF16),
        in_specs=[
            pl.BlockSpec((NEAR, RECV), lambda k: (0, 0)),
            pl.BlockSpec((2 * NEAR, RECV), lambda k: (0, 0)),
            pl.BlockSpec((2, 1, RECV, depth), lambda k: (0, 0, 0, k)),
            pl.BlockSpec((2, 1, depth, total_out), lambda k: (0, 0, k, 0)),
        ],
        out_specs=pl.BlockSpec((src_count, SLOT_ROWS, RECV), lambda k: (0, 0, 0)),
        scratch_shapes=[pltpu.VMEM((2, RECV, total_out), F32), pltpu.VMEM((RECV, RECV), BF16)],
        cost_estimate=pl.CostEstimate(flops=8 * RECV * points * total_out, bytes_accessed=5000000, transcendentals=0),
    )(gap.T, recip_rows, data, weights)
    parts = lax.all_to_all(parts, "src", 0, 0, tiled=True)
    copies = call(
        sum_and_fill,
        jax.ShapeDtypeStruct((NF, 16, RECV), F32),
        (owner, parts),
        [pl.BlockSpec(memory_space=pl.ANY), VMEM],
        [
            pltpu.VMEM((NEAR * src_count, 2 * RECV), BF16),
            pltpu.VMEM((NEAR * src_count, RECV), BF16),
            pltpu.VMEM((RECV, 2 * RECV), F32),
            pltpu.SMEM((src_count,), jnp.int32),
            pltpu.SemaphoreType.DMA,
        ],
    )
    spread = lax.all_to_all(copies, "freq", 0, 0, tiled=True).reshape(NF * 16, RECV)

    begin = freq_here * T_DEV - HALO
    first, last = start_row[0] - begin, end_row[0] - begin
    row = lax.broadcasted_iota(jnp.int32, (WROWS, RECV), 0)
    keep_rows = ((row >= first) & (row < last)).astype(F32)
    row = jnp.arange(GROWS, dtype=jnp.int32) // GROUP - LEAD
    keep = (row >= first) & (row < last)
    rows = lax.dynamic_index_in_dim(jnp.asarray(phase_rows()), freq_here, 0, keepdims=False)
    rows = jnp.where(keep[:, None], rows, jnp.zeros_like(rows))
    target = jnp.pad(recorded.reshape(WROWS, -1), ((0, 16), (0, 0)))
    trace_rows = 8 * (WROWS + 2 * LEAD)
    gram, trace = call(
        trace_and_gram,
        (jax.ShapeDtypeStruct((src_count, 8, RECV), F32), jax.ShapeDtypeStruct((trace_rows, RECV), F32)),
        (keep_rows, spread, rows, target),
        [VMEM] * 4,
        [pltpu.VMEM((8 * GROWS, RECV), F32), pltpu.VMEM((GROWS, GROWS), F32)],
    )
    gram = lax.all_to_all(gram, "src", 0, 0, tiled=True)
    damping = float(WROWS * total_out * RECV)
    primaries, filters = call(
        functools.partial(solve_and_filter, damping),
        (jax.ShapeDtypeStruct(recorded.shape, BF16), jax.ShapeDtypeStruct((1, UNKNOWNS), F32)),
        (keep_rows, gram, trace, recorded),
        [VMEM] * 4,
        [pltpu.VMEM((SIDE, RECV), F32)],
    )
    return primaries, filters


def solution(mesh):
    placed = (
        P(None, "freq", None, "src"),
        P(None, "freq", None, "src"),
        P(None, "src"),
        P(),
        P(None, "freq", "src", None),
        P("freq"),
        P("freq"),
        P("freq", "src", None),
    )
    return jax.shard_map(
        body,
        mesh=mesh,
        in_specs=placed,
        out_specs=(P("freq", "src", None), P("freq", None)),
        check_vma=False,
    )
```

```python
import functools
import math

import jax
import jax.numpy as jnp
import ml_dtypes
import numpy as np
from jax import lax
from jax.experimental import pallas as pl
from jax.experimental.pallas import tpu as pltpu
from jax.sharding import Mesh, PartitionSpec as P

RECV = 128
NFFT = 512
F_LOW = 40
NEAR = 16
HALO = 8
LAGS_T = 9
LAGS_X = 3
LEAD = LAGS_T // 2
T_DEV = 32
WROWS = T_DEV + 2 * HALO
NF = 16
GROUP = 4
GROWS = 256
SIDE = 40
UNKNOWNS = LAGS_T * LAGS_X
TARGET_COL = GROUP * LEAD + 3
CENTRE_ROW = GROUP * LEAD + 1
PACK_AT = (0, 40, 72, 96, 112)
LOW_AT, RECIP_AT, GAP_AT, SLOT_ROWS = 16, 32, 48, 64
HALF = RECV // 2
VMEM = pl.BlockSpec(memory_space=pltpu.VMEM)
F32 = jnp.float32
BF16 = jnp.bfloat16


def split3(x):
    high = x.astype(ml_dtypes.bfloat16)
    rest = x - high.astype(np.float32)
    mid = rest.astype(ml_dtypes.bfloat16)
    low = (rest - mid.astype(np.float32)).astype(ml_dtypes.bfloat16)
    return high, mid, low


@functools.cache
def phase_rows():
    table = np.zeros((NF, GROWS, 256), ml_dtypes.bfloat16)
    freqs = np.arange(NF)
    scale = 1.0 / math.sqrt(NF)
    for window in range(NF):
        for row in range(WROWS):
            time = window * T_DEV - HALO + row
            if not 0 <= time < NFFT:
                continue
            turns = (F_LOW + freqs) * time % NFFT
            angle = turns * (2.0 * math.pi / NFFT)
            phase = np.stack([np.cos(angle), -np.sin(angle)], axis=0).reshape(-1) * scale
            high, mid, low = split3(phase.astype(np.float32))
            at = GROUP * (row + LEAD)
            table[window, at : at + 3, :192] = np.concatenate([high, high, mid, high, low, mid])
            table[window, at + 3, 192 + row] = 1
    return table


def halves(first, second):
    lanes = lax.broadcasted_iota(jnp.int32, first.shape, 1)
    low = jnp.where(lanes < HALF, first, pltpu.roll(second, HALF, 1))
    return low, jnp.where(lanes < HALF, pltpu.roll(first, HALF, 1), second)


def main_product(gap_ref, recip_ref, data_ref, weights_ref, out_ref, acc_ref, mask_ref):
    step = pl.program_id(0)
    depth = data_ref.shape[3]
    pairs = out_ref.shape[0]

    @pl.when(step == 0)
    def _():
        acc_ref[...] = jnp.zeros_like(acc_ref)
        gap = jnp.where(gap_ref[...] == 1, 1.0, 0.0)
        full = jnp.concatenate([gap, jnp.zeros((RECV - NEAR, RECV), F32)], axis=0)
        mask_ref[...] = (1.0 - full.T).astype(BF16)
        recip = recip_ref[...].astype(F32)
        recip = halves(recip[:NEAR], recip[NEAR:])
        gaps = gap, pltpu.roll(gap, HALF, 1)
        lanes = lax.broadcasted_iota(jnp.int32, (NEAR, RECV), 1)
        for half in range(2):
            out_ref[:, half, RECIP_AT:GAP_AT] = jnp.broadcast_to(
                recip[half].astype(BF16)[None], (pairs, NEAR, RECV)
            )
        for group in range(pairs // 2):
            at, off = RECV * (group // 4), 32 * (group % 4)
            real = weights_ref[0, 0, :NEAR, at : at + RECV].astype(F32)
            imag = weights_ref[1, 0, :NEAR, at : at + RECV].astype(F32)
            real = pltpu.roll(real, (HALF - off) % RECV, 1)
            imag = pltpu.roll(imag, (HALF + 32 - off) % RECV, 1)
            near = jnp.where(lanes < HALF + 32, real, imag)
            for half in range(2):
                tile = jnp.where(lanes < HALF, gaps[half], near).astype(BF16)
                out_ref[2 * group : 2 * group + 2, half, GAP_AT:] = jnp.broadcast_to(tile[None], (2, NEAR, RECV))

    @pl.when(step == 1)
    def _():
        mask_ref[...] = jnp.ones_like(mask_ref)

    panel = data_ref[...].reshape(2 * RECV, depth)
    mask = mask_ref[...]
    near = panel[:, :RECV] * jnp.concatenate([mask, mask], axis=0)
    panel = jnp.concatenate([near, panel[:, RECV:]], axis=1)
    both = jnp.concatenate([weights_ref[0, 0], weights_ref[1, 0]], axis=1)
    product = jnp.dot(panel, both, preferred_element_type=F32)
    width = product.shape[1] // 2
    acc_ref[0] += product[:RECV, :width] - product[RECV:, width:]
    acc_ref[1] += product[:RECV, width:] + product[RECV:, :width]

    @pl.when(step == pl.num_programs(0) - 1)
    def _():
        for half, pred in enumerate(halves(acc_ref[0].T, acc_ref[1].T)):
            high, low = two_parts(pred.reshape(pairs, 16, RECV))
            out_ref[:, half, :LOW_AT] = high
            out_ref[:, half, LOW_AT:RECIP_AT] = low


def sum_and_fill(owner_ref, part_ref, out_ref, z_ref, w_ref, f_ref, block_ref, sem):
    slots = part_ref.shape[0]
    copy = pltpu.make_async_copy(owner_ref, block_ref, sem)
    copy.start()
    place = lax.rem(lax.axis_index("pair"), 2)
    total = jnp.zeros((16, RECV), F32)
    for j in range(slots):
        total = total + part_ref[j, :LOW_AT].astype(F32) + part_ref[j, LOW_AT:RECIP_AT].astype(F32)
    copy.wait()
    lanes = lax.broadcasted_iota(jnp.int32, (NEAR, RECV), 1)
    for j in range(slots):
        tile = part_ref[block_ref[j], GAP_AT:]
        gap = tile.astype(F32)
        gap = jnp.where(lanes < HALF, gap, pltpu.roll(gap, HALF, 1))
        at = slice(NEAR * j, NEAR * j + NEAR)
        z_ref[at, :] = (part_ref[j, RECIP_AT:GAP_AT].astype(F32) * gap).astype(BF16)
        w_ref[at, :] = tile
    f_ref[...] = lax.dot_general(
        w_ref[...], z_ref[...], (((0,), (0,)), ((), ())), preferred_element_type=F32
    )
    at = pl.multiple_of(HALF + place * 16, 16)
    by_real = f_ref[pl.ds(at, 16), :]
    by_imag = pltpu.roll(f_ref[pl.ds(at + 32, 16), :], HALF, 1)
    pred = total + by_real + jnp.where(lanes < HALF, -by_imag, by_imag)
    out_ref[...] = jnp.broadcast_to(pred.reshape(1, 2, 8, RECV), out_ref.shape)


def two_parts(x):
    high = x.astype(BF16)
    return high, (x - high.astype(F32)).astype(BF16)


def trace_and_gram(keep_ref, x_ref, rows_ref, target_ref, gram_ref, trace_ref, a_ref, g_ref):
    sources = 8
    columns = []
    for s in range(sources):
        low, high = (x_ref[pl.ds(8 * half + s, NF, stride=16), :] for half in range(2))
        columns.append(jnp.concatenate(halves(low, high), axis=0))
    x = jnp.concatenate(columns, axis=1)
    high, rest = x.astype(BF16), x
    rest = rest - high.astype(F32)
    mid = rest.astype(BF16)
    low = (rest - mid.astype(F32)).astype(BF16)
    stack = jnp.concatenate([high, mid, high, low, high, mid, target_ref[...]], axis=0)
    base = jnp.dot(rows_ref[...], stack, preferred_element_type=F32)
    lag = lax.rem(lax.broadcasted_iota(jnp.int32, (GROWS, RECV), 0), GROUP)
    recv = lax.broadcasted_iota(jnp.int32, (GROWS, RECV), 1)
    ahead = (lag == 0) & (recv < RECV - 1)
    behind = (lag == 2) & (recv > 0)
    same = (lag == 1) | (lag == 3)
    for s in range(sources):
        at = slice(s * RECV, (s + 1) * RECV)
        here = base[:, at]
        shifted = jnp.where(
            same,
            here,
            jnp.where(
                ahead,
                pltpu.roll(here, RECV - 1, 1),
                jnp.where(behind, pltpu.roll(here, 1, 1), 0.0),
            ),
        )
        a_ref[s * GROWS : (s + 1) * GROWS, :] = shifted
    for s in range(sources):
        mine = a_ref[pl.ds(s * GROWS + 1, WROWS + 2 * LEAD, stride=GROUP), :]
        trace_ref[pl.ds(s, WROWS + 2 * LEAD, stride=sources), :] = mine
    high, low = two_parts(jnp.concatenate([a_ref[s * GROWS : (s + 1) * GROWS, :] for s in range(sources)], axis=1))
    dims = (((1,), (1,)), ((), ()))
    g_ref[...] = lax.dot_general(high, high, dims, preferred_element_type=F32) + 2.0 * lax.dot_general(
        high, low, dims, preferred_element_type=F32
    )
    total = jnp.zeros((SIDE, RECV), F32)
    for u in range(WROWS):
        at = GROUP * u
        if at + SIDE <= RECV:
            part = g_ref[at : at + SIDE, :RECV]
            part = pltpu.roll(part, (RECV - at) % RECV, 1)
        elif at >= RECV:
            part = g_ref[at : at + SIDE, RECV:]
            part = pltpu.roll(part, (2 * RECV - at) % RECV, 1)
        else:
            part = pltpu.roll(g_ref[at : at + SIDE, :], 2 * RECV - at, 1)[:, :RECV]
        total = total + part * keep_ref[u : u + 1, :]
    full = jnp.concatenate([total, jnp.zeros((RECV - SIDE, RECV), F32)], axis=0)
    total = 0.5 * (total + full.T[:SIDE])
    lanes = lax.broadcasted_iota(jnp.int32, (8, RECV), 1)
    packed = jnp.zeros((8, RECV), F32)
    for g, at in enumerate(PACK_AT):
        piece = total[8 * g : 8 * g + 8]
        piece = jnp.where((lanes >= 8 * g) & (lanes < SIDE), piece, 0.0)
        packed = packed + pltpu.roll(piece, at - 8 * g, 1)
    gram_ref[...] = jnp.broadcast_to(packed[None], gram_ref.shape)


def solve_and_filter(damping, keep_ref, gram_ref, trace_ref, recorded_ref, out_ref, filters_ref, h_ref):
    packed = jnp.sum(gram_ref[...], axis=0)
    lanes = lax.broadcasted_iota(jnp.int32, (8, RECV), 1)
    pieces = []
    for g, at in enumerate(PACK_AT):
        piece = pltpu.roll(packed, (RECV + 8 * g - at) % RECV, 1)
        pieces.append(jnp.where((lanes >= 8 * g) & (lanes < SIDE), piece, 0.0))
    upper = jnp.concatenate(pieces, axis=0)
    full = jnp.concatenate([upper, jnp.zeros((RECV - SIDE, RECV), F32)], axis=0)
    row = lax.broadcasted_iota(jnp.int32, (SIDE, RECV), 0)
    lane = lax.broadcasted_iota(jnp.int32, (SIDE, RECV), 1)
    system = jnp.where(lane // 8 < row // 8, full.T[:SIDE], upper)
    unknown = lax.rem(row, GROUP) < LAGS_X
    system = system + jnp.where((row == lane) & unknown, damping, 0.0)
    system = system + jnp.where((row == CENTRE_ROW) & (lane == TARGET_COL), damping, 0.0)
    order = [k for k in range(GROUP * LAGS_T) if k % GROUP < LAGS_X]
    for one, two in zip(order[:-1:2], order[1::2]):
        first = jnp.broadcast_to(system[:, one : one + 1], (SIDE, RECV))
        second = jnp.broadcast_to(system[:, two : two + 1], (SIDE, RECV))
        top, bottom = system[one : one + 1, :], system[two : two + 1, :]
        a, b, d = first[one : one + 1], second[one : one + 1], second[two : two + 1]
        scale = 1.0 / (a * d - b * b)
        top, bottom = (d * top - b * bottom) * scale, (a * bottom - b * top) * scale
        rest = system - first * top - second * bottom
        system = jnp.where(row == one, top, jnp.where(row == two, bottom, rest))
    last = order[-1]
    column = jnp.broadcast_to(system[:, last : last + 1], (SIDE, RECV))
    pivot_row = system[last : last + 1, :] / column[last : last + 1]
    system = jnp.where(row == last, pivot_row, system - column * pivot_row)
    chosen = (lane < UNKNOWNS) & (row == GROUP * (LAGS_T - 1 - lane // LAGS_X) + lane % LAGS_X)
    h_ref[...] = jnp.broadcast_to(system[:, TARGET_COL : TARGET_COL + 1], (SIDE, RECV))
    filters_ref[...] = jnp.sum(jnp.where(chosen, h_ref[...], 0.0), axis=0, keepdims=True)[:, :UNKNOWNS]
    recv = lax.broadcasted_iota(jnp.int32, (8, RECV), 1)
    taps = [[jnp.broadcast_to(h_ref[GROUP * p + c : GROUP * p + c + 1, :], (8, RECV)) for c in range(LAGS_X)] for p in range(LAGS_T)]
    for u in range(WROWS):
        sums = [None] * LAGS_X
        for p in range(LAGS_T):
            value = trace_ref[8 * (u + p) : 8 * (u + p) + 8, :]
            for c in range(LAGS_X):
                term = taps[p][c] * value
                sums[c] = term if sums[c] is None else sums[c] + term
        ahead = jnp.where(recv < RECV - 1, pltpu.roll(sums[0], RECV - 1, 1), 0.0)
        behind = jnp.where(recv > 0, pltpu.roll(sums[2], 1, 1), 0.0)
        value = recorded_ref[u].astype(F32) - (sums[1] + ahead + behind)
        out_ref[u] = (value * keep_ref[u : u + 1, :]).astype(BF16)


def call(kernel, out_shape, args, specs, scratch=(), flops=1000000):
    return pl.pallas_call(
        kernel,
        out_shape=out_shape,
        in_specs=specs,
        out_specs=jax.tree.map(lambda _: VMEM, out_shape),
        scratch_shapes=list(scratch),
        compiler_params=pltpu.CompilerParams(vmem_limit_bytes=32 * 2**20),
        cost_estimate=pl.CostEstimate(flops=flops, bytes_accessed=1000000, transcendentals=0),
    )(*args)


def body(data, recip, gap, owner, weights, start_row, end_row, recorded):
    freq_here = lax.axis_index("freq")
    src_count = lax.axis_size("pair") * lax.axis_size("half")
    pairs = src_count // 2
    total_out = weights.shape[3]
    points = data.shape[3]

    recip_rows = jnp.swapaxes(recip[:, 0], 1, 2).reshape(2 * NEAR, RECV)
    depth = points // 2
    parts = pl.pallas_call(
        main_product,
        grid=(points // depth,),
        out_shape=jax.ShapeDtypeStruct((pairs, 2, SLOT_ROWS, RECV), BF16),
        in_specs=[
            pl.BlockSpec((NEAR, RECV), lambda k: (0, 0)),
            pl.BlockSpec((2 * NEAR, RECV), lambda k: (0, 0)),
            pl.BlockSpec((2, 1, RECV, depth), lambda k: (0, 0, 0, k)),
            pl.BlockSpec((2, 1, depth, total_out), lambda k: (0, 0, k, 0)),
        ],
        out_specs=pl.BlockSpec((pairs, 2, SLOT_ROWS, RECV), lambda k: (0, 0, 0, 0)),
        scratch_shapes=[pltpu.VMEM((2, RECV, total_out), F32), pltpu.VMEM((RECV, RECV), BF16)],
        cost_estimate=pl.CostEstimate(flops=8 * RECV * points * total_out, bytes_accessed=5000000, transcendentals=0),
    )(gap.T, recip_rows, data, weights)
    parts = parts.reshape(src_count, SLOT_ROWS, RECV)
    parts = lax.all_to_all(parts, ("pair", "half"), 0, 0, tiled=True)
    copies = call(
        sum_and_fill,
        jax.ShapeDtypeStruct((NF, 2, 8, RECV), F32),
        (owner, parts),
        [pl.BlockSpec(memory_space=pl.ANY), VMEM],
        [
            pltpu.VMEM((NEAR * src_count, RECV), BF16),
            pltpu.VMEM((NEAR * src_count, RECV), BF16),
            pltpu.VMEM((RECV, RECV), F32),
            pltpu.SMEM((src_count,), jnp.int32),
            pltpu.SemaphoreType.DMA,
        ],
    )
    copies = copies.reshape(NF * 2, 8, RECV)
    spread = lax.all_to_all(copies, ("freq", "half"), 0, 0, tiled=True).reshape(NF * 16, RECV)

    begin = freq_here * T_DEV - HALO
    first, last = start_row[0] - begin, end_row[0] - begin
    row = lax.broadcasted_iota(jnp.int32, (WROWS, RECV), 0)
    keep_rows = ((row >= first) & (row < last)).astype(F32)
    row = jnp.arange(GROWS, dtype=jnp.int32) // GROUP - LEAD
    keep = (row >= first) & (row < last)
    rows = lax.dynamic_index_in_dim(jnp.asarray(phase_rows()), freq_here, 0, keepdims=False)
    rows = jnp.where(keep[:, None], rows, jnp.zeros_like(rows))
    target = jnp.pad(recorded.reshape(WROWS, -1), ((0, 16), (0, 0)))
    trace_rows = 8 * (WROWS + 2 * LEAD)
    gram, trace = call(
        trace_and_gram,
        (jax.ShapeDtypeStruct((src_count, 8, RECV), F32), jax.ShapeDtypeStruct((trace_rows, RECV), F32)),
        (keep_rows, spread, rows, target),
        [VMEM] * 4,
        [pltpu.VMEM((8 * GROWS, RECV), F32), pltpu.VMEM((GROWS, GROWS), F32)],
    )
    gram = lax.all_to_all(gram, ("pair", "half"), 0, 0, tiled=True)
    damping = float(WROWS * total_out * RECV)
    primaries, filters = call(
        functools.partial(solve_and_filter, damping),
        (jax.ShapeDtypeStruct(recorded.shape, BF16), jax.ShapeDtypeStruct((1, UNKNOWNS), F32)),
        (keep_rows, gram, trace, recorded),
        [VMEM] * 4,
        [pltpu.VMEM((SIDE, RECV), F32)],
    )
    return primaries, filters


def solution(mesh):
    freq, src = mesh.devices.shape
    mesh = Mesh(mesh.devices.reshape(freq, src // 2, 2), ("freq", "pair", "half"))
    src = ("pair", "half")
    placed = (
        P(None, "freq", None, src),
        P(None, "freq", None, src),
        P(None, src),
        P(),
        P(None, "freq", src, None),
        P("freq"),
        P("freq"),
        P("freq", src, None),
    )
    return jax.shard_map(
        body,
        mesh=mesh,
        in_specs=placed,
        out_specs=(P("freq", src, None), P("freq", None)),
        check_vma=False,
    )
```

```python
import functools
import math

import jax
import jax.numpy as jnp
import ml_dtypes
import numpy as np
from jax import lax
from jax.experimental import pallas as pl
from jax.experimental.pallas import tpu as pltpu
from jax.sharding import Mesh, PartitionSpec as P

RECV = 128
NFFT = 512
F_LOW = 40
NEAR = 16
HALO = 8
LAGS_T = 9
LAGS_X = 3
LEAD = LAGS_T // 2
T_DEV = 32
WROWS = T_DEV + 2 * HALO
NF = 16
GROUP = 4
GROWS = 256
SIDE = 40
UNKNOWNS = LAGS_T * LAGS_X
TARGET_COL = GROUP * LEAD + 3
CENTRE_ROW = GROUP * LEAD + 1
PACK_AT = (0, 40, 72, 96, 112)
LOW_AT, RECIP_AT, GAP_AT, SLOT_ROWS = 16, 32, 48, 64
HALF = RECV // 2
VMEM = pl.BlockSpec(memory_space=pltpu.VMEM)
F32 = jnp.float32
BF16 = jnp.bfloat16


def split3(x):
    high = x.astype(ml_dtypes.bfloat16)
    rest = x - high.astype(np.float32)
    mid = rest.astype(ml_dtypes.bfloat16)
    low = (rest - mid.astype(np.float32)).astype(ml_dtypes.bfloat16)
    return high, mid, low


@functools.cache
def phase_rows():
    table = np.zeros((NF, GROWS, 256), ml_dtypes.bfloat16)
    freqs = np.arange(NF)
    scale = 1.0 / math.sqrt(NF)
    for window in range(NF):
        for row in range(WROWS):
            time = window * T_DEV - HALO + row
            if not 0 <= time < NFFT:
                continue
            turns = (F_LOW + freqs) * time % NFFT
            angle = turns * (2.0 * math.pi / NFFT)
            phase = np.stack([np.cos(angle), -np.sin(angle)], axis=0).reshape(-1) * scale
            high, mid, low = split3(phase.astype(np.float32))
            at = GROUP * (row + LEAD)
            table[window, at : at + 3, :192] = np.concatenate([high, high, mid, high, low, mid])
            table[window, at + 3, 192 + row] = 1
    return table


def halves(first, second):
    lanes = lax.broadcasted_iota(jnp.int32, first.shape, 1)
    low = jnp.where(lanes < HALF, first, pltpu.roll(second, HALF, 1))
    return low, jnp.where(lanes < HALF, pltpu.roll(first, HALF, 1), second)


def main_product(gap_ref, recip_ref, data_ref, weights_ref, out_ref, acc_ref, mask_ref):
    step = pl.program_id(0)
    depth = data_ref.shape[3]
    pairs = out_ref.shape[0]

    @pl.when(step == 0)
    def _():
        acc_ref[...] = jnp.zeros_like(acc_ref)
        gap = jnp.where(gap_ref[...] == 1, 1.0, 0.0)
        full = jnp.concatenate([gap, jnp.zeros((RECV - NEAR, RECV), F32)], axis=0)
        mask_ref[...] = (1.0 - full.T).astype(BF16)
        recip = recip_ref[...].astype(F32)
        recip = halves(recip[:NEAR], recip[NEAR:])
        gaps = gap, pltpu.roll(gap, HALF, 1)
        lanes = lax.broadcasted_iota(jnp.int32, (NEAR, RECV), 1)
        for half in range(2):
            out_ref[:, half, RECIP_AT:GAP_AT] = jnp.broadcast_to(
                recip[half].astype(BF16)[None], (pairs, NEAR, RECV)
            )
        for group in range(pairs // 2):
            at, off = RECV * (group // 4), 32 * (group % 4)
            real = weights_ref[0, 0, :NEAR, at : at + RECV].astype(F32)
            imag = weights_ref[1, 0, :NEAR, at : at + RECV].astype(F32)
            real = pltpu.roll(real, (HALF - off) % RECV, 1)
            imag = pltpu.roll(imag, (HALF + 32 - off) % RECV, 1)
            near = jnp.where(lanes < HALF + 32, real, imag)
            for half in range(2):
                tile = jnp.where(lanes < HALF, gaps[half], near).astype(BF16)
                out_ref[2 * group : 2 * group + 2, half, GAP_AT:] = jnp.broadcast_to(tile[None], (2, NEAR, RECV))

    @pl.when(step == 1)
    def _():
        mask_ref[...] = jnp.ones_like(mask_ref)

    panel = data_ref[...].reshape(2 * RECV, depth)
    mask = mask_ref[...]
    near = panel[:, :RECV] * jnp.concatenate([mask, mask], axis=0)
    panel = jnp.concatenate([near, panel[:, RECV:]], axis=1)
    both = jnp.concatenate([weights_ref[0, 0], weights_ref[1, 0]], axis=1)
    product = jnp.dot(panel, both, preferred_element_type=F32)
    width = product.shape[1] // 2
    acc_ref[0] += product[:RECV, :width] - product[RECV:, width:]
    acc_ref[1] += product[:RECV, width:] + product[RECV:, :width]

    @pl.when(step == pl.num_programs(0) - 1)
    def _():
        for half, pred in enumerate(halves(acc_ref[0].T, acc_ref[1].T)):
            high, low = two_parts(pred.reshape(pairs, 16, RECV))
            out_ref[:, half, :LOW_AT] = high
            out_ref[:, half, LOW_AT:RECIP_AT] = low


def sum_and_fill(owner_ref, part_ref, out_ref, z_ref, w_ref, f_ref):
    slots = part_ref.shape[0]
    place = lax.rem(lax.axis_index("pair"), 2)
    total = jnp.zeros((16, RECV), F32)
    for j in range(slots):
        total = total + part_ref[j, :LOW_AT].astype(F32) + part_ref[j, LOW_AT:RECIP_AT].astype(F32)
    lanes = lax.broadcasted_iota(jnp.int32, (NEAR, RECV), 1)
    for j in range(slots):
        tile = part_ref[owner_ref[0, j], GAP_AT:]
        gap = tile.astype(F32)
        gap = jnp.where(lanes < HALF, gap, pltpu.roll(gap, HALF, 1))
        at = slice(NEAR * j, NEAR * j + NEAR)
        z_ref[at, :] = (part_ref[j, RECIP_AT:GAP_AT].astype(F32) * gap).astype(BF16)
        w_ref[at, :] = tile
    f_ref[...] = lax.dot_general(
        w_ref[...], z_ref[...], (((0,), (0,)), ((), ())), preferred_element_type=F32
    )
    at = pl.multiple_of(HALF + place * 16, 16)
    by_real = f_ref[pl.ds(at, 16), :]
    by_imag = pltpu.roll(f_ref[pl.ds(at + 32, 16), :], HALF, 1)
    pred = total + by_real + jnp.where(lanes < HALF, -by_imag, by_imag)
    out_ref[...] = jnp.broadcast_to(pred.reshape(1, 2, 8, RECV), out_ref.shape)


def two_parts(x):
    high = x.astype(BF16)
    return high, (x - high.astype(F32)).astype(BF16)


def trace_and_gram(keep_ref, x_ref, rows_ref, target_ref, gram_ref, trace_ref, a_ref, g_ref):
    sources = 8
    columns = []
    for s in range(sources):
        low, high = (x_ref[pl.ds(8 * half + s, NF, stride=16), :] for half in range(2))
        columns.append(jnp.concatenate(halves(low, high), axis=0))
    x = jnp.concatenate(columns, axis=1)
    high, rest = x.astype(BF16), x
    rest = rest - high.astype(F32)
    mid = rest.astype(BF16)
    low = (rest - mid.astype(F32)).astype(BF16)
    stack = jnp.concatenate([high, mid, high, low, high, mid, target_ref[...]], axis=0)
    base = jnp.dot(rows_ref[...], stack, preferred_element_type=F32)
    lag = lax.rem(lax.broadcasted_iota(jnp.int32, (GROWS, RECV), 0), GROUP)
    recv = lax.broadcasted_iota(jnp.int32, (GROWS, RECV), 1)
    ahead = (lag == 0) & (recv < RECV - 1)
    behind = (lag == 2) & (recv > 0)
    same = (lag == 1) | (lag == 3)
    for s in range(sources):
        at = slice(s * RECV, (s + 1) * RECV)
        here = base[:, at]
        shifted = jnp.where(
            same,
            here,
            jnp.where(
                ahead,
                pltpu.roll(here, RECV - 1, 1),
                jnp.where(behind, pltpu.roll(here, 1, 1), 0.0),
            ),
        )
        a_ref[s * GROWS : (s + 1) * GROWS, :] = shifted
    for s in range(sources):
        mine = a_ref[pl.ds(s * GROWS + 1, WROWS + 2 * LEAD, stride=GROUP), :]
        trace_ref[pl.ds(s, WROWS + 2 * LEAD, stride=sources), :] = mine
    high, low = two_parts(jnp.concatenate([a_ref[s * GROWS : (s + 1) * GROWS, :] for s in range(sources)], axis=1))
    dims = (((1,), (1,)), ((), ()))
    g_ref[...] = lax.dot_general(high, high, dims, preferred_element_type=F32) + 2.0 * lax.dot_general(
        high, low, dims, preferred_element_type=F32
    )
    total = jnp.zeros((SIDE, RECV), F32)
    for u in range(WROWS):
        at = GROUP * u
        if at + SIDE <= RECV:
            part = g_ref[at : at + SIDE, :RECV]
            part = pltpu.roll(part, (RECV - at) % RECV, 1)
        elif at >= RECV:
            part = g_ref[at : at + SIDE, RECV:]
            part = pltpu.roll(part, (2 * RECV - at) % RECV, 1)
        else:
            part = pltpu.roll(g_ref[at : at + SIDE, :], 2 * RECV - at, 1)[:, :RECV]
        total = total + part * keep_ref[u : u + 1, :]
    full = jnp.concatenate([total, jnp.zeros((RECV - SIDE, RECV), F32)], axis=0)
    total = 0.5 * (total + full.T[:SIDE])
    lanes = lax.broadcasted_iota(jnp.int32, (8, RECV), 1)
    packed = jnp.zeros((8, RECV), F32)
    for g, at in enumerate(PACK_AT):
        piece = total[8 * g : 8 * g + 8]
        piece = jnp.where((lanes >= 8 * g) & (lanes < SIDE), piece, 0.0)
        packed = packed + pltpu.roll(piece, at - 8 * g, 1)
    gram_ref[...] = jnp.broadcast_to(packed[None], gram_ref.shape)


def solve_and_filter(damping, keep_ref, gram_ref, trace_ref, recorded_ref, out_ref, filters_ref, h_ref):
    packed = jnp.sum(gram_ref[...], axis=0)
    lanes = lax.broadcasted_iota(jnp.int32, (8, RECV), 1)
    pieces = []
    for g, at in enumerate(PACK_AT):
        piece = pltpu.roll(packed, (RECV + 8 * g - at) % RECV, 1)
        pieces.append(jnp.where((lanes >= 8 * g) & (lanes < SIDE), piece, 0.0))
    upper = jnp.concatenate(pieces, axis=0)
    full = jnp.concatenate([upper, jnp.zeros((RECV - SIDE, RECV), F32)], axis=0)
    row = lax.broadcasted_iota(jnp.int32, (SIDE, RECV), 0)
    lane = lax.broadcasted_iota(jnp.int32, (SIDE, RECV), 1)
    system = jnp.where(lane // 8 < row // 8, full.T[:SIDE], upper)
    unknown = lax.rem(row, GROUP) < LAGS_X
    system = system + jnp.where((row == lane) & unknown, damping, 0.0)
    system = system + jnp.where((row == CENTRE_ROW) & (lane == TARGET_COL), damping, 0.0)
    order = [k for k in range(GROUP * LAGS_T) if k % GROUP < LAGS_X]
    for one, two in zip(order[:-1:2], order[1::2]):
        first = jnp.broadcast_to(system[:, one : one + 1], (SIDE, RECV))
        second = jnp.broadcast_to(system[:, two : two + 1], (SIDE, RECV))
        top, bottom = system[one : one + 1, :], system[two : two + 1, :]
        a, b, d = first[one : one + 1], second[one : one + 1], second[two : two + 1]
        scale = 1.0 / (a * d - b * b)
        top, bottom = (d * top - b * bottom) * scale, (a * bottom - b * top) * scale
        rest = system - first * top - second * bottom
        system = jnp.where(row == one, top, jnp.where(row == two, bottom, rest))
    last = order[-1]
    column = jnp.broadcast_to(system[:, last : last + 1], (SIDE, RECV))
    pivot_row = system[last : last + 1, :] / column[last : last + 1]
    system = jnp.where(row == last, pivot_row, system - column * pivot_row)
    chosen = (lane < UNKNOWNS) & (row == GROUP * (LAGS_T - 1 - lane // LAGS_X) + lane % LAGS_X)
    h_ref[...] = jnp.broadcast_to(system[:, TARGET_COL : TARGET_COL + 1], (SIDE, RECV))
    filters_ref[...] = jnp.sum(jnp.where(chosen, h_ref[...], 0.0), axis=0, keepdims=True)[:, :UNKNOWNS]
    recv = lax.broadcasted_iota(jnp.int32, (8, RECV), 1)
    taps = [[jnp.broadcast_to(h_ref[GROUP * p + c : GROUP * p + c + 1, :], (8, RECV)) for c in range(LAGS_X)] for p in range(LAGS_T)]
    for u in range(WROWS):
        sums = [None] * LAGS_X
        for p in range(LAGS_T):
            value = trace_ref[8 * (u + p) : 8 * (u + p) + 8, :]
            for c in range(LAGS_X):
                term = taps[p][c] * value
                sums[c] = term if sums[c] is None else sums[c] + term
        ahead = jnp.where(recv < RECV - 1, pltpu.roll(sums[0], RECV - 1, 1), 0.0)
        behind = jnp.where(recv > 0, pltpu.roll(sums[2], 1, 1), 0.0)
        value = recorded_ref[u].astype(F32) - (sums[1] + ahead + behind)
        out_ref[u] = (value * keep_ref[u : u + 1, :]).astype(BF16)


def call(kernel, out_shape, args, specs, scratch=(), flops=1000000):
    return pl.pallas_call(
        kernel,
        out_shape=out_shape,
        in_specs=specs,
        out_specs=jax.tree.map(lambda _: VMEM, out_shape),
        scratch_shapes=list(scratch),
        compiler_params=pltpu.CompilerParams(vmem_limit_bytes=32 * 2**20),
        cost_estimate=pl.CostEstimate(flops=flops, bytes_accessed=1000000, transcendentals=0),
    )(*args)


def body(data, recip, gap, owner, weights, start_row, end_row, recorded):
    freq_here = lax.axis_index("freq")
    src_count = lax.axis_size("pair") * lax.axis_size("half")
    pairs = src_count // 2
    total_out = weights.shape[3]
    points = data.shape[3]

    recip_rows = jnp.swapaxes(recip[:, 0], 1, 2).reshape(2 * NEAR, RECV)
    depth = points // 2
    parts = pl.pallas_call(
        main_product,
        grid=(points // depth,),
        out_shape=jax.ShapeDtypeStruct((pairs, 2, SLOT_ROWS, RECV), BF16),
        in_specs=[
            pl.BlockSpec((NEAR, RECV), lambda k: (0, 0)),
            pl.BlockSpec((2 * NEAR, RECV), lambda k: (0, 0)),
            pl.BlockSpec((2, 1, RECV, depth), lambda k: (0, 0, 0, k)),
            pl.BlockSpec((2, 1, depth, total_out), lambda k: (0, 0, k, 0)),
        ],
        out_specs=pl.BlockSpec((pairs, 2, SLOT_ROWS, RECV), lambda k: (0, 0, 0, 0)),
        scratch_shapes=[pltpu.VMEM((2, RECV, total_out), F32), pltpu.VMEM((RECV, RECV), BF16)],
        cost_estimate=pl.CostEstimate(flops=8 * RECV * points * total_out, bytes_accessed=5000000, transcendentals=0),
    )(gap.T, recip_rows, data, weights)
    parts = parts.reshape(src_count, SLOT_ROWS, RECV)
    parts = lax.all_to_all(parts, ("pair", "half"), 0, 0, tiled=True)
    copies = call(
        sum_and_fill,
        jax.ShapeDtypeStruct((NF, 2, 8, RECV), F32),
        (owner.reshape(1, src_count), parts),
        [VMEM, VMEM],
        [
            pltpu.VMEM((NEAR * src_count, RECV), BF16),
            pltpu.VMEM((NEAR * src_count, RECV), BF16),
            pltpu.VMEM((RECV, RECV), F32),
        ],
    )
    copies = copies.reshape(NF * 2, 8, RECV)
    spread = lax.all_to_all(copies, ("freq", "half"), 0, 0, tiled=True).reshape(NF * 16, RECV)

    begin = freq_here * T_DEV - HALO
    first, last = start_row[0] - begin, end_row[0] - begin
    row = lax.broadcasted_iota(jnp.int32, (WROWS, RECV), 0)
    keep_rows = ((row >= first) & (row < last)).astype(F32)
    row = jnp.arange(GROWS, dtype=jnp.int32) // GROUP - LEAD
    keep = (row >= first) & (row < last)
    rows = lax.dynamic_index_in_dim(jnp.asarray(phase_rows()), freq_here, 0, keepdims=False)
    rows = jnp.where(keep[:, None], rows, jnp.zeros_like(rows))
    target = jnp.pad(recorded.reshape(WROWS, -1), ((0, 16), (0, 0)))
    trace_rows = 8 * (WROWS + 2 * LEAD)
    gram, trace = call(
        trace_and_gram,
        (jax.ShapeDtypeStruct((src_count, 8, RECV), F32), jax.ShapeDtypeStruct((trace_rows, RECV), F32)),
        (keep_rows, spread, rows, target),
        [VMEM] * 4,
        [pltpu.VMEM((8 * GROWS, RECV), F32), pltpu.VMEM((GROWS, GROWS), F32)],
    )
    gram = lax.all_to_all(gram, ("pair", "half"), 0, 0, tiled=True)
    damping = float(WROWS * total_out * RECV)
    primaries, filters = call(
        functools.partial(solve_and_filter, damping),
        (jax.ShapeDtypeStruct(recorded.shape, BF16), jax.ShapeDtypeStruct((1, UNKNOWNS), F32)),
        (keep_rows, gram, trace, recorded),
        [VMEM] * 4,
        [pltpu.VMEM((SIDE, RECV), F32)],
    )
    return primaries, filters


def solution(mesh):
    freq, src = mesh.devices.shape
    mesh = Mesh(mesh.devices.reshape(freq, src // 2, 2), ("freq", "pair", "half"))
    src = ("pair", "half")
    placed = (
        P(None, "freq", None, src),
        P(None, "freq", None, src),
        P(None, src),
        P(),
        P(None, "freq", src, None),
        P("freq"),
        P("freq"),
        P("freq", src, None),
    )
    return jax.shard_map(
        body,
        mesh=mesh,
        in_specs=placed,
        out_specs=(P("freq", src, None), P("freq", None)),
        check_vma=False,
    )
```

```python
import functools
import math

import jax
import jax.numpy as jnp
import ml_dtypes
import numpy as np
from jax import lax
from jax.experimental import pallas as pl
from jax.experimental.pallas import tpu as pltpu
from jax.sharding import Mesh, PartitionSpec as P

RECV = 128
NFFT = 512
F_LOW = 40
NEAR = 16
HALO = 8
LAGS_T = 9
LAGS_X = 3
LEAD = LAGS_T // 2
T_DEV = 32
WROWS = T_DEV + 2 * HALO
NF = 16
GROUP = 4
GROWS = 256
SIDE = 40
UNKNOWNS = LAGS_T * LAGS_X
TARGET_COL = GROUP * LEAD + 3
CENTRE_ROW = GROUP * LEAD + 1
PACK_AT = (0, 40, 72, 96, 112)
RECIP_AT, GAP_AT, SLOT_ROWS = 16, 32, 48
HALF = RECV // 2
IMAG_AT, SCALE_AT = HALF + 16, HALF + 32
SPAN = 166.0
VMEM = pl.BlockSpec(memory_space=pltpu.VMEM)
F32 = jnp.float32
BF16 = jnp.bfloat16


def split3(x):
    high = x.astype(ml_dtypes.bfloat16)
    rest = x - high.astype(np.float32)
    mid = rest.astype(ml_dtypes.bfloat16)
    low = (rest - mid.astype(np.float32)).astype(ml_dtypes.bfloat16)
    return high, mid, low


@functools.cache
def phase_rows():
    table = np.zeros((NF, GROWS, 256), ml_dtypes.bfloat16)
    freqs = np.arange(NF)
    scale = 1.0 / math.sqrt(NF)
    for window in range(NF):
        for row in range(WROWS):
            time = window * T_DEV - HALO + row
            if not 0 <= time < NFFT:
                continue
            turns = (F_LOW + freqs) * time % NFFT
            angle = turns * (2.0 * math.pi / NFFT)
            phase = np.stack([np.cos(angle), -np.sin(angle)], axis=0).reshape(-1) * scale
            high, mid, low = split3(phase.astype(np.float32))
            at = GROUP * (row + LEAD)
            table[window, at : at + 3, :192] = np.concatenate([high, high, mid, high, low, mid])
            table[window, at + 3, 192 + row] = 1
    return table


def halves(first, second):
    lanes = lax.broadcasted_iota(jnp.int32, first.shape, 1)
    low = jnp.where(lanes < HALF, first, pltpu.roll(second, HALF, 1))
    return low, jnp.where(lanes < HALF, pltpu.roll(first, HALF, 1), second)


def encode(value, scale):
    size = jnp.exp(jnp.abs(value) * (SPAN / scale) - SPAN / 2)
    return jnp.where(value < 0, -size, size)


def decode(code, scale):
    size = (jnp.log(jnp.abs(code)) + SPAN / 2) * (scale * (1.0 / SPAN))
    return jnp.where(code < 0, -size, size)


def main_product(gap_ref, recip_ref, data_ref, weights_ref, out_ref, acc_ref, mask_ref, near_ref):
    step = pl.program_id(0)
    depth = data_ref.shape[3]
    pairs = out_ref.shape[0]

    @pl.when(step == 0)
    def _():
        acc_ref[...] = jnp.zeros_like(acc_ref)
        gap = jnp.where(gap_ref[...] == 1, 1.0, 0.0)
        full = jnp.concatenate([gap, jnp.zeros((RECV - NEAR, RECV), F32)], axis=0)
        mask_ref[...] = (1.0 - full.T).astype(BF16)
        recip = recip_ref[...].astype(F32)
        recip = halves(recip[:NEAR], recip[NEAR:])
        lanes = lax.broadcasted_iota(jnp.int32, (NEAR, RECV), 1)
        for half in range(2):
            out_ref[:, half, RECIP_AT:GAP_AT] = jnp.broadcast_to(
                recip[half].astype(BF16)[None], (pairs, NEAR, RECV)
            )
        for pair in range(pairs):
            at, off = RECV * (pair // 8), 16 * (pair % 8)
            real = weights_ref[0, 0, :NEAR, at : at + RECV].astype(F32)
            imag = weights_ref[1, 0, :NEAR, at : at + RECV].astype(F32)
            real = pltpu.roll(real, (HALF - off) % RECV, 1)
            imag = pltpu.roll(imag, (IMAG_AT - off) % RECV, 1)
            near_ref[pair] = jnp.where(lanes < IMAG_AT, real, imag)

    @pl.when(step == 1)
    def _():
        mask_ref[...] = jnp.ones_like(mask_ref)

    panel = data_ref[...].reshape(2 * RECV, depth)
    mask = mask_ref[...]
    near = panel[:, :RECV] * jnp.concatenate([mask, mask], axis=0)
    panel = jnp.concatenate([near, panel[:, RECV:]], axis=1)
    both = jnp.concatenate([weights_ref[0, 0], weights_ref[1, 0]], axis=1)
    product = jnp.dot(panel, both, preferred_element_type=F32)
    width = product.shape[1] // 2
    acc_ref[0] += product[:RECV, :width] - product[RECV:, width:]
    acc_ref[1] += product[:RECV, width:] + product[RECV:, :width]

    @pl.when(step == pl.num_programs(0) - 1)
    def _():
        gap = jnp.where(gap_ref[...] == 1, 1.0, 0.0)
        gaps = gap, pltpu.roll(gap, HALF, 1)
        lanes = lax.broadcasted_iota(jnp.int32, (pairs, NEAR, RECV), 2)
        for half, pred in enumerate(halves(acc_ref[0].T, acc_ref[1].T)):
            pred = pred.reshape(pairs, 16, RECV)
            scale = jnp.max(jnp.abs(pred), axis=(1, 2), keepdims=True) * 1.01 + 1e-30
            scale = scale.astype(BF16).astype(F32)
            out_ref[:, half, :RECIP_AT] = encode(pred, scale).astype(BF16)
            tile = jnp.where(lanes < SCALE_AT, near_ref[...], jnp.broadcast_to(scale, lanes.shape))
            tile = jnp.where(lanes < HALF, jnp.broadcast_to(gaps[half][None], lanes.shape), tile)
            out_ref[:, half, GAP_AT:] = tile.astype(BF16)


def sum_and_fill(owner_ref, part_ref, out_ref, z_ref, w_ref, f_ref):
    slots = part_ref.shape[0]
    total = jnp.zeros((16, RECV), F32)
    for j in range(slots):
        scale = part_ref[j, GAP_AT:].astype(F32)[:, SCALE_AT : SCALE_AT + 1]
        code = part_ref[j, :RECIP_AT].astype(F32)
        total = total + decode(code, jnp.broadcast_to(scale, code.shape))
    lanes = lax.broadcasted_iota(jnp.int32, (NEAR, RECV), 1)
    for j in range(slots):
        tile = part_ref[owner_ref[0, j], GAP_AT:]
        gap = tile.astype(F32)
        gap = jnp.where(lanes < HALF, gap, pltpu.roll(gap, HALF, 1))
        at = slice(NEAR * j, NEAR * j + NEAR)
        z_ref[at, :] = (part_ref[j, RECIP_AT:GAP_AT].astype(F32) * gap).astype(BF16)
        w_ref[at, :] = tile
    f_ref[...] = lax.dot_general(
        w_ref[...], z_ref[...], (((0,), (0,)), ((), ())), preferred_element_type=F32
    )
    by_real = f_ref[HALF:IMAG_AT, :]
    by_imag = pltpu.roll(f_ref[IMAG_AT:SCALE_AT, :], HALF, 1)
    pred = total + by_real + jnp.where(lanes < HALF, -by_imag, by_imag)
    out_ref[...] = jnp.broadcast_to(pred.reshape(1, 2, 8, RECV), out_ref.shape)


def two_parts(x):
    high = x.astype(BF16)
    return high, (x - high.astype(F32)).astype(BF16)


def trace_and_gram(keep_ref, x_ref, rows_ref, target_ref, gram_ref, trace_ref, a_ref, g_ref):
    sources = 8
    columns = []
    for s in range(sources):
        low, high = (x_ref[pl.ds(8 * half + s, NF, stride=16), :] for half in range(2))
        columns.append(jnp.concatenate(halves(low, high), axis=0))
    x = jnp.concatenate(columns, axis=1)
    high, rest = x.astype(BF16), x
    rest = rest - high.astype(F32)
    mid = rest.astype(BF16)
    low = (rest - mid.astype(F32)).astype(BF16)
    stack = jnp.concatenate([high, mid, high, low, high, mid, target_ref[...]], axis=0)
    base = jnp.dot(rows_ref[...], stack, preferred_element_type=F32)
    lag = lax.rem(lax.broadcasted_iota(jnp.int32, (GROWS, RECV), 0), GROUP)
    recv = lax.broadcasted_iota(jnp.int32, (GROWS, RECV), 1)
    ahead = (lag == 0) & (recv < RECV - 1)
    behind = (lag == 2) & (recv > 0)
    same = (lag == 1) | (lag == 3)
    for s in range(sources):
        at = slice(s * RECV, (s + 1) * RECV)
        here = base[:, at]
        shifted = jnp.where(
            same,
            here,
            jnp.where(
                ahead,
                pltpu.roll(here, RECV - 1, 1),
                jnp.where(behind, pltpu.roll(here, 1, 1), 0.0),
            ),
        )
        a_ref[s * GROWS : (s + 1) * GROWS, :] = shifted
    for s in range(sources):
        mine = a_ref[pl.ds(s * GROWS + 1, WROWS + 2 * LEAD, stride=GROUP), :]
        trace_ref[pl.ds(s, WROWS + 2 * LEAD, stride=sources), :] = mine
    high, low = two_parts(jnp.concatenate([a_ref[s * GROWS : (s + 1) * GROWS, :] for s in range(sources)], axis=1))
    dims = (((1,), (1,)), ((), ()))
    g_ref[...] = lax.dot_general(high, high, dims, preferred_element_type=F32) + 2.0 * lax.dot_general(
        high, low, dims, preferred_element_type=F32
    )
    total = jnp.zeros((SIDE, RECV), F32)
    for u in range(WROWS):
        at = GROUP * u
        if at + SIDE <= RECV:
            part = g_ref[at : at + SIDE, :RECV]
            part = pltpu.roll(part, (RECV - at) % RECV, 1)
        elif at >= RECV:
            part = g_ref[at : at + SIDE, RECV:]
            part = pltpu.roll(part, (2 * RECV - at) % RECV, 1)
        else:
            part = pltpu.roll(g_ref[at : at + SIDE, :], 2 * RECV - at, 1)[:, :RECV]
        total = total + part * keep_ref[u : u + 1, :]
    full = jnp.concatenate([total, jnp.zeros((RECV - SIDE, RECV), F32)], axis=0)
    total = 0.5 * (total + full.T[:SIDE])
    lanes = lax.broadcasted_iota(jnp.int32, (8, RECV), 1)
    packed = jnp.zeros((8, RECV), F32)
    for g, at in enumerate(PACK_AT):
        piece = total[8 * g : 8 * g + 8]
        piece = jnp.where((lanes >= 8 * g) & (lanes < SIDE), piece, 0.0)
        packed = packed + pltpu.roll(piece, at - 8 * g, 1)
    gram_ref[...] = jnp.broadcast_to(packed[None], gram_ref.shape)


def solve_and_filter(damping, keep_ref, gram_ref, trace_ref, recorded_ref, out_ref, filters_ref, h_ref):
    packed = jnp.sum(gram_ref[...], axis=0)
    lanes = lax.broadcasted_iota(jnp.int32, (8, RECV), 1)
    pieces = []
    for g, at in enumerate(PACK_AT):
        piece = pltpu.roll(packed, (RECV + 8 * g - at) % RECV, 1)
        pieces.append(jnp.where((lanes >= 8 * g) & (lanes < SIDE), piece, 0.0))
    upper = jnp.concatenate(pieces, axis=0)
    full = jnp.concatenate([upper, jnp.zeros((RECV - SIDE, RECV), F32)], axis=0)
    row = lax.broadcasted_iota(jnp.int32, (SIDE, RECV), 0)
    lane = lax.broadcasted_iota(jnp.int32, (SIDE, RECV), 1)
    system = jnp.where(lane // 8 < row // 8, full.T[:SIDE], upper)
    unknown = lax.rem(row, GROUP) < LAGS_X
    system = system + jnp.where((row == lane) & unknown, damping, 0.0)
    system = system + jnp.where((row == CENTRE_ROW) & (lane == TARGET_COL), damping, 0.0)
    order = [k for k in range(GROUP * LAGS_T) if k % GROUP < LAGS_X]
    for one, two in zip(order[:-1:2], order[1::2]):
        first = jnp.broadcast_to(system[:, one : one + 1], (SIDE, RECV))
        second = jnp.broadcast_to(system[:, two : two + 1], (SIDE, RECV))
        top, bottom = system[one : one + 1, :], system[two : two + 1, :]
        a, b, d = first[one : one + 1], second[one : one + 1], second[two : two + 1]
        scale = 1.0 / (a * d - b * b)
        top, bottom = (d * top - b * bottom) * scale, (a * bottom - b * top) * scale
        rest = system - first * top - second * bottom
        system = jnp.where(row == one, top, jnp.where(row == two, bottom, rest))
    last = order[-1]
    column = jnp.broadcast_to(system[:, last : last + 1], (SIDE, RECV))
    pivot_row = system[last : last + 1, :] / column[last : last + 1]
    system = jnp.where(row == last, pivot_row, system - column * pivot_row)
    chosen = (lane < UNKNOWNS) & (row == GROUP * (LAGS_T - 1 - lane // LAGS_X) + lane % LAGS_X)
    h_ref[...] = jnp.broadcast_to(system[:, TARGET_COL : TARGET_COL + 1], (SIDE, RECV))
    filters_ref[...] = jnp.sum(jnp.where(chosen, h_ref[...], 0.0), axis=0, keepdims=True)[:, :UNKNOWNS]
    recv = lax.broadcasted_iota(jnp.int32, (8, RECV), 1)
    taps = [[jnp.broadcast_to(h_ref[GROUP * p + c : GROUP * p + c + 1, :], (8, RECV)) for c in range(LAGS_X)] for p in range(LAGS_T)]
    for u in range(WROWS):
        sums = [None] * LAGS_X
        for p in range(LAGS_T):
            value = trace_ref[8 * (u + p) : 8 * (u + p) + 8, :]
            for c in range(LAGS_X):
                term = taps[p][c] * value
                sums[c] = term if sums[c] is None else sums[c] + term
        ahead = jnp.where(recv < RECV - 1, pltpu.roll(sums[0], RECV - 1, 1), 0.0)
        behind = jnp.where(recv > 0, pltpu.roll(sums[2], 1, 1), 0.0)
        value = recorded_ref[u].astype(F32) - (sums[1] + ahead + behind)
        out_ref[u] = (value * keep_ref[u : u + 1, :]).astype(BF16)


def call(kernel, out_shape, args, specs, scratch=(), flops=1000000):
    return pl.pallas_call(
        kernel,
        out_shape=out_shape,
        in_specs=specs,
        out_specs=jax.tree.map(lambda _: VMEM, out_shape),
        scratch_shapes=list(scratch),
        compiler_params=pltpu.CompilerParams(vmem_limit_bytes=32 * 2**20),
        cost_estimate=pl.CostEstimate(flops=flops, bytes_accessed=1000000, transcendentals=0),
    )(*args)


def body(data, recip, gap, owner, weights, start_row, end_row, recorded):
    freq_here = lax.axis_index("freq")
    src_count = lax.axis_size("pair") * lax.axis_size("half")
    pairs = src_count // 2
    total_out = weights.shape[3]
    points = data.shape[3]

    recip_rows = jnp.swapaxes(recip[:, 0], 1, 2).reshape(2 * NEAR, RECV)
    depth = points // 2
    parts = pl.pallas_call(
        main_product,
        grid=(points // depth,),
        out_shape=jax.ShapeDtypeStruct((pairs, 2, SLOT_ROWS, RECV), BF16),
        in_specs=[
            pl.BlockSpec((NEAR, RECV), lambda k: (0, 0)),
            pl.BlockSpec((2 * NEAR, RECV), lambda k: (0, 0)),
            pl.BlockSpec((2, 1, RECV, depth), lambda k: (0, 0, 0, k)),
            pl.BlockSpec((2, 1, depth, total_out), lambda k: (0, 0, k, 0)),
        ],
        out_specs=pl.BlockSpec((pairs, 2, SLOT_ROWS, RECV), lambda k: (0, 0, 0, 0)),
        scratch_shapes=[
            pltpu.VMEM((2, RECV, total_out), F32),
            pltpu.VMEM((RECV, RECV), BF16),
            pltpu.VMEM((pairs, NEAR, RECV), F32),
        ],
        cost_estimate=pl.CostEstimate(flops=8 * RECV * points * total_out, bytes_accessed=5000000, transcendentals=0),
    )(gap.T, recip_rows, data, weights)
    parts = parts.reshape(src_count, SLOT_ROWS, RECV)
    parts = lax.all_to_all(parts, ("pair", "half"), 0, 0, tiled=True)
    copies = call(
        sum_and_fill,
        jax.ShapeDtypeStruct((NF, 2, 8, RECV), F32),
        (jnp.broadcast_to(owner[None], (8, src_count)), parts),
        [VMEM, VMEM],
        [
            pltpu.VMEM((NEAR * src_count, RECV), BF16),
            pltpu.VMEM((NEAR * src_count, RECV), BF16),
            pltpu.VMEM((RECV, RECV), F32),
        ],
    )
    copies = copies.reshape(NF * 2, 8, RECV)
    spread = lax.all_to_all(copies, ("freq", "half"), 0, 0, tiled=True).reshape(NF * 16, RECV)

    begin = freq_here * T_DEV - HALO
    first, last = start_row[0] - begin, end_row[0] - begin
    row = lax.broadcasted_iota(jnp.int32, (WROWS, RECV), 0)
    keep_rows = ((row >= first) & (row < last)).astype(F32)
    row = jnp.arange(GROWS, dtype=jnp.int32) // GROUP - LEAD
    keep = (row >= first) & (row < last)
    rows = lax.dynamic_index_in_dim(jnp.asarray(phase_rows()), freq_here, 0, keepdims=False)
    rows = jnp.where(keep[:, None], rows, jnp.zeros_like(rows))
    target = jnp.pad(recorded.reshape(WROWS, -1), ((0, 16), (0, 0)))
    trace_rows = 8 * (WROWS + 2 * LEAD)
    gram, trace = call(
        trace_and_gram,
        (jax.ShapeDtypeStruct((src_count, 8, RECV), F32), jax.ShapeDtypeStruct((trace_rows, RECV), F32)),
        (keep_rows, spread, rows, target),
        [VMEM] * 4,
        [pltpu.VMEM((8 * GROWS, RECV), F32), pltpu.VMEM((GROWS, GROWS), F32)],
    )
    gram = lax.all_to_all(gram, ("pair", "half"), 0, 0, tiled=True)
    damping = float(WROWS * total_out * RECV)
    primaries, filters = call(
        functools.partial(solve_and_filter, damping),
        (jax.ShapeDtypeStruct(recorded.shape, BF16), jax.ShapeDtypeStruct((1, UNKNOWNS), F32)),
        (keep_rows, gram, trace, recorded),
        [VMEM] * 4,
        [pltpu.VMEM((SIDE, RECV), F32)],
    )
    return primaries, filters


def solution(mesh):
    freq, src = mesh.devices.shape
    mesh = Mesh(mesh.devices.reshape(freq, src // 2, 2), ("freq", "pair", "half"))
    src = ("pair", "half")
    placed = (
        P(None, "freq", None, src),
        P(None, "freq", None, src),
        P(None, src),
        P(),
        P(None, "freq", src, None),
        P("freq"),
        P("freq"),
        P("freq", src, None),
    )
    return jax.shard_map(
        body,
        mesh=mesh,
        in_specs=placed,
        out_specs=(P("freq", src, None), P("freq", None)),
        check_vma=False,
    )
```

```python
import functools
import math

import jax
import jax.numpy as jnp
import ml_dtypes
import numpy as np
from jax import lax
from jax.experimental import pallas as pl
from jax.experimental.pallas import tpu as pltpu
from jax.sharding import Mesh, PartitionSpec as P

RECV = 128
NFFT = 512
F_LOW = 40
NEAR = 16
HALO = 8
LAGS_T = 9
LAGS_X = 3
LEAD = LAGS_T // 2
T_DEV = 32
WROWS = T_DEV + 2 * HALO
NF = 16
GROUP = 4
GROWS = 256
SIDE = 40
UNKNOWNS = LAGS_T * LAGS_X
TARGET_COL = GROUP * LEAD + 3
CENTRE_ROW = GROUP * LEAD + 1
PACK_AT = (0, 40, 72, 96, 112)
RECIP_AT, GAP_AT, SLOT_ROWS = 16, 32, 48
HALF = RECV // 2
IMAG_AT, SCALE_AT = HALF + 16, HALF + 32
SPAN = 166.0
VMEM = pl.BlockSpec(memory_space=pltpu.VMEM)
ANY = pl.BlockSpec(memory_space=pl.ANY)
F32 = jnp.float32
BF16 = jnp.bfloat16


def split3(x):
    high = x.astype(ml_dtypes.bfloat16)
    rest = x - high.astype(np.float32)
    mid = rest.astype(ml_dtypes.bfloat16)
    low = (rest - mid.astype(np.float32)).astype(ml_dtypes.bfloat16)
    return high, mid, low


@functools.cache
def phase_rows():
    table = np.zeros((NF, GROWS, 256), ml_dtypes.bfloat16)
    freqs = np.arange(NF)
    scale = 1.0 / math.sqrt(NF)
    for window in range(NF):
        for row in range(WROWS):
            time = window * T_DEV - HALO + row
            if not 0 <= time < NFFT:
                continue
            turns = (F_LOW + freqs) * time % NFFT
            angle = turns * (2.0 * math.pi / NFFT)
            phase = np.stack([np.cos(angle), -np.sin(angle)], axis=0).reshape(-1) * scale
            high, mid, low = split3(phase.astype(np.float32))
            at = GROUP * (row + LEAD)
            table[window, at : at + 3, :192] = np.concatenate([high, high, mid, high, low, mid])
            table[window, at + 3, 192 + row] = 1
    return table


def halves(first, second):
    lanes = lax.broadcasted_iota(jnp.int32, first.shape, 1)
    low = jnp.where(lanes < HALF, first, pltpu.roll(second, HALF, 1))
    return low, jnp.where(lanes < HALF, pltpu.roll(first, HALF, 1), second)


def encode(value, scale):
    size = jnp.exp(jnp.abs(value) * (SPAN / scale) - SPAN / 2)
    return jnp.where(value < 0, -size, size)


def decode(code, scale):
    size = (jnp.log(jnp.abs(code)) + SPAN / 2) * (scale * (1.0 / SPAN))
    return jnp.where(code < 0, -size, size)


def main_product(gap_ref, recip_ref, data_ref, weights_ref, out_ref, acc_ref, mask_ref, near_ref):
    step = pl.program_id(0)
    depth = data_ref.shape[3]
    pairs = out_ref.shape[0]

    @pl.when(step == 0)
    def _():
        acc_ref[...] = jnp.zeros_like(acc_ref)
        gap = jnp.where(gap_ref[...] == 1, 1.0, 0.0)
        full = jnp.concatenate([gap, jnp.zeros((RECV - NEAR, RECV), F32)], axis=0)
        mask_ref[...] = (1.0 - full.T).astype(BF16)
        recip = recip_ref[...].astype(F32)
        recip = halves(recip[:NEAR], recip[NEAR:])
        lanes = lax.broadcasted_iota(jnp.int32, (NEAR, RECV), 1)
        for half in range(2):
            out_ref[:, half, RECIP_AT:GAP_AT] = jnp.broadcast_to(
                recip[half].astype(BF16)[None], (pairs, NEAR, RECV)
            )
        for pair in range(pairs):
            at, off = RECV * (pair // 8), 16 * (pair % 8)
            real = weights_ref[0, 0, :NEAR, at : at + RECV].astype(F32)
            imag = weights_ref[1, 0, :NEAR, at : at + RECV].astype(F32)
            real = pltpu.roll(real, (HALF - off) % RECV, 1)
            imag = pltpu.roll(imag, (IMAG_AT - off) % RECV, 1)
            near_ref[pair] = jnp.where(lanes < IMAG_AT, real, imag)

    @pl.when(step == 1)
    def _():
        mask_ref[...] = jnp.ones_like(mask_ref)

    panel = data_ref[...].reshape(2 * RECV, depth)
    mask = mask_ref[...]
    near = panel[:, :RECV] * jnp.concatenate([mask, mask], axis=0)
    panel = jnp.concatenate([near, panel[:, RECV:]], axis=1)
    both = jnp.concatenate([weights_ref[0, 0], weights_ref[1, 0]], axis=1)
    product = jnp.dot(panel, both, preferred_element_type=F32)
    width = product.shape[1] // 2
    acc_ref[0] += product[:RECV, :width] - product[RECV:, width:]
    acc_ref[1] += product[:RECV, width:] + product[RECV:, :width]

    @pl.when(step == pl.num_programs(0) - 1)
    def _():
        gap = jnp.where(gap_ref[...] == 1, 1.0, 0.0)
        gaps = gap, pltpu.roll(gap, HALF, 1)
        lanes = lax.broadcasted_iota(jnp.int32, (pairs, NEAR, RECV), 2)
        for half, pred in enumerate(halves(acc_ref[0].T, acc_ref[1].T)):
            pred = pred.reshape(pairs, 16, RECV)
            scale = jnp.max(jnp.abs(pred), axis=(1, 2), keepdims=True) * 1.01 + 1e-30
            scale = scale.astype(BF16).astype(F32)
            out_ref[:, half, :RECIP_AT] = encode(pred, scale).astype(BF16)
            tile = jnp.where(lanes < SCALE_AT, near_ref[...], jnp.broadcast_to(scale, lanes.shape))
            tile = jnp.where(lanes < HALF, jnp.broadcast_to(gaps[half][None], lanes.shape), tile)
            out_ref[:, half, GAP_AT:] = tile.astype(BF16)


def sum_and_fill(owner_ref, part_ref, keep_ref, rows_ref, target_ref, out_ref, z_ref, w_ref, f_ref):
    del keep_ref, rows_ref, target_ref
    slots = part_ref.shape[0]
    total = jnp.zeros((16, RECV), F32)
    for j in range(slots):
        scale = part_ref[j, GAP_AT:].astype(F32)[:, SCALE_AT : SCALE_AT + 1]
        code = part_ref[j, :RECIP_AT].astype(F32)
        total = total + decode(code, jnp.broadcast_to(scale, code.shape))
    lanes = lax.broadcasted_iota(jnp.int32, (NEAR, RECV), 1)
    for j in range(slots):
        tile = part_ref[owner_ref[0, j], GAP_AT:]
        gap = tile.astype(F32)
        gap = jnp.where(lanes < HALF, gap, pltpu.roll(gap, HALF, 1))
        at = slice(NEAR * j, NEAR * j + NEAR)
        z_ref[at, :] = (part_ref[j, RECIP_AT:GAP_AT].astype(F32) * gap).astype(BF16)
        w_ref[at, :] = tile
    f_ref[...] = lax.dot_general(
        w_ref[...], z_ref[...], (((0,), (0,)), ((), ())), preferred_element_type=F32
    )
    by_real = f_ref[HALF:IMAG_AT, :]
    by_imag = pltpu.roll(f_ref[IMAG_AT:SCALE_AT, :], HALF, 1)
    pred = total + by_real + jnp.where(lanes < HALF, -by_imag, by_imag)
    out_ref[...] = jnp.broadcast_to(pred.reshape(1, 2, 8, RECV), out_ref.shape)


def two_parts(x):
    high = x.astype(BF16)
    return high, (x - high.astype(F32)).astype(BF16)


def trace_and_gram(keep_ref, x_ref, rows_ref, target_ref, gram_ref, trace_ref, a_ref, g_ref):
    sources = 8
    columns = []
    for s in range(sources):
        low, high = (x_ref[pl.ds(8 * half + s, NF, stride=16), :] for half in range(2))
        columns.append(jnp.concatenate(halves(low, high), axis=0))
    x = jnp.concatenate(columns, axis=1)
    high, rest = x.astype(BF16), x
    rest = rest - high.astype(F32)
    mid = rest.astype(BF16)
    low = (rest - mid.astype(F32)).astype(BF16)
    stack = jnp.concatenate([high, mid, high, low, high, mid, target_ref[...]], axis=0)
    base = jnp.dot(rows_ref[...], stack, preferred_element_type=F32)
    lag = lax.rem(lax.broadcasted_iota(jnp.int32, (GROWS, RECV), 0), GROUP)
    recv = lax.broadcasted_iota(jnp.int32, (GROWS, RECV), 1)
    ahead = (lag == 0) & (recv < RECV - 1)
    behind = (lag == 2) & (recv > 0)
    same = (lag == 1) | (lag == 3)
    for s in range(sources):
        at = slice(s * RECV, (s + 1) * RECV)
        here = base[:, at]
        shifted = jnp.where(
            same,
            here,
            jnp.where(
                ahead,
                pltpu.roll(here, RECV - 1, 1),
                jnp.where(behind, pltpu.roll(here, 1, 1), 0.0),
            ),
        )
        a_ref[s * GROWS : (s + 1) * GROWS, :] = shifted
    for s in range(sources):
        mine = a_ref[pl.ds(s * GROWS + 1, WROWS + 2 * LEAD, stride=GROUP), :]
        trace_ref[pl.ds(s, WROWS + 2 * LEAD, stride=sources), :] = mine
    high, low = two_parts(jnp.concatenate([a_ref[s * GROWS : (s + 1) * GROWS, :] for s in range(sources)], axis=1))
    dims = (((1,), (1,)), ((), ()))
    g_ref[...] = lax.dot_general(high, high, dims, preferred_element_type=F32) + 2.0 * lax.dot_general(
        high, low, dims, preferred_element_type=F32
    )
    total = jnp.zeros((SIDE, RECV), F32)
    for u in range(WROWS):
        at = GROUP * u
        if at + SIDE <= RECV:
            part = g_ref[at : at + SIDE, :RECV]
            part = pltpu.roll(part, (RECV - at) % RECV, 1)
        elif at >= RECV:
            part = g_ref[at : at + SIDE, RECV:]
            part = pltpu.roll(part, (2 * RECV - at) % RECV, 1)
        else:
            part = pltpu.roll(g_ref[at : at + SIDE, :], 2 * RECV - at, 1)[:, :RECV]
        total = total + part * keep_ref[u : u + 1, :]
    full = jnp.concatenate([total, jnp.zeros((RECV - SIDE, RECV), F32)], axis=0)
    total = 0.5 * (total + full.T[:SIDE])
    lanes = lax.broadcasted_iota(jnp.int32, (8, RECV), 1)
    packed = jnp.zeros((8, RECV), F32)
    for g, at in enumerate(PACK_AT):
        piece = total[8 * g : 8 * g + 8]
        piece = jnp.where((lanes >= 8 * g) & (lanes < SIDE), piece, 0.0)
        packed = packed + pltpu.roll(piece, at - 8 * g, 1)
    gram_ref[...] = jnp.broadcast_to(packed[None], gram_ref.shape)


def solve_and_filter(damping, keep_ref, gram_ref, trace_ref, recorded_ref, out_ref, filters_ref, h_ref):
    packed = jnp.sum(gram_ref[...], axis=0)
    lanes = lax.broadcasted_iota(jnp.int32, (8, RECV), 1)
    pieces = []
    for g, at in enumerate(PACK_AT):
        piece = pltpu.roll(packed, (RECV + 8 * g - at) % RECV, 1)
        pieces.append(jnp.where((lanes >= 8 * g) & (lanes < SIDE), piece, 0.0))
    upper = jnp.concatenate(pieces, axis=0)
    full = jnp.concatenate([upper, jnp.zeros((RECV - SIDE, RECV), F32)], axis=0)
    row = lax.broadcasted_iota(jnp.int32, (SIDE, RECV), 0)
    lane = lax.broadcasted_iota(jnp.int32, (SIDE, RECV), 1)
    system = jnp.where(lane // 8 < row // 8, full.T[:SIDE], upper)
    unknown = lax.rem(row, GROUP) < LAGS_X
    system = system + jnp.where((row == lane) & unknown, damping, 0.0)
    system = system + jnp.where((row == CENTRE_ROW) & (lane == TARGET_COL), damping, 0.0)
    order = [k for k in range(GROUP * LAGS_T) if k % GROUP < LAGS_X]
    for one, two in zip(order[:-1:2], order[1::2]):
        first = jnp.broadcast_to(system[:, one : one + 1], (SIDE, RECV))
        second = jnp.broadcast_to(system[:, two : two + 1], (SIDE, RECV))
        top, bottom = system[one : one + 1, :], system[two : two + 1, :]
        a, b, d = first[one : one + 1], second[one : one + 1], second[two : two + 1]
        scale = 1.0 / (a * d - b * b)
        top, bottom = (d * top - b * bottom) * scale, (a * bottom - b * top) * scale
        rest = system - first * top - second * bottom
        system = jnp.where(row == one, top, jnp.where(row == two, bottom, rest))
    last = order[-1]
    column = jnp.broadcast_to(system[:, last : last + 1], (SIDE, RECV))
    pivot_row = system[last : last + 1, :] / column[last : last + 1]
    system = jnp.where(row == last, pivot_row, system - column * pivot_row)
    chosen = (lane < UNKNOWNS) & (row == GROUP * (LAGS_T - 1 - lane // LAGS_X) + lane % LAGS_X)
    h_ref[...] = jnp.broadcast_to(system[:, TARGET_COL : TARGET_COL + 1], (SIDE, RECV))
    filters_ref[...] = jnp.sum(jnp.where(chosen, h_ref[...], 0.0), axis=0, keepdims=True)[:, :UNKNOWNS]
    recv = lax.broadcasted_iota(jnp.int32, (8, RECV), 1)
    taps = [[jnp.broadcast_to(h_ref[GROUP * p + c : GROUP * p + c + 1, :], (8, RECV)) for c in range(LAGS_X)] for p in range(LAGS_T)]
    for u in range(WROWS):
        sums = [None] * LAGS_X
        for p in range(LAGS_T):
            value = trace_ref[8 * (u + p) : 8 * (u + p) + 8, :]
            for c in range(LAGS_X):
                term = taps[p][c] * value
                sums[c] = term if sums[c] is None else sums[c] + term
        ahead = jnp.where(recv < RECV - 1, pltpu.roll(sums[0], RECV - 1, 1), 0.0)
        behind = jnp.where(recv > 0, pltpu.roll(sums[2], 1, 1), 0.0)
        value = recorded_ref[u].astype(F32) - (sums[1] + ahead + behind)
        out_ref[u] = (value * keep_ref[u : u + 1, :]).astype(BF16)


def call(kernel, out_shape, args, specs, scratch=(), flops=1000000):
    return pl.pallas_call(
        kernel,
        out_shape=out_shape,
        in_specs=specs,
        out_specs=jax.tree.map(lambda _: VMEM, out_shape),
        scratch_shapes=list(scratch),
        compiler_params=pltpu.CompilerParams(vmem_limit_bytes=32 * 2**20),
        cost_estimate=pl.CostEstimate(flops=flops, bytes_accessed=1000000, transcendentals=0),
    )(*args)


def body(data, recip, gap, owner, weights, start_row, end_row, recorded):
    freq_here = lax.axis_index("freq")
    src_count = lax.axis_size("pair") * lax.axis_size("half")
    pairs = src_count // 2
    total_out = weights.shape[3]
    points = data.shape[3]

    recip_rows = jnp.swapaxes(recip[:, 0], 1, 2).reshape(2 * NEAR, RECV)
    depth = points // 2
    parts = pl.pallas_call(
        main_product,
        grid=(points // depth,),
        out_shape=jax.ShapeDtypeStruct((pairs, 2, SLOT_ROWS, RECV), BF16),
        in_specs=[
            pl.BlockSpec((NEAR, RECV), lambda k: (0, 0)),
            pl.BlockSpec((2 * NEAR, RECV), lambda k: (0, 0)),
            pl.BlockSpec((2, 1, RECV, depth), lambda k: (0, 0, 0, k)),
            pl.BlockSpec((2, 1, depth, total_out), lambda k: (0, 0, k, 0)),
        ],
        out_specs=pl.BlockSpec((pairs, 2, SLOT_ROWS, RECV), lambda k: (0, 0, 0, 0)),
        scratch_shapes=[
            pltpu.VMEM((2, RECV, total_out), F32),
            pltpu.VMEM((RECV, RECV), BF16),
            pltpu.VMEM((pairs, NEAR, RECV), F32),
        ],
        cost_estimate=pl.CostEstimate(flops=8 * RECV * points * total_out, bytes_accessed=5000000, transcendentals=0),
    )(gap.T, recip_rows, data, weights)
    parts = parts.reshape(src_count, SLOT_ROWS, RECV)
    parts = lax.all_to_all(parts, ("pair", "half"), 0, 0, tiled=True)
    begin = freq_here * T_DEV - HALO
    first, last = start_row[0] - begin, end_row[0] - begin
    row = lax.broadcasted_iota(jnp.int32, (WROWS, RECV), 0)
    keep_rows = ((row >= first) & (row < last)).astype(F32)
    row = jnp.arange(GROWS, dtype=jnp.int32) // GROUP - LEAD
    keep = (row >= first) & (row < last)
    rows = lax.dynamic_index_in_dim(jnp.asarray(phase_rows()), freq_here, 0, keepdims=False)
    rows = jnp.where(keep[:, None], rows, jnp.zeros_like(rows))
    target = jnp.pad(recorded.reshape(WROWS, -1), ((0, 16), (0, 0)))

    copies = call(
        sum_and_fill,
        jax.ShapeDtypeStruct((NF, 2, 8, RECV), F32),
        (jnp.broadcast_to(owner[None], (8, src_count)), parts, keep_rows, rows, target),
        [VMEM, VMEM, ANY, ANY, ANY],
        [
            pltpu.VMEM((NEAR * src_count, RECV), BF16),
            pltpu.VMEM((NEAR * src_count, RECV), BF16),
            pltpu.VMEM((RECV, RECV), F32),
        ],
    )
    copies = copies.reshape(NF * 2, 8, RECV)
    spread = lax.all_to_all(copies, ("freq", "half"), 0, 0, tiled=True).reshape(NF * 16, RECV)

    trace_rows = 8 * (WROWS + 2 * LEAD)
    gram, trace = call(
        trace_and_gram,
        (jax.ShapeDtypeStruct((src_count, 8, RECV), F32), jax.ShapeDtypeStruct((trace_rows, RECV), F32)),
        (keep_rows, spread, rows, target),
        [VMEM] * 4,
        [pltpu.VMEM((8 * GROWS, RECV), F32), pltpu.VMEM((GROWS, GROWS), F32)],
    )
    gram = lax.all_to_all(gram, ("pair", "half"), 0, 0, tiled=True)
    damping = float(WROWS * total_out * RECV)
    primaries, filters = call(
        functools.partial(solve_and_filter, damping),
        (jax.ShapeDtypeStruct(recorded.shape, BF16), jax.ShapeDtypeStruct((1, UNKNOWNS), F32)),
        (keep_rows, gram, trace, recorded),
        [VMEM] * 4,
        [pltpu.VMEM((SIDE, RECV), F32)],
    )
    return primaries, filters


def solution(mesh):
    freq, src = mesh.devices.shape
    mesh = Mesh(mesh.devices.reshape(freq, src // 2, 2), ("freq", "pair", "half"))
    src = ("pair", "half")
    placed = (
        P(None, "freq", None, src),
        P(None, "freq", None, src),
        P(None, src),
        P(),
        P(None, "freq", src, None),
        P("freq"),
        P("freq"),
        P("freq", src, None),
    )
    return jax.shard_map(
        body,
        mesh=mesh,
        in_specs=placed,
        out_specs=(P("freq", src, None), P("freq", None)),
        check_vma=False,
    )
```

```python
import functools
import math

import jax
import jax.numpy as jnp
import ml_dtypes
import numpy as np
from jax import lax
from jax.experimental import pallas as pl
from jax.experimental.pallas import tpu as pltpu
from jax.sharding import Mesh, PartitionSpec as P

RECV = 128
NFFT = 512
F_LOW = 40
NEAR = 16
HALO = 8
LAGS_T = 9
LAGS_X = 3
LEAD = LAGS_T // 2
T_DEV = 32
WROWS = T_DEV + 2 * HALO
NF = 16
GROUP = 4
GROWS = 256
SIDE = 40
UNKNOWNS = LAGS_T * LAGS_X
TARGET_COL = GROUP * LEAD + 3
CENTRE_ROW = GROUP * LEAD + 1
PACK_AT = (0, 40, 72, 96, 112)
RECIP_AT, GAP_AT, SLOT_ROWS = 16, 32, 48
HALF = RECV // 2
IMAG_AT, SCALE_AT = HALF + 16, HALF + 32
SPAN = 166.0
VMEM = pl.BlockSpec(memory_space=pltpu.VMEM)
ANY = pl.BlockSpec(memory_space=pl.ANY)
F32 = jnp.float32
BF16 = jnp.bfloat16


def split3(x):
    high = x.astype(ml_dtypes.bfloat16)
    rest = x - high.astype(np.float32)
    mid = rest.astype(ml_dtypes.bfloat16)
    low = (rest - mid.astype(np.float32)).astype(ml_dtypes.bfloat16)
    return high, mid, low


@functools.cache
def phase_rows():
    table = np.zeros((NF, GROWS, 256), ml_dtypes.bfloat16)
    freqs = np.arange(NF)
    scale = 1.0 / math.sqrt(NF)
    for window in range(NF):
        for row in range(WROWS):
            time = window * T_DEV - HALO + row
            if not 0 <= time < NFFT:
                continue
            turns = (F_LOW + freqs) * time % NFFT
            angle = turns * (2.0 * math.pi / NFFT)
            phase = np.stack([np.cos(angle), -np.sin(angle)], axis=0).reshape(-1) * scale
            high, mid, low = split3(phase.astype(np.float32))
            at = GROUP * (row + LEAD)
            table[window, at : at + 3, :192] = np.concatenate([high, high, mid, high, low, mid])
            table[window, at + 3, 192 + row] = 1
    return table


def halves(first, second):
    lanes = lax.broadcasted_iota(jnp.int32, first.shape, 1)
    low = jnp.where(lanes < HALF, first, pltpu.roll(second, HALF, 1))
    return low, jnp.where(lanes < HALF, pltpu.roll(first, HALF, 1), second)


def encode(value, scale):
    size = jnp.exp(jnp.abs(value) * (SPAN / scale) - SPAN / 2)
    return jnp.where(value < 0, -size, size)


def decode(code, scale):
    size = (jnp.log(jnp.abs(code)) + SPAN / 2) * (scale * (1.0 / SPAN))
    return jnp.where(code < 0, -size, size)


def main_product(gap_ref, recip_ref, data_ref, weights_ref, out_ref, acc_ref, mask_ref, near_ref):
    step = pl.program_id(0)
    depth = data_ref.shape[3]
    pairs = out_ref.shape[0]

    @pl.when(step == 0)
    def _():
        acc_ref[...] = jnp.zeros_like(acc_ref)
        gap = jnp.where(gap_ref[...] == 1, 1.0, 0.0)
        full = jnp.concatenate([gap, jnp.zeros((RECV - NEAR, RECV), F32)], axis=0)
        mask_ref[...] = (1.0 - full.T).astype(BF16)
        recip = recip_ref[...].astype(F32)
        recip = halves(recip[:NEAR], recip[NEAR:])
        lanes = lax.broadcasted_iota(jnp.int32, (NEAR, RECV), 1)
        for half in range(2):
            out_ref[:, half, RECIP_AT:GAP_AT] = jnp.broadcast_to(
                recip[half].astype(BF16)[None], (pairs, NEAR, RECV)
            )
        for pair in range(pairs):
            at, off = RECV * (pair // 8), 16 * (pair % 8)
            real = weights_ref[0, 0, :NEAR, at : at + RECV].astype(F32)
            imag = weights_ref[1, 0, :NEAR, at : at + RECV].astype(F32)
            real = pltpu.roll(real, (HALF - off) % RECV, 1)
            imag = pltpu.roll(imag, (IMAG_AT - off) % RECV, 1)
            near_ref[pair] = jnp.where(lanes < IMAG_AT, real, imag)

    @pl.when(step == 1)
    def _():
        mask_ref[...] = jnp.ones_like(mask_ref)

    panel = data_ref[...].reshape(2 * RECV, depth)
    mask = mask_ref[...]
    near = panel[:, :RECV] * jnp.concatenate([mask, mask], axis=0)
    panel = jnp.concatenate([near, panel[:, RECV:]], axis=1)
    both = jnp.concatenate([weights_ref[0, 0], weights_ref[1, 0]], axis=1)
    product = jnp.dot(panel, both, preferred_element_type=F32)
    width = product.shape[1] // 2
    acc_ref[0] += product[:RECV, :width] - product[RECV:, width:]
    acc_ref[1] += product[:RECV, width:] + product[RECV:, :width]

    @pl.when(step == pl.num_programs(0) - 1)
    def _():
        gap = jnp.where(gap_ref[...] == 1, 1.0, 0.0)
        gaps = gap, pltpu.roll(gap, HALF, 1)
        lanes = lax.broadcasted_iota(jnp.int32, (pairs, NEAR, RECV), 2)
        for half, pred in enumerate(halves(acc_ref[0].T, acc_ref[1].T)):
            pred = pred.reshape(pairs, 16, RECV)
            scale = jnp.max(jnp.abs(pred), axis=(1, 2), keepdims=True) * 1.01 + 1e-30
            scale = scale.astype(BF16).astype(F32)
            out_ref[:, half, :RECIP_AT] = encode(pred, scale).astype(BF16)
            tile = jnp.where(lanes < SCALE_AT, near_ref[...], jnp.broadcast_to(scale, lanes.shape))
            tile = jnp.where(lanes < HALF, jnp.broadcast_to(gaps[half][None], lanes.shape), tile)
            out_ref[:, half, GAP_AT:] = tile.astype(BF16)


def sum_and_fill(owner_ref, part_ref, keep_ref, rows_ref, target_ref, out_ref, z_ref, w_ref, f_ref):
    del keep_ref, rows_ref, target_ref
    slots = part_ref.shape[0]
    total = jnp.zeros((16, RECV), F32)
    for j in range(slots):
        scale = part_ref[j, GAP_AT:].astype(F32)[:, SCALE_AT : SCALE_AT + 1]
        code = part_ref[j, :RECIP_AT].astype(F32)
        total = total + decode(code, jnp.broadcast_to(scale, code.shape))
    lanes = lax.broadcasted_iota(jnp.int32, (NEAR, RECV), 1)
    for j in range(slots):
        tile = part_ref[owner_ref[0, j], GAP_AT:]
        gap = tile.astype(F32)
        gap = jnp.where(lanes < HALF, gap, pltpu.roll(gap, HALF, 1))
        at = slice(NEAR * j, NEAR * j + NEAR)
        z_ref[at, :] = (part_ref[j, RECIP_AT:GAP_AT].astype(F32) * gap).astype(BF16)
        w_ref[at, :] = tile
    f_ref[...] = lax.dot_general(
        w_ref[...], z_ref[...], (((0,), (0,)), ((), ())), preferred_element_type=F32
    )
    by_real = f_ref[HALF:IMAG_AT, :]
    by_imag = pltpu.roll(f_ref[IMAG_AT:SCALE_AT, :], HALF, 1)
    pred = total + by_real + jnp.where(lanes < HALF, -by_imag, by_imag)
    out_ref[...] = jnp.broadcast_to(pred.reshape(1, 2, 8, RECV), out_ref.shape)


def two_parts(x):
    high = x.astype(BF16)
    return high, (x - high.astype(F32)).astype(BF16)


def trace_and_gram(keep_ref, x_ref, rows_ref, target_ref, gram_ref, trace_ref, a_ref, g_ref):
    sources = 8
    columns = []
    for s in range(sources):
        low, high = (x_ref[pl.ds(8 * half + s, NF, stride=16), :] for half in range(2))
        columns.append(jnp.concatenate(halves(low, high), axis=0))
    x = jnp.concatenate(columns, axis=1)
    high, rest = x.astype(BF16), x
    rest = rest - high.astype(F32)
    mid = rest.astype(BF16)
    low = (rest - mid.astype(F32)).astype(BF16)
    stack = jnp.concatenate([high, mid, high, low, high, mid, target_ref[...]], axis=0)
    base = jnp.dot(rows_ref[...], stack, preferred_element_type=F32)
    times = GROWS // GROUP
    recv = lax.broadcasted_iota(jnp.int32, (times, RECV), 1)
    for s in range(sources):
        a_ref[s * GROWS : (s + 1) * GROWS, :] = base[:, s * RECV : (s + 1) * RECV]
    for s in range(sources):
        ahead = pl.ds(s * GROWS, times, stride=GROUP)
        a_ref[ahead, :] = jnp.where(recv < RECV - 1, pltpu.roll(a_ref[ahead, :], RECV - 1, 1), 0.0)
        behind = pl.ds(s * GROWS + 2, times, stride=GROUP)
        a_ref[behind, :] = jnp.where(recv > 0, pltpu.roll(a_ref[behind, :], 1, 1), 0.0)
    for s in range(sources):
        mine = a_ref[pl.ds(s * GROWS + 1, WROWS + 2 * LEAD, stride=GROUP), :]
        trace_ref[pl.ds(s, WROWS + 2 * LEAD, stride=sources), :] = mine
    high, low = two_parts(jnp.concatenate([a_ref[s * GROWS : (s + 1) * GROWS, :] for s in range(sources)], axis=1))
    dims = (((1,), (1,)), ((), ()))
    g_ref[...] = lax.dot_general(high, high, dims, preferred_element_type=F32) + 2.0 * lax.dot_general(
        high, low, dims, preferred_element_type=F32
    )
    total = jnp.zeros((SIDE, RECV), F32)
    for u in range(WROWS):
        at = GROUP * u
        if at + SIDE <= RECV:
            part = g_ref[at : at + SIDE, :RECV]
            part = pltpu.roll(part, (RECV - at) % RECV, 1)
        elif at >= RECV:
            part = g_ref[at : at + SIDE, RECV:]
            part = pltpu.roll(part, (2 * RECV - at) % RECV, 1)
        else:
            part = pltpu.roll(g_ref[at : at + SIDE, :], 2 * RECV - at, 1)[:, :RECV]
        total = total + part * keep_ref[u : u + 1, :]
    full = jnp.concatenate([total, jnp.zeros((RECV - SIDE, RECV), F32)], axis=0)
    total = 0.5 * (total + full.T[:SIDE])
    lanes = lax.broadcasted_iota(jnp.int32, (8, RECV), 1)
    packed = jnp.zeros((8, RECV), F32)
    for g, at in enumerate(PACK_AT):
        piece = total[8 * g : 8 * g + 8]
        piece = jnp.where((lanes >= 8 * g) & (lanes < SIDE), piece, 0.0)
        packed = packed + pltpu.roll(piece, at - 8 * g, 1)
    gram_ref[...] = jnp.broadcast_to(packed[None], gram_ref.shape)


def solve_and_filter(damping, keep_ref, gram_ref, trace_ref, recorded_ref, out_ref, filters_ref, h_ref):
    packed = jnp.sum(gram_ref[...], axis=0)
    lanes = lax.broadcasted_iota(jnp.int32, (8, RECV), 1)
    pieces = []
    for g, at in enumerate(PACK_AT):
        piece = pltpu.roll(packed, (RECV + 8 * g - at) % RECV, 1)
        pieces.append(jnp.where((lanes >= 8 * g) & (lanes < SIDE), piece, 0.0))
    upper = jnp.concatenate(pieces, axis=0)
    full = jnp.concatenate([upper, jnp.zeros((RECV - SIDE, RECV), F32)], axis=0)
    row = lax.broadcasted_iota(jnp.int32, (SIDE, RECV), 0)
    lane = lax.broadcasted_iota(jnp.int32, (SIDE, RECV), 1)
    system = jnp.where(lane // 8 < row // 8, full.T[:SIDE], upper)
    unknown = lax.rem(row, GROUP) < LAGS_X
    system = system + jnp.where((row == lane) & unknown, damping, 0.0)
    system = system + jnp.where((row == CENTRE_ROW) & (lane == TARGET_COL), damping, 0.0)
    order = [k for k in range(GROUP * LAGS_T) if k % GROUP < LAGS_X]
    for one, two in zip(order[:-1:2], order[1::2]):
        first = jnp.broadcast_to(system[:, one : one + 1], (SIDE, RECV))
        second = jnp.broadcast_to(system[:, two : two + 1], (SIDE, RECV))
        top, bottom = system[one : one + 1, :], system[two : two + 1, :]
        a, b, d = first[one : one + 1], second[one : one + 1], second[two : two + 1]
        scale = 1.0 / (a * d - b * b)
        top, bottom = (d * top - b * bottom) * scale, (a * bottom - b * top) * scale
        rest = system - first * top - second * bottom
        system = jnp.where(row == one, top, jnp.where(row == two, bottom, rest))
    last = order[-1]
    column = jnp.broadcast_to(system[:, last : last + 1], (SIDE, RECV))
    pivot_row = system[last : last + 1, :] / column[last : last + 1]
    system = jnp.where(row == last, pivot_row, system - column * pivot_row)
    chosen = (lane < UNKNOWNS) & (row == GROUP * (LAGS_T - 1 - lane // LAGS_X) + lane % LAGS_X)
    h_ref[...] = jnp.broadcast_to(system[:, TARGET_COL : TARGET_COL + 1], (SIDE, RECV))
    filters_ref[...] = jnp.sum(jnp.where(chosen, h_ref[...], 0.0), axis=0, keepdims=True)[:, :UNKNOWNS]
    recv = lax.broadcasted_iota(jnp.int32, (8, RECV), 1)
    taps = [[jnp.broadcast_to(h_ref[GROUP * p + c : GROUP * p + c + 1, :], (8, RECV)) for c in range(LAGS_X)] for p in range(LAGS_T)]
    for u in range(WROWS):
        sums = [None] * LAGS_X
        for p in range(LAGS_T):
            value = trace_ref[8 * (u + p) : 8 * (u + p) + 8, :]
            for c in range(LAGS_X):
                term = taps[p][c] * value
                sums[c] = term if sums[c] is None else sums[c] + term
        ahead = jnp.where(recv < RECV - 1, pltpu.roll(sums[0], RECV - 1, 1), 0.0)
        behind = jnp.where(recv > 0, pltpu.roll(sums[2], 1, 1), 0.0)
        value = recorded_ref[u].astype(F32) - (sums[1] + ahead + behind)
        out_ref[u] = (value * keep_ref[u : u + 1, :]).astype(BF16)


def call(kernel, out_shape, args, specs, scratch=(), flops=1000000):
    return pl.pallas_call(
        kernel,
        out_shape=out_shape,
        in_specs=specs,
        out_specs=jax.tree.map(lambda _: VMEM, out_shape),
        scratch_shapes=list(scratch),
        compiler_params=pltpu.CompilerParams(vmem_limit_bytes=32 * 2**20),
        cost_estimate=pl.CostEstimate(flops=flops, bytes_accessed=1000000, transcendentals=0),
    )(*args)


def body(data, recip, gap, owner, weights, start_row, end_row, recorded):
    freq_here = lax.axis_index("freq")
    src_count = lax.axis_size("pair") * lax.axis_size("half")
    pairs = src_count // 2
    total_out = weights.shape[3]
    points = data.shape[3]

    recip_rows = jnp.swapaxes(recip[:, 0], 1, 2).reshape(2 * NEAR, RECV)
    depth = points // 2
    parts = pl.pallas_call(
        main_product,
        grid=(points // depth,),
        out_shape=jax.ShapeDtypeStruct((pairs, 2, SLOT_ROWS, RECV), BF16),
        in_specs=[
            pl.BlockSpec((NEAR, RECV), lambda k: (0, 0)),
            pl.BlockSpec((2 * NEAR, RECV), lambda k: (0, 0)),
            pl.BlockSpec((2, 1, RECV, depth), lambda k: (0, 0, 0, k)),
            pl.BlockSpec((2, 1, depth, total_out), lambda k: (0, 0, k, 0)),
        ],
        out_specs=pl.BlockSpec((pairs, 2, SLOT_ROWS, RECV), lambda k: (0, 0, 0, 0)),
        scratch_shapes=[
            pltpu.VMEM((2, RECV, total_out), F32),
            pltpu.VMEM((RECV, RECV), BF16),
            pltpu.VMEM((pairs, NEAR, RECV), F32),
        ],
        cost_estimate=pl.CostEstimate(flops=8 * RECV * points * total_out, bytes_accessed=5000000, transcendentals=0),
    )(gap.T, recip_rows, data, weights)
    parts = parts.reshape(src_count, SLOT_ROWS, RECV)
    parts = lax.all_to_all(parts, ("pair", "half"), 0, 0, tiled=True)
    begin = freq_here * T_DEV - HALO
    first, last = start_row[0] - begin, end_row[0] - begin
    row = lax.broadcasted_iota(jnp.int32, (WROWS, RECV), 0)
    keep_rows = ((row >= first) & (row < last)).astype(F32)
    row = jnp.arange(GROWS, dtype=jnp.int32) // GROUP - LEAD
    keep = (row >= first) & (row < last)
    rows = lax.dynamic_index_in_dim(jnp.asarray(phase_rows()), freq_here, 0, keepdims=False)
    rows = jnp.where(keep[:, None], rows, jnp.zeros_like(rows))
    target = jnp.pad(recorded.reshape(WROWS, -1), ((0, 16), (0, 0)))

    copies = call(
        sum_and_fill,
        jax.ShapeDtypeStruct((NF, 2, 8, RECV), F32),
        (jnp.broadcast_to(owner[None], (8, src_count)), parts, keep_rows, rows, target),
        [VMEM, VMEM, ANY, ANY, ANY],
        [
            pltpu.VMEM((NEAR * src_count, RECV), BF16),
            pltpu.VMEM((NEAR * src_count, RECV), BF16),
            pltpu.VMEM((RECV, RECV), F32),
        ],
    )
    copies = copies.reshape(NF * 2, 8, RECV)
    spread = lax.all_to_all(copies, ("freq", "half"), 0, 0, tiled=True).reshape(NF * 16, RECV)

    trace_rows = 8 * (WROWS + 2 * LEAD)
    gram, trace = call(
        trace_and_gram,
        (jax.ShapeDtypeStruct((src_count, 8, RECV), F32), jax.ShapeDtypeStruct((trace_rows, RECV), F32)),
        (keep_rows, spread, rows, target),
        [VMEM] * 4,
        [pltpu.VMEM((8 * GROWS, RECV), F32), pltpu.VMEM((GROWS, GROWS), F32)],
    )
    gram = lax.all_to_all(gram, ("pair", "half"), 0, 0, tiled=True)
    damping = float(WROWS * total_out * RECV)
    primaries, filters = call(
        functools.partial(solve_and_filter, damping),
        (jax.ShapeDtypeStruct(recorded.shape, BF16), jax.ShapeDtypeStruct((1, UNKNOWNS), F32)),
        (keep_rows, gram, trace, recorded),
        [VMEM] * 4,
        [pltpu.VMEM((SIDE, RECV), F32)],
    )
    return primaries, filters


def solution(mesh):
    freq, src = mesh.devices.shape
    mesh = Mesh(mesh.devices.reshape(freq, src // 2, 2), ("freq", "pair", "half"))
    src = ("pair", "half")
    placed = (
        P(None, "freq", None, src),
        P(None, "freq", None, src),
        P(None, src),
        P(),
        P(None, "freq", src, None),
        P("freq"),
        P("freq"),
        P("freq", src, None),
    )
    return jax.shard_map(
        body,
        mesh=mesh,
        in_specs=placed,
        out_specs=(P("freq", src, None), P("freq", None)),
        check_vma=False,
    )
```

```python
import functools
import math

import jax
import jax.numpy as jnp
import ml_dtypes
import numpy as np
from jax import lax
from jax.experimental import pallas as pl
from jax.experimental.pallas import tpu as pltpu
from jax.sharding import Mesh, PartitionSpec as P

RECV = 128
NFFT = 512
F_LOW = 40
NEAR = 16
HALO = 8
LAGS_T = 9
LAGS_X = 3
LEAD = LAGS_T // 2
T_DEV = 32
WROWS = T_DEV + 2 * HALO
NF = 16
GROUP = 4
GROWS = 256
SIDE = 40
UNKNOWNS = LAGS_T * LAGS_X
TARGET_COL = GROUP * LEAD + 3
CENTRE_ROW = GROUP * LEAD + 1
PACK_AT = (0, 40, 72, 96, 112)
RECIP_AT, GAP_AT, SLOT_ROWS = 16, 32, 48
HALF = RECV // 2
IMAG_AT, SCALE_AT = HALF + 16, HALF + 32
SPAN = 166.0
VMEM = pl.BlockSpec(memory_space=pltpu.VMEM)
ANY = pl.BlockSpec(memory_space=pl.ANY)
F32 = jnp.float32
BF16 = jnp.bfloat16


def split3(x):
    high = x.astype(ml_dtypes.bfloat16)
    rest = x - high.astype(np.float32)
    mid = rest.astype(ml_dtypes.bfloat16)
    low = (rest - mid.astype(np.float32)).astype(ml_dtypes.bfloat16)
    return high, mid, low


@functools.cache
def phase_rows():
    table = np.zeros((NF, GROWS, 256), ml_dtypes.bfloat16)
    freqs = np.arange(NF)
    scale = 1.0 / math.sqrt(NF)
    for window in range(NF):
        for row in range(WROWS):
            time = window * T_DEV - HALO + row
            if not 0 <= time < NFFT:
                continue
            turns = (F_LOW + freqs) * time % NFFT
            angle = turns * (2.0 * math.pi / NFFT)
            phase = np.stack([np.cos(angle), -np.sin(angle)], axis=0).reshape(-1) * scale
            high, mid, low = split3(phase.astype(np.float32))
            at = GROUP * (row + LEAD)
            table[window, at : at + 3, :192] = np.concatenate([high, high, mid, high, low, mid])
            table[window, at + 3, 192 + row] = 1
    return table


def halves(first, second):
    lanes = lax.broadcasted_iota(jnp.int32, first.shape, 1)
    low = jnp.where(lanes < HALF, first, pltpu.roll(second, HALF, 1))
    return low, jnp.where(lanes < HALF, pltpu.roll(first, HALF, 1), second)


def encode(value, scale):
    size = jnp.exp(jnp.abs(value) * (SPAN / scale) - SPAN / 2)
    return jnp.where(value < 0, -size, size)


def decode(code, scale):
    size = (jnp.log(jnp.abs(code)) + SPAN / 2) * (scale * (1.0 / SPAN))
    return jnp.where(code < 0, -size, size)


def main_product(gap_ref, recip_ref, data_ref, weights_ref, out_ref, acc_ref, mask_ref, near_ref):
    step = pl.program_id(0)
    depth = data_ref.shape[3]
    pairs = out_ref.shape[0]

    @pl.when(step == 0)
    def _():
        acc_ref[...] = jnp.zeros_like(acc_ref)
        gap = jnp.where(gap_ref[...] == 1, 1.0, 0.0)
        full = jnp.concatenate([gap, jnp.zeros((RECV - NEAR, RECV), F32)], axis=0)
        mask_ref[...] = (1.0 - full.T).astype(BF16)
        recip = recip_ref[...].astype(F32)
        recip = halves(recip[:NEAR], recip[NEAR:])
        lanes = lax.broadcasted_iota(jnp.int32, (NEAR, RECV), 1)
        for half in range(2):
            out_ref[:, half, RECIP_AT:GAP_AT] = jnp.broadcast_to(
                recip[half].astype(BF16)[None], (pairs, NEAR, RECV)
            )
        for pair in range(pairs):
            at, off = RECV * (pair // 8), 16 * (pair % 8)
            real = weights_ref[0, 0, :NEAR, at : at + RECV].astype(F32)
            imag = weights_ref[1, 0, :NEAR, at : at + RECV].astype(F32)
            real = pltpu.roll(real, (HALF - off) % RECV, 1)
            imag = pltpu.roll(imag, (IMAG_AT - off) % RECV, 1)
            near_ref[pair] = jnp.where(lanes < IMAG_AT, real, imag)

    @pl.when(step == 1)
    def _():
        mask_ref[...] = jnp.ones_like(mask_ref)

    panel = data_ref[...].reshape(2 * RECV, depth)
    mask = mask_ref[...]
    near = panel[:, :RECV] * jnp.concatenate([mask, mask], axis=0)
    panel = jnp.concatenate([near, panel[:, RECV:]], axis=1)
    both = jnp.concatenate([weights_ref[0, 0], weights_ref[1, 0]], axis=1)
    product = jnp.dot(panel, both, preferred_element_type=F32)
    width = product.shape[1] // 2
    acc_ref[0] += product[:RECV, :width] - product[RECV:, width:]
    acc_ref[1] += product[:RECV, width:] + product[RECV:, :width]

    @pl.when(step == pl.num_programs(0) - 1)
    def _():
        gap = jnp.where(gap_ref[...] == 1, 1.0, 0.0)
        gaps = gap, pltpu.roll(gap, HALF, 1)
        lanes = lax.broadcasted_iota(jnp.int32, (pairs, NEAR, RECV), 2)
        for half, pred in enumerate(halves(acc_ref[0].T, acc_ref[1].T)):
            pred = pred.reshape(pairs, 16, RECV)
            scale = jnp.max(jnp.abs(pred), axis=(1, 2), keepdims=True) * 1.01 + 1e-30
            scale = scale.astype(BF16).astype(F32)
            out_ref[:, half, :RECIP_AT] = encode(pred, scale).astype(BF16)
            tile = jnp.where(lanes < SCALE_AT, near_ref[...], jnp.broadcast_to(scale, lanes.shape))
            tile = jnp.where(lanes < HALF, jnp.broadcast_to(gaps[half][None], lanes.shape), tile)
            out_ref[:, half, GAP_AT:] = tile.astype(BF16)


def sum_and_fill(owner_ref, part_ref, keep_ref, rows_ref, target_ref, out_ref, z_ref, w_ref, f_ref):
    del keep_ref, rows_ref, target_ref
    slots = part_ref.shape[0]
    total = jnp.zeros((16, RECV), F32)
    for j in range(slots):
        scale = part_ref[j, GAP_AT:].astype(F32)[:, SCALE_AT : SCALE_AT + 1]
        code = part_ref[j, :RECIP_AT].astype(F32)
        total = total + decode(code, jnp.broadcast_to(scale, code.shape))
    lanes = lax.broadcasted_iota(jnp.int32, (NEAR, RECV), 1)
    for j in range(slots):
        tile = part_ref[owner_ref[0, j], GAP_AT:]
        gap = tile.astype(F32)
        gap = jnp.where(lanes < HALF, gap, pltpu.roll(gap, HALF, 1))
        at = slice(NEAR * j, NEAR * j + NEAR)
        z_ref[at, :] = (part_ref[j, RECIP_AT:GAP_AT].astype(F32) * gap).astype(BF16)
        w_ref[at, :] = tile
    f_ref[...] = lax.dot_general(
        w_ref[...], z_ref[...], (((0,), (0,)), ((), ())), preferred_element_type=F32
    )
    by_real = f_ref[HALF:IMAG_AT, :]
    by_imag = pltpu.roll(f_ref[IMAG_AT:SCALE_AT, :], HALF, 1)
    pred = total + by_real + jnp.where(lanes < HALF, -by_imag, by_imag)
    out_ref[...] = jnp.broadcast_to(pred.reshape(1, 2, 8, RECV), out_ref.shape)


def two_parts(x):
    high = x.astype(BF16)
    return high, (x - high.astype(F32)).astype(BF16)


def trace_and_gram(keep_ref, x_ref, rows_ref, target_ref, gram_ref, trace_ref, a_ref, g_ref):
    sources = 8
    columns = []
    for s in range(sources):
        low, high = (x_ref[pl.ds(8 * half + s, NF, stride=16), :] for half in range(2))
        columns.append(jnp.concatenate(halves(low, high), axis=0))
    x = jnp.concatenate(columns, axis=1)
    high, rest = x.astype(BF16), x
    rest = rest - high.astype(F32)
    mid = rest.astype(BF16)
    low = (rest - mid.astype(F32)).astype(BF16)
    stack = jnp.concatenate([high, mid, high, low, high, mid, target_ref[...]], axis=0)
    base = jnp.dot(rows_ref[...], stack, preferred_element_type=F32)
    times = GROWS // GROUP
    recv = lax.broadcasted_iota(jnp.int32, (times, RECV), 1)
    for s in range(sources):
        a_ref[s * GROWS : (s + 1) * GROWS, :] = base[:, s * RECV : (s + 1) * RECV]
    for s in range(sources):
        ahead = pl.ds(s * GROWS, times, stride=GROUP)
        a_ref[ahead, :] = jnp.where(recv < RECV - 1, pltpu.roll(a_ref[ahead, :], RECV - 1, 1), 0.0)
        behind = pl.ds(s * GROWS + 2, times, stride=GROUP)
        a_ref[behind, :] = jnp.where(recv > 0, pltpu.roll(a_ref[behind, :], 1, 1), 0.0)
    for s in range(sources):
        mine = a_ref[pl.ds(s * GROWS + 1, WROWS + 2 * LEAD, stride=GROUP), :]
        trace_ref[pl.ds(s, WROWS + 2 * LEAD, stride=sources), :] = mine
    high, low = two_parts(jnp.concatenate([a_ref[s * GROWS : (s + 1) * GROWS, :] for s in range(sources)], axis=1))
    dims = (((1,), (1,)), ((), ()))
    left = jnp.concatenate([high, high, low], axis=1)
    right = jnp.concatenate([high, 2.0 * low, low], axis=1)
    g_ref[...] = lax.dot_general(left, right, dims, preferred_element_type=F32)
    total = jnp.zeros((SIDE, RECV), F32)
    for u in range(WROWS):
        at = GROUP * u
        if at + SIDE <= RECV:
            part = g_ref[at : at + SIDE, :RECV]
            part = pltpu.roll(part, (RECV - at) % RECV, 1)
        elif at >= RECV:
            part = g_ref[at : at + SIDE, RECV:]
            part = pltpu.roll(part, (2 * RECV - at) % RECV, 1)
        else:
            part = pltpu.roll(g_ref[at : at + SIDE, :], 2 * RECV - at, 1)[:, :RECV]
        total = total + part * keep_ref[u : u + 1, :]
    full = jnp.concatenate([total, jnp.zeros((RECV - SIDE, RECV), F32)], axis=0)
    total = 0.5 * (total + full.T[:SIDE])
    lanes = lax.broadcasted_iota(jnp.int32, (8, RECV), 1)
    packed = jnp.zeros((8, RECV), F32)
    for g, at in enumerate(PACK_AT):
        piece = total[8 * g : 8 * g + 8]
        piece = jnp.where((lanes >= 8 * g) & (lanes < SIDE), piece, 0.0)
        packed = packed + pltpu.roll(piece, at - 8 * g, 1)
    gram_ref[...] = jnp.broadcast_to(packed[None], gram_ref.shape)


def solve_and_filter(damping, keep_ref, gram_ref, trace_ref, recorded_ref, out_ref, filters_ref, h_ref):
    packed = jnp.sum(gram_ref[...], axis=0)
    lanes = lax.broadcasted_iota(jnp.int32, (8, RECV), 1)
    pieces = []
    for g, at in enumerate(PACK_AT):
        piece = pltpu.roll(packed, (RECV + 8 * g - at) % RECV, 1)
        pieces.append(jnp.where((lanes >= 8 * g) & (lanes < SIDE), piece, 0.0))
    upper = jnp.concatenate(pieces, axis=0)
    full = jnp.concatenate([upper, jnp.zeros((RECV - SIDE, RECV), F32)], axis=0)
    row = lax.broadcasted_iota(jnp.int32, (SIDE, RECV), 0)
    lane = lax.broadcasted_iota(jnp.int32, (SIDE, RECV), 1)
    system = jnp.where(lane // 8 < row // 8, full.T[:SIDE], upper)
    unknown = lax.rem(row, GROUP) < LAGS_X
    system = system + jnp.where((row == lane) & unknown, damping, 0.0)
    system = system + jnp.where((row == CENTRE_ROW) & (lane == TARGET_COL), damping, 0.0)
    order = [k for k in range(GROUP * LAGS_T) if k % GROUP < LAGS_X]
    for one, two in zip(order[:-1:2], order[1::2]):
        first = jnp.broadcast_to(system[:, one : one + 1], (SIDE, RECV))
        second = jnp.broadcast_to(system[:, two : two + 1], (SIDE, RECV))
        top, bottom = system[one : one + 1, :], system[two : two + 1, :]
        a, b, d = first[one : one + 1], second[one : one + 1], second[two : two + 1]
        scale = 1.0 / (a * d - b * b)
        top, bottom = (d * top - b * bottom) * scale, (a * bottom - b * top) * scale
        rest = system - first * top - second * bottom
        system = jnp.where(row == one, top, jnp.where(row == two, bottom, rest))
    last = order[-1]
    column = jnp.broadcast_to(system[:, last : last + 1], (SIDE, RECV))
    pivot_row = system[last : last + 1, :] / column[last : last + 1]
    system = jnp.where(row == last, pivot_row, system - column * pivot_row)
    chosen = (lane < UNKNOWNS) & (row == GROUP * (LAGS_T - 1 - lane // LAGS_X) + lane % LAGS_X)
    h_ref[...] = jnp.broadcast_to(system[:, TARGET_COL : TARGET_COL + 1], (SIDE, RECV))
    filters_ref[...] = jnp.sum(jnp.where(chosen, h_ref[...], 0.0), axis=0, keepdims=True)[:, :UNKNOWNS]
    recv = lax.broadcasted_iota(jnp.int32, (8, RECV), 1)
    taps = [[jnp.broadcast_to(h_ref[GROUP * p + c : GROUP * p + c + 1, :], (8, RECV)) for c in range(LAGS_X)] for p in range(LAGS_T)]
    for u in range(WROWS):
        sums = [None] * LAGS_X
        for p in range(LAGS_T):
            value = trace_ref[8 * (u + p) : 8 * (u + p) + 8, :]
            for c in range(LAGS_X):
                term = taps[p][c] * value
                sums[c] = term if sums[c] is None else sums[c] + term
        ahead = jnp.where(recv < RECV - 1, pltpu.roll(sums[0], RECV - 1, 1), 0.0)
        behind = jnp.where(recv > 0, pltpu.roll(sums[2], 1, 1), 0.0)
        value = recorded_ref[u].astype(F32) - (sums[1] + ahead + behind)
        out_ref[u] = (value * keep_ref[u : u + 1, :]).astype(BF16)


def call(kernel, out_shape, args, specs, scratch=(), flops=1000000):
    return pl.pallas_call(
        kernel,
        out_shape=out_shape,
        in_specs=specs,
        out_specs=jax.tree.map(lambda _: VMEM, out_shape),
        scratch_shapes=list(scratch),
        compiler_params=pltpu.CompilerParams(vmem_limit_bytes=32 * 2**20),
        cost_estimate=pl.CostEstimate(flops=flops, bytes_accessed=1000000, transcendentals=0),
    )(*args)


def body(data, recip, gap, owner, weights, start_row, end_row, recorded):
    freq_here = lax.axis_index("freq")
    src_count = lax.axis_size("pair") * lax.axis_size("half")
    pairs = src_count // 2
    total_out = weights.shape[3]
    points = data.shape[3]

    recip_rows = jnp.swapaxes(recip[:, 0], 1, 2).reshape(2 * NEAR, RECV)
    depth = points // 2
    parts = pl.pallas_call(
        main_product,
        grid=(points // depth,),
        out_shape=jax.ShapeDtypeStruct((pairs, 2, SLOT_ROWS, RECV), BF16),
        in_specs=[
            pl.BlockSpec((NEAR, RECV), lambda k: (0, 0)),
            pl.BlockSpec((2 * NEAR, RECV), lambda k: (0, 0)),
            pl.BlockSpec((2, 1, RECV, depth), lambda k: (0, 0, 0, k)),
            pl.BlockSpec((2, 1, depth, total_out), lambda k: (0, 0, k, 0)),
        ],
        out_specs=pl.BlockSpec((pairs, 2, SLOT_ROWS, RECV), lambda k: (0, 0, 0, 0)),
        scratch_shapes=[
            pltpu.VMEM((2, RECV, total_out), F32),
            pltpu.VMEM((RECV, RECV), BF16),
            pltpu.VMEM((pairs, NEAR, RECV), F32),
        ],
        cost_estimate=pl.CostEstimate(flops=8 * RECV * points * total_out, bytes_accessed=5000000, transcendentals=0),
    )(gap.T, recip_rows, data, weights)
    parts = parts.reshape(src_count, SLOT_ROWS, RECV)
    parts = lax.all_to_all(parts, ("pair", "half"), 0, 0, tiled=True)
    begin = freq_here * T_DEV - HALO
    first, last = start_row[0] - begin, end_row[0] - begin
    row = lax.broadcasted_iota(jnp.int32, (WROWS, RECV), 0)
    keep_rows = ((row >= first) & (row < last)).astype(F32)
    row = jnp.arange(GROWS, dtype=jnp.int32) // GROUP - LEAD
    keep = (row >= first) & (row < last)
    rows = lax.dynamic_index_in_dim(jnp.asarray(phase_rows()), freq_here, 0, keepdims=False)
    rows = jnp.where(keep[:, None], rows, jnp.zeros_like(rows))
    target = jnp.pad(recorded.reshape(WROWS, -1), ((0, 16), (0, 0)))

    copies = call(
        sum_and_fill,
        jax.ShapeDtypeStruct((NF, 2, 8, RECV), F32),
        (jnp.broadcast_to(owner[None], (8, src_count)), parts, keep_rows, rows, target),
        [VMEM, VMEM, ANY, ANY, ANY],
        [
            pltpu.VMEM((NEAR * src_count, RECV), BF16),
            pltpu.VMEM((NEAR * src_count, RECV), BF16),
            pltpu.VMEM((RECV, RECV), F32),
        ],
    )
    copies = copies.reshape(NF * 2, 8, RECV)
    spread = lax.all_to_all(copies, ("freq", "half"), 0, 0, tiled=True).reshape(NF * 16, RECV)

    trace_rows = 8 * (WROWS + 2 * LEAD)
    gram, trace = call(
        trace_and_gram,
        (jax.ShapeDtypeStruct((src_count, 8, RECV), F32), jax.ShapeDtypeStruct((trace_rows, RECV), F32)),
        (keep_rows, spread, rows, target),
        [VMEM] * 4,
        [pltpu.VMEM((8 * GROWS, RECV), F32), pltpu.VMEM((GROWS, GROWS), F32)],
    )
    gram = lax.all_to_all(gram, ("pair", "half"), 0, 0, tiled=True)
    damping = float(WROWS * total_out * RECV)
    primaries, filters = call(
        functools.partial(solve_and_filter, damping),
        (jax.ShapeDtypeStruct(recorded.shape, BF16), jax.ShapeDtypeStruct((1, UNKNOWNS), F32)),
        (keep_rows, gram, trace, recorded),
        [VMEM] * 4,
        [pltpu.VMEM((SIDE, RECV), F32)],
    )
    return primaries, filters


def solution(mesh):
    freq, src = mesh.devices.shape
    mesh = Mesh(mesh.devices.reshape(freq, src // 2, 2), ("freq", "pair", "half"))
    src = ("pair", "half")
    placed = (
        P(None, "freq", None, src),
        P(None, "freq", None, src),
        P(None, src),
        P(),
        P(None, "freq", src, None),
        P("freq"),
        P("freq"),
        P("freq", src, None),
    )
    return jax.shard_map(
        body,
        mesh=mesh,
        in_specs=placed,
        out_specs=(P("freq", src, None), P("freq", None)),
        check_vma=False,
    )
```

```python
import functools
import math

import jax
import jax.numpy as jnp
import ml_dtypes
import numpy as np
from jax import lax
from jax.experimental import pallas as pl
from jax.experimental.pallas import tpu as pltpu
from jax.sharding import Mesh, PartitionSpec as P

RECV = 128
NFFT = 512
F_LOW = 40
NEAR = 16
HALO = 8
LAGS_T = 9
LAGS_X = 3
LEAD = LAGS_T // 2
T_DEV = 32
WROWS = T_DEV + 2 * HALO
NF = 16
GROUP = 4
GROWS = 256
AROWS = GROUP * (WROWS + 2 * LEAD)
SIDE = 40
UNKNOWNS = LAGS_T * LAGS_X
TARGET_COL = GROUP * LEAD + 3
CENTRE_ROW = GROUP * LEAD + 1
PACK_AT = (0, 40, 72, 96, 112)
RECIP_AT, GAP_AT, SLOT_ROWS = 16, 32, 48
HALF = RECV // 2
IMAG_AT, SCALE_AT = HALF + 16, HALF + 32
SPAN = 166.0
VMEM = pl.BlockSpec(memory_space=pltpu.VMEM)
ANY = pl.BlockSpec(memory_space=pl.ANY)
F32 = jnp.float32
BF16 = jnp.bfloat16


def split3(x):
    high = x.astype(ml_dtypes.bfloat16)
    rest = x - high.astype(np.float32)
    mid = rest.astype(ml_dtypes.bfloat16)
    low = (rest - mid.astype(np.float32)).astype(ml_dtypes.bfloat16)
    return high, mid, low


@functools.cache
def phase_rows():
    table = np.zeros((NF, AROWS, 256), ml_dtypes.bfloat16)
    freqs = np.arange(NF)
    scale = 1.0 / math.sqrt(NF)
    for window in range(NF):
        for row in range(WROWS):
            time = window * T_DEV - HALO + row
            if not 0 <= time < NFFT:
                continue
            turns = (F_LOW + freqs) * time % NFFT
            angle = turns * (2.0 * math.pi / NFFT)
            phase = np.stack([np.cos(angle), -np.sin(angle)], axis=0).reshape(-1) * scale
            high, mid, low = split3(phase.astype(np.float32))
            at = GROUP * (row + LEAD)
            table[window, at : at + 3, :192] = np.concatenate([high, high, mid, high, low, mid])
            table[window, at + 3, 192 + row] = 1
    return table


def halves(first, second):
    lanes = lax.broadcasted_iota(jnp.int32, first.shape, 1)
    low = jnp.where(lanes < HALF, first, pltpu.roll(second, HALF, 1))
    return low, jnp.where(lanes < HALF, pltpu.roll(first, HALF, 1), second)


def encode(value, scale):
    size = jnp.exp(jnp.abs(value) * (SPAN / scale) - SPAN / 2)
    return jnp.where(value < 0, -size, size)


def decode(code, scale):
    size = (jnp.log(jnp.abs(code)) + SPAN / 2) * (scale * (1.0 / SPAN))
    return jnp.where(code < 0, -size, size)


def main_product(gap_ref, recip_ref, data_ref, weights_ref, out_ref, acc_ref, mask_ref, near_ref):
    step = pl.program_id(0)
    depth = data_ref.shape[3]
    pairs = out_ref.shape[0]

    @pl.when(step == 0)
    def _():
        acc_ref[...] = jnp.zeros_like(acc_ref)
        gap = jnp.where(gap_ref[...] == 1, 1.0, 0.0)
        full = jnp.concatenate([gap, jnp.zeros((RECV - NEAR, RECV), F32)], axis=0)
        mask_ref[...] = (1.0 - full.T).astype(BF16)
        recip = recip_ref[...].astype(F32)
        recip = halves(recip[:NEAR], recip[NEAR:])
        lanes = lax.broadcasted_iota(jnp.int32, (NEAR, RECV), 1)
        for half in range(2):
            out_ref[:, half, RECIP_AT:GAP_AT] = jnp.broadcast_to(
                recip[half].astype(BF16)[None], (pairs, NEAR, RECV)
            )
        for pair in range(pairs):
            at, off = RECV * (pair // 8), 16 * (pair % 8)
            real = weights_ref[0, 0, :NEAR, at : at + RECV].astype(F32)
            imag = weights_ref[1, 0, :NEAR, at : at + RECV].astype(F32)
            real = pltpu.roll(real, (HALF - off) % RECV, 1)
            imag = pltpu.roll(imag, (IMAG_AT - off) % RECV, 1)
            near_ref[pair] = jnp.where(lanes < IMAG_AT, real, imag)

    @pl.when(step == 1)
    def _():
        mask_ref[...] = jnp.ones_like(mask_ref)

    panel = data_ref[...].reshape(2 * RECV, depth)
    mask = mask_ref[...]
    near = panel[:, :RECV] * jnp.concatenate([mask, mask], axis=0)
    panel = jnp.concatenate([near, panel[:, RECV:]], axis=1)
    both = jnp.concatenate([weights_ref[0, 0], weights_ref[1, 0]], axis=1)
    product = jnp.dot(panel, both, preferred_element_type=F32)
    width = product.shape[1] // 2
    acc_ref[0] += product[:RECV, :width] - product[RECV:, width:]
    acc_ref[1] += product[:RECV, width:] + product[RECV:, :width]

    @pl.when(step == pl.num_programs(0) - 1)
    def _():
        gap = jnp.where(gap_ref[...] == 1, 1.0, 0.0)
        gaps = gap, pltpu.roll(gap, HALF, 1)
        lanes = lax.broadcasted_iota(jnp.int32, (pairs, NEAR, RECV), 2)
        for half, pred in enumerate(halves(acc_ref[0].T, acc_ref[1].T)):
            pred = pred.reshape(pairs, 16, RECV)
            scale = jnp.max(jnp.abs(pred), axis=(1, 2), keepdims=True) * 1.01 + 1e-30
            scale = scale.astype(BF16).astype(F32)
            out_ref[:, half, :RECIP_AT] = encode(pred, scale).astype(BF16)
            tile = jnp.where(lanes < SCALE_AT, near_ref[...], jnp.broadcast_to(scale, lanes.shape))
            tile = jnp.where(lanes < HALF, jnp.broadcast_to(gaps[half][None], lanes.shape), tile)
            out_ref[:, half, GAP_AT:] = tile.astype(BF16)


def sum_and_fill(owner_ref, part_ref, keep_ref, rows_ref, target_ref, out_ref, z_ref, w_ref, f_ref):
    del keep_ref, rows_ref, target_ref
    slots = part_ref.shape[0]
    total = jnp.zeros((16, RECV), F32)
    for j in range(slots):
        scale = part_ref[j, GAP_AT:].astype(F32)[:, SCALE_AT : SCALE_AT + 1]
        code = part_ref[j, :RECIP_AT].astype(F32)
        total = total + decode(code, jnp.broadcast_to(scale, code.shape))
    lanes = lax.broadcasted_iota(jnp.int32, (NEAR, RECV), 1)
    for j in range(slots):
        tile = part_ref[owner_ref[0, j], GAP_AT:]
        gap = tile.astype(F32)
        gap = jnp.where(lanes < HALF, gap, pltpu.roll(gap, HALF, 1))
        at = slice(NEAR * j, NEAR * j + NEAR)
        z_ref[at, :] = (part_ref[j, RECIP_AT:GAP_AT].astype(F32) * gap).astype(BF16)
        w_ref[at, :] = tile
    f_ref[...] = lax.dot_general(
        w_ref[...], z_ref[...], (((0,), (0,)), ((), ())), preferred_element_type=F32
    )
    by_real = f_ref[HALF:IMAG_AT, :]
    by_imag = pltpu.roll(f_ref[IMAG_AT:SCALE_AT, :], HALF, 1)
    pred = total + by_real + jnp.where(lanes < HALF, -by_imag, by_imag)
    out_ref[...] = jnp.broadcast_to(pred.reshape(1, 2, 8, RECV), out_ref.shape)


def two_parts(x):
    high = x.astype(BF16)
    return high, (x - high.astype(F32)).astype(BF16)


def trace_and_gram(keep_ref, x_ref, rows_ref, target_ref, gram_ref, trace_ref, a_ref, g_ref):
    sources = 8
    columns = []
    for s in range(sources):
        low, high = (x_ref[pl.ds(8 * half + s, NF, stride=16), :] for half in range(2))
        columns.append(jnp.concatenate(halves(low, high), axis=0))
    x = jnp.concatenate(columns, axis=1)
    high, rest = x.astype(BF16), x
    rest = rest - high.astype(F32)
    mid = rest.astype(BF16)
    low = (rest - mid.astype(F32)).astype(BF16)
    stack = jnp.concatenate([high, mid, high, low, high, mid, target_ref[...]], axis=0)
    base = jnp.dot(rows_ref[...], stack, preferred_element_type=F32)
    times = AROWS // GROUP
    recv = lax.broadcasted_iota(jnp.int32, (times, RECV), 1)
    for s in range(sources):
        a_ref[s * AROWS : (s + 1) * AROWS, :] = base[:, s * RECV : (s + 1) * RECV]
    for s in range(sources):
        ahead = pl.ds(s * AROWS, times, stride=GROUP)
        a_ref[ahead, :] = jnp.where(recv < RECV - 1, pltpu.roll(a_ref[ahead, :], RECV - 1, 1), 0.0)
        behind = pl.ds(s * AROWS + 2, times, stride=GROUP)
        a_ref[behind, :] = jnp.where(recv > 0, pltpu.roll(a_ref[behind, :], 1, 1), 0.0)
    for s in range(sources):
        mine = a_ref[pl.ds(s * AROWS + 1, WROWS + 2 * LEAD, stride=GROUP), :]
        trace_ref[pl.ds(s, WROWS + 2 * LEAD, stride=sources), :] = mine
    high, low = two_parts(jnp.concatenate([a_ref[s * AROWS : (s + 1) * AROWS, :] for s in range(sources)], axis=1))
    dims = (((1,), (1,)), ((), ()))
    rest = jnp.zeros((GROWS - AROWS, high.shape[1]), BF16)
    wide, narrow = (jnp.concatenate([part, rest], axis=0) for part in (high, low))
    g_ref[:AROWS] = lax.dot_general(high, wide, dims, preferred_element_type=F32) + 2.0 * lax.dot_general(
        high, narrow, dims, preferred_element_type=F32
    )
    g_ref[AROWS:] = jnp.zeros((GROWS - AROWS, GROWS), F32)
    total = jnp.zeros((SIDE, RECV), F32)
    for u in range(WROWS):
        at = GROUP * u
        if at + SIDE <= RECV:
            part = g_ref[at : at + SIDE, :RECV]
            part = pltpu.roll(part, (RECV - at) % RECV, 1)
        elif at >= RECV:
            part = g_ref[at : at + SIDE, RECV:]
            part = pltpu.roll(part, (2 * RECV - at) % RECV, 1)
        else:
            part = pltpu.roll(g_ref[at : at + SIDE, :], 2 * RECV - at, 1)[:, :RECV]
        total = total + part * keep_ref[u : u + 1, :]
    full = jnp.concatenate([total, jnp.zeros((RECV - SIDE, RECV), F32)], axis=0)
    total = 0.5 * (total + full.T[:SIDE])
    lanes = lax.broadcasted_iota(jnp.int32, (8, RECV), 1)
    packed = jnp.zeros((8, RECV), F32)
    for g, at in enumerate(PACK_AT):
        piece = total[8 * g : 8 * g + 8]
        piece = jnp.where((lanes >= 8 * g) & (lanes < SIDE), piece, 0.0)
        packed = packed + pltpu.roll(piece, at - 8 * g, 1)
    gram_ref[...] = jnp.broadcast_to(packed[None], gram_ref.shape)


def solve_and_filter(damping, keep_ref, gram_ref, trace_ref, recorded_ref, out_ref, filters_ref, h_ref):
    packed = jnp.sum(gram_ref[...], axis=0)
    lanes = lax.broadcasted_iota(jnp.int32, (8, RECV), 1)
    pieces = []
    for g, at in enumerate(PACK_AT):
        piece = pltpu.roll(packed, (RECV + 8 * g - at) % RECV, 1)
        pieces.append(jnp.where((lanes >= 8 * g) & (lanes < SIDE), piece, 0.0))
    upper = jnp.concatenate(pieces, axis=0)
    full = jnp.concatenate([upper, jnp.zeros((RECV - SIDE, RECV), F32)], axis=0)
    row = lax.broadcasted_iota(jnp.int32, (SIDE, RECV), 0)
    lane = lax.broadcasted_iota(jnp.int32, (SIDE, RECV), 1)
    system = jnp.where(lane // 8 < row // 8, full.T[:SIDE], upper)
    unknown = lax.rem(row, GROUP) < LAGS_X
    system = system + jnp.where((row == lane) & unknown, damping, 0.0)
    system = system + jnp.where((row == CENTRE_ROW) & (lane == TARGET_COL), damping, 0.0)
    order = [k for k in range(GROUP * LAGS_T) if k % GROUP < LAGS_X]
    for one, two in zip(order[:-1:2], order[1::2]):
        first = jnp.broadcast_to(system[:, one : one + 1], (SIDE, RECV))
        second = jnp.broadcast_to(system[:, two : two + 1], (SIDE, RECV))
        top, bottom = system[one : one + 1, :], system[two : two + 1, :]
        a, b, d = first[one : one + 1], second[one : one + 1], second[two : two + 1]
        scale = 1.0 / (a * d - b * b)
        top, bottom = (d * top - b * bottom) * scale, (a * bottom - b * top) * scale
        rest = system - first * top - second * bottom
        system = jnp.where(row == one, top, jnp.where(row == two, bottom, rest))
    last = order[-1]
    column = jnp.broadcast_to(system[:, last : last + 1], (SIDE, RECV))
    pivot_row = system[last : last + 1, :] / column[last : last + 1]
    system = jnp.where(row == last, pivot_row, system - column * pivot_row)
    chosen = (lane < UNKNOWNS) & (row == GROUP * (LAGS_T - 1 - lane // LAGS_X) + lane % LAGS_X)
    h_ref[...] = jnp.broadcast_to(system[:, TARGET_COL : TARGET_COL + 1], (SIDE, RECV))
    filters_ref[...] = jnp.sum(jnp.where(chosen, h_ref[...], 0.0), axis=0, keepdims=True)[:, :UNKNOWNS]
    recv = lax.broadcasted_iota(jnp.int32, (8, RECV), 1)
    taps = [[jnp.broadcast_to(h_ref[GROUP * p + c : GROUP * p + c + 1, :], (8, RECV)) for c in range(LAGS_X)] for p in range(LAGS_T)]
    for u in range(WROWS):
        sums = [None] * LAGS_X
        for p in range(LAGS_T):
            value = trace_ref[8 * (u + p) : 8 * (u + p) + 8, :]
            for c in range(LAGS_X):
                term = taps[p][c] * value
                sums[c] = term if sums[c] is None else sums[c] + term
        ahead = jnp.where(recv < RECV - 1, pltpu.roll(sums[0], RECV - 1, 1), 0.0)
        behind = jnp.where(recv > 0, pltpu.roll(sums[2], 1, 1), 0.0)
        value = recorded_ref[u].astype(F32) - (sums[1] + ahead + behind)
        out_ref[u] = (value * keep_ref[u : u + 1, :]).astype(BF16)


def call(kernel, out_shape, args, specs, scratch=(), flops=1000000):
    return pl.pallas_call(
        kernel,
        out_shape=out_shape,
        in_specs=specs,
        out_specs=jax.tree.map(lambda _: VMEM, out_shape),
        scratch_shapes=list(scratch),
        compiler_params=pltpu.CompilerParams(vmem_limit_bytes=32 * 2**20),
        cost_estimate=pl.CostEstimate(flops=flops, bytes_accessed=1000000, transcendentals=0),
    )(*args)


def body(data, recip, gap, owner, weights, start_row, end_row, recorded):
    freq_here = lax.axis_index("freq")
    src_count = lax.axis_size("pair") * lax.axis_size("half")
    pairs = src_count // 2
    total_out = weights.shape[3]
    points = data.shape[3]

    recip_rows = jnp.swapaxes(recip[:, 0], 1, 2).reshape(2 * NEAR, RECV)
    depth = points // 2
    parts = pl.pallas_call(
        main_product,
        grid=(points // depth,),
        out_shape=jax.ShapeDtypeStruct((pairs, 2, SLOT_ROWS, RECV), BF16),
        in_specs=[
            pl.BlockSpec((NEAR, RECV), lambda k: (0, 0)),
            pl.BlockSpec((2 * NEAR, RECV), lambda k: (0, 0)),
            pl.BlockSpec((2, 1, RECV, depth), lambda k: (0, 0, 0, k)),
            pl.BlockSpec((2, 1, depth, total_out), lambda k: (0, 0, k, 0)),
        ],
        out_specs=pl.BlockSpec((pairs, 2, SLOT_ROWS, RECV), lambda k: (0, 0, 0, 0)),
        scratch_shapes=[
            pltpu.VMEM((2, RECV, total_out), F32),
            pltpu.VMEM((RECV, RECV), BF16),
            pltpu.VMEM((pairs, NEAR, RECV), F32),
        ],
        cost_estimate=pl.CostEstimate(flops=8 * RECV * points * total_out, bytes_accessed=5000000, transcendentals=0),
    )(gap.T, recip_rows, data, weights)
    parts = parts.reshape(src_count, SLOT_ROWS, RECV)
    parts = lax.all_to_all(parts, ("pair", "half"), 0, 0, tiled=True)
    begin = freq_here * T_DEV - HALO
    first, last = start_row[0] - begin, end_row[0] - begin
    row = lax.broadcasted_iota(jnp.int32, (WROWS, RECV), 0)
    keep_rows = ((row >= first) & (row < last)).astype(F32)
    row = jnp.arange(AROWS, dtype=jnp.int32) // GROUP - LEAD
    keep = (row >= first) & (row < last)
    rows = lax.dynamic_index_in_dim(jnp.asarray(phase_rows()), freq_here, 0, keepdims=False)
    rows = jnp.where(keep[:, None], rows, jnp.zeros_like(rows))
    target = jnp.pad(recorded.reshape(WROWS, -1), ((0, 16), (0, 0)))

    copies = call(
        sum_and_fill,
        jax.ShapeDtypeStruct((NF, 2, 8, RECV), F32),
        (jnp.broadcast_to(owner[None], (8, src_count)), parts, keep_rows, rows, target),
        [VMEM, VMEM, ANY, ANY, ANY],
        [
            pltpu.VMEM((NEAR * src_count, RECV), BF16),
            pltpu.VMEM((NEAR * src_count, RECV), BF16),
            pltpu.VMEM((RECV, RECV), F32),
        ],
    )
    copies = copies.reshape(NF * 2, 8, RECV)
    spread = lax.all_to_all(copies, ("freq", "half"), 0, 0, tiled=True).reshape(NF * 16, RECV)

    trace_rows = 8 * (WROWS + 2 * LEAD)
    gram, trace = call(
        trace_and_gram,
        (jax.ShapeDtypeStruct((src_count, 8, RECV), F32), jax.ShapeDtypeStruct((trace_rows, RECV), F32)),
        (keep_rows, spread, rows, target),
        [VMEM] * 4,
        [pltpu.VMEM((8 * AROWS, RECV), F32), pltpu.VMEM((GROWS, GROWS), F32)],
    )
    gram = lax.all_to_all(gram, ("pair", "half"), 0, 0, tiled=True)
    damping = float(WROWS * total_out * RECV)
    primaries, filters = call(
        functools.partial(solve_and_filter, damping),
        (jax.ShapeDtypeStruct(recorded.shape, BF16), jax.ShapeDtypeStruct((1, UNKNOWNS), F32)),
        (keep_rows, gram, trace, recorded),
        [VMEM] * 4,
        [pltpu.VMEM((SIDE, RECV), F32)],
    )
    return primaries, filters


def solution(mesh):
    freq, src = mesh.devices.shape
    mesh = Mesh(mesh.devices.reshape(freq, src // 2, 2), ("freq", "pair", "half"))
    src = ("pair", "half")
    placed = (
        P(None, "freq", None, src),
        P(None, "freq", None, src),
        P(None, src),
        P(),
        P(None, "freq", src, None),
        P("freq"),
        P("freq"),
        P("freq", src, None),
    )
    return jax.shard_map(
        body,
        mesh=mesh,
        in_specs=placed,
        out_specs=(P("freq", src, None), P("freq", None)),
        check_vma=False,
    )
```

```python
import functools
import math

import jax
import jax.numpy as jnp
import ml_dtypes
import numpy as np
from jax import lax
from jax.experimental import pallas as pl
from jax.experimental.pallas import tpu as pltpu
from jax.sharding import Mesh, PartitionSpec as P

RECV = 128
NFFT = 512
F_LOW = 40
NEAR = 16
HALO = 8
LAGS_T = 9
LAGS_X = 3
LEAD = LAGS_T // 2
T_DEV = 32
WROWS = T_DEV + 2 * HALO
NF = 16
GROUP = 4
GROWS = 256
AROWS = GROUP * (WROWS + 2 * LEAD)
SIDE = 40
UNKNOWNS = LAGS_T * LAGS_X
TARGET_COL = GROUP * LEAD + 3
CENTRE_ROW = GROUP * LEAD + 1
PACK_AT = (0, 40, 72, 96, 112)
RECIP_AT, GAP_AT, SLOT_ROWS = 16, 32, 48
HALF = RECV // 2
IMAG_AT, SCALE_AT = HALF + 16, HALF + 32
SPAN = 166.0
VMEM = pl.BlockSpec(memory_space=pltpu.VMEM)
ANY = pl.BlockSpec(memory_space=pl.ANY)
F32 = jnp.float32
BF16 = jnp.bfloat16


def split3(x):
    high = x.astype(ml_dtypes.bfloat16)
    rest = x - high.astype(np.float32)
    mid = rest.astype(ml_dtypes.bfloat16)
    low = (rest - mid.astype(np.float32)).astype(ml_dtypes.bfloat16)
    return high, mid, low


@functools.cache
def phase_rows():
    table = np.zeros((NF, AROWS, 256), ml_dtypes.bfloat16)
    freqs = np.arange(NF)
    scale = 1.0 / math.sqrt(NF)
    for window in range(NF):
        for row in range(WROWS):
            time = window * T_DEV - HALO + row
            if not 0 <= time < NFFT:
                continue
            turns = (F_LOW + freqs) * time % NFFT
            angle = turns * (2.0 * math.pi / NFFT)
            phase = np.stack([np.cos(angle), -np.sin(angle)], axis=0).reshape(-1) * scale
            high, mid, low = split3(phase.astype(np.float32))
            at = GROUP * (row + LEAD)
            table[window, at : at + 3, :192] = np.concatenate([high, high, mid, high, low, mid])
            table[window, at + 3, 192 + row] = 1
    return table


def halves(first, second):
    lanes = lax.broadcasted_iota(jnp.int32, first.shape, 1)
    low = jnp.where(lanes < HALF, first, pltpu.roll(second, HALF, 1))
    return low, jnp.where(lanes < HALF, pltpu.roll(first, HALF, 1), second)


def encode(value, scale):
    size = jnp.exp(jnp.abs(value) * (SPAN / scale) - SPAN / 2)
    return jnp.where(value < 0, -size, size)


def decode(code, scale):
    size = (jnp.log(jnp.abs(code)) + SPAN / 2) * (scale * (1.0 / SPAN))
    return jnp.where(code < 0, -size, size)


def main_product(gap_ref, recip_ref, data_ref, weights_ref, out_ref, acc_ref, mask_ref, near_ref):
    step = pl.program_id(0)
    depth = data_ref.shape[3]
    pairs = out_ref.shape[0]

    @pl.when(step == 0)
    def _():
        acc_ref[...] = jnp.zeros_like(acc_ref)
        gap = jnp.where(gap_ref[...] == 1, 1.0, 0.0)
        full = jnp.concatenate([gap, jnp.zeros((RECV - NEAR, RECV), F32)], axis=0)
        mask_ref[...] = (1.0 - full.T).astype(BF16)
        recip = recip_ref[...].astype(F32)
        recip = halves(recip[:NEAR], recip[NEAR:])
        lanes = lax.broadcasted_iota(jnp.int32, (NEAR, RECV), 1)
        for half in range(2):
            out_ref[:, half, RECIP_AT:GAP_AT] = jnp.broadcast_to(
                recip[half].astype(BF16)[None], (pairs, NEAR, RECV)
            )
        for pair in range(pairs):
            at, off = RECV * (pair // 8), 16 * (pair % 8)
            real = weights_ref[0, 0, :NEAR, at : at + RECV].astype(F32)
            imag = weights_ref[1, 0, :NEAR, at : at + RECV].astype(F32)
            real = pltpu.roll(real, (HALF - off) % RECV, 1)
            imag = pltpu.roll(imag, (IMAG_AT - off) % RECV, 1)
            near_ref[pair] = jnp.where(lanes < IMAG_AT, real, imag)

    @pl.when(step == 1)
    def _():
        mask_ref[...] = jnp.ones_like(mask_ref)

    panel = data_ref[...].reshape(2 * RECV, depth)
    mask = mask_ref[...]
    near = panel[:, :RECV] * jnp.concatenate([mask, mask], axis=0)
    panel = jnp.concatenate([near, panel[:, RECV:]], axis=1)
    both = jnp.concatenate([weights_ref[0, 0], weights_ref[1, 0]], axis=1)
    product = jnp.dot(panel, both, preferred_element_type=F32)
    width = product.shape[1] // 2
    acc_ref[0] += product[:RECV, :width] - product[RECV:, width:]
    acc_ref[1] += product[:RECV, width:] + product[RECV:, :width]

    @pl.when(step == pl.num_programs(0) - 1)
    def _():
        gap = jnp.where(gap_ref[...] == 1, 1.0, 0.0)
        gaps = gap, pltpu.roll(gap, HALF, 1)
        lanes = lax.broadcasted_iota(jnp.int32, (pairs, NEAR, RECV), 2)
        for half, pred in enumerate(halves(acc_ref[0].T, acc_ref[1].T)):
            pred = pred.reshape(pairs, 16, RECV)
            scale = jnp.max(jnp.abs(pred), axis=(1, 2), keepdims=True) * 1.01 + 1e-30
            scale = scale.astype(BF16).astype(F32)
            out_ref[:, half, :RECIP_AT] = encode(pred, scale).astype(BF16)
            tile = jnp.where(lanes < SCALE_AT, near_ref[...], jnp.broadcast_to(scale, lanes.shape))
            tile = jnp.where(lanes < HALF, jnp.broadcast_to(gaps[half][None], lanes.shape), tile)
            out_ref[:, half, GAP_AT:] = tile.astype(BF16)


def sum_and_fill(owner_ref, part_ref, keep_ref, rows_ref, target_ref, out_ref, z_ref, w_ref, f_ref):
    del keep_ref, rows_ref, target_ref
    slots = part_ref.shape[0]
    total = jnp.zeros((16, RECV), F32)
    for j in range(slots):
        scale = part_ref[j, GAP_AT:].astype(F32)[:, SCALE_AT : SCALE_AT + 1]
        code = part_ref[j, :RECIP_AT].astype(F32)
        total = total + decode(code, jnp.broadcast_to(scale, code.shape))
    lanes = lax.broadcasted_iota(jnp.int32, (NEAR, RECV), 1)
    for j in range(slots):
        tile = part_ref[owner_ref[0, j], GAP_AT:]
        gap = tile.astype(F32)
        gap = jnp.where(lanes < HALF, gap, pltpu.roll(gap, HALF, 1))
        at = slice(NEAR * j, NEAR * j + NEAR)
        z_ref[at, :] = (part_ref[j, RECIP_AT:GAP_AT].astype(F32) * gap).astype(BF16)
        w_ref[at, :] = tile
    f_ref[...] = lax.dot_general(
        w_ref[...], z_ref[...], (((0,), (0,)), ((), ())), preferred_element_type=F32
    )
    by_real = f_ref[HALF:IMAG_AT, :]
    by_imag = pltpu.roll(f_ref[IMAG_AT:SCALE_AT, :], HALF, 1)
    pred = total + by_real + jnp.where(lanes < HALF, -by_imag, by_imag)
    out_ref[...] = jnp.broadcast_to(pred.reshape(1, 2, 8, RECV), out_ref.shape)


def two_parts(x):
    high = x.astype(BF16)
    return high, (x - high.astype(F32)).astype(BF16)


def trace_and_gram(keep_ref, x_ref, rows_ref, target_ref, gram_ref, trace_ref, a_ref, g_ref):
    sources = 8
    columns = []
    for s in range(sources):
        low, high = (x_ref[pl.ds(8 * half + s, NF, stride=16), :] for half in range(2))
        columns.append(jnp.concatenate(halves(low, high), axis=0))
    x = jnp.concatenate(columns, axis=1)
    high, rest = x.astype(BF16), x
    rest = rest - high.astype(F32)
    mid = rest.astype(BF16)
    low = (rest - mid.astype(F32)).astype(BF16)
    stack = jnp.concatenate([high, mid, high, low, high, mid, target_ref[...]], axis=0)
    base = jnp.dot(rows_ref[...], stack, preferred_element_type=F32)
    times = AROWS // GROUP
    recv = lax.broadcasted_iota(jnp.int32, (times, RECV), 1)
    for s in range(sources):
        a_ref[s * AROWS : (s + 1) * AROWS, :] = base[:, s * RECV : (s + 1) * RECV]
    for s in range(sources):
        ahead = pl.ds(s * AROWS, times, stride=GROUP)
        a_ref[ahead, :] = jnp.where(recv < RECV - 1, pltpu.roll(a_ref[ahead, :], RECV - 1, 1), 0.0)
        behind = pl.ds(s * AROWS + 2, times, stride=GROUP)
        a_ref[behind, :] = jnp.where(recv > 0, pltpu.roll(a_ref[behind, :], 1, 1), 0.0)
    for s in range(sources):
        mine = a_ref[pl.ds(s * AROWS + 1, WROWS + 2 * LEAD, stride=GROUP), :]
        trace_ref[pl.ds(s, WROWS + 2 * LEAD, stride=sources), :] = mine
    high, low = two_parts(jnp.concatenate([a_ref[s * AROWS : (s + 1) * AROWS, :] for s in range(sources)], axis=1))
    dims = (((1,), (1,)), ((), ()))
    rest = jnp.zeros((GROWS - AROWS, high.shape[1]), BF16)
    wide, narrow = (jnp.concatenate([part, rest], axis=0) for part in (high, low))
    g_ref[:AROWS] = lax.dot_general(high, wide, dims, preferred_element_type=F32) + 2.0 * lax.dot_general(
        high, narrow, dims, preferred_element_type=F32
    )
    g_ref[AROWS:] = jnp.zeros((GROWS - AROWS, GROWS), F32)
    total = jnp.zeros((SIDE, RECV), F32)
    for u in range(WROWS):
        at = GROUP * u
        if at + SIDE <= RECV:
            part = g_ref[at : at + SIDE, :RECV]
            part = pltpu.roll(part, (RECV - at) % RECV, 1)
        elif at >= RECV:
            part = g_ref[at : at + SIDE, RECV:]
            part = pltpu.roll(part, (2 * RECV - at) % RECV, 1)
        else:
            lane = lax.broadcasted_iota(jnp.int32, (SIDE, RECV), 1)
            part = jnp.where(lane >= at, g_ref[at : at + SIDE, :RECV], g_ref[at : at + SIDE, RECV:])
            part = pltpu.roll(part, RECV - at, 1)
        total = total + part * keep_ref[u : u + 1, :]
    full = jnp.concatenate([total, jnp.zeros((RECV - SIDE, RECV), F32)], axis=0)
    total = 0.5 * (total + full.T[:SIDE])
    lanes = lax.broadcasted_iota(jnp.int32, (8, RECV), 1)
    packed = jnp.zeros((8, RECV), F32)
    for g, at in enumerate(PACK_AT):
        piece = total[8 * g : 8 * g + 8]
        piece = jnp.where((lanes >= 8 * g) & (lanes < SIDE), piece, 0.0)
        packed = packed + pltpu.roll(piece, at - 8 * g, 1)
    gram_ref[...] = jnp.broadcast_to(packed[None], gram_ref.shape)


def solve_and_filter(damping, keep_ref, gram_ref, trace_ref, recorded_ref, out_ref, filters_ref, h_ref):
    packed = jnp.sum(gram_ref[...], axis=0)
    lanes = lax.broadcasted_iota(jnp.int32, (8, RECV), 1)
    pieces = []
    for g, at in enumerate(PACK_AT):
        piece = pltpu.roll(packed, (RECV + 8 * g - at) % RECV, 1)
        pieces.append(jnp.where((lanes >= 8 * g) & (lanes < SIDE), piece, 0.0))
    upper = jnp.concatenate(pieces, axis=0)
    full = jnp.concatenate([upper, jnp.zeros((RECV - SIDE, RECV), F32)], axis=0)
    row = lax.broadcasted_iota(jnp.int32, (SIDE, RECV), 0)
    lane = lax.broadcasted_iota(jnp.int32, (SIDE, RECV), 1)
    system = jnp.where(lane // 8 < row // 8, full.T[:SIDE], upper)
    unknown = lax.rem(row, GROUP) < LAGS_X
    system = system + jnp.where((row == lane) & unknown, damping, 0.0)
    system = system + jnp.where((row == CENTRE_ROW) & (lane == TARGET_COL), damping, 0.0)
    order = [k for k in range(GROUP * LAGS_T) if k % GROUP < LAGS_X]
    for one, two in zip(order[:-1:2], order[1::2]):
        first = jnp.broadcast_to(system[:, one : one + 1], (SIDE, RECV))
        second = jnp.broadcast_to(system[:, two : two + 1], (SIDE, RECV))
        top, bottom = system[one : one + 1, :], system[two : two + 1, :]
        a, b, d = first[one : one + 1], second[one : one + 1], second[two : two + 1]
        scale = 1.0 / (a * d - b * b)
        top, bottom = (d * top - b * bottom) * scale, (a * bottom - b * top) * scale
        rest = system - first * top - second * bottom
        system = jnp.where(row == one, top, jnp.where(row == two, bottom, rest))
    last = order[-1]
    column = jnp.broadcast_to(system[:, last : last + 1], (SIDE, RECV))
    pivot_row = system[last : last + 1, :] / column[last : last + 1]
    system = jnp.where(row == last, pivot_row, system - column * pivot_row)
    chosen = (lane < UNKNOWNS) & (row == GROUP * (LAGS_T - 1 - lane // LAGS_X) + lane % LAGS_X)
    h_ref[...] = jnp.broadcast_to(system[:, TARGET_COL : TARGET_COL + 1], (SIDE, RECV))
    filters_ref[...] = jnp.sum(jnp.where(chosen, h_ref[...], 0.0), axis=0, keepdims=True)[:, :UNKNOWNS]
    recv = lax.broadcasted_iota(jnp.int32, (8, RECV), 1)
    taps = [[jnp.broadcast_to(h_ref[GROUP * p + c : GROUP * p + c + 1, :], (8, RECV)) for c in range(LAGS_X)] for p in range(LAGS_T)]
    for u in range(WROWS):
        sums = [None] * LAGS_X
        for p in range(LAGS_T):
            value = trace_ref[8 * (u + p) : 8 * (u + p) + 8, :]
            for c in range(LAGS_X):
                term = taps[p][c] * value
                sums[c] = term if sums[c] is None else sums[c] + term
        ahead = jnp.where(recv < RECV - 1, pltpu.roll(sums[0], RECV - 1, 1), 0.0)
        behind = jnp.where(recv > 0, pltpu.roll(sums[2], 1, 1), 0.0)
        value = recorded_ref[u].astype(F32) - (sums[1] + ahead + behind)
        out_ref[u] = (value * keep_ref[u : u + 1, :]).astype(BF16)


def call(kernel, out_shape, args, specs, scratch=(), flops=1000000):
    return pl.pallas_call(
        kernel,
        out_shape=out_shape,
        in_specs=specs,
        out_specs=jax.tree.map(lambda _: VMEM, out_shape),
        scratch_shapes=list(scratch),
        compiler_params=pltpu.CompilerParams(vmem_limit_bytes=32 * 2**20),
        cost_estimate=pl.CostEstimate(flops=flops, bytes_accessed=1000000, transcendentals=0),
    )(*args)


def body(data, recip, gap, owner, weights, start_row, end_row, recorded):
    freq_here = lax.axis_index("freq")
    src_count = lax.axis_size("pair") * lax.axis_size("half")
    pairs = src_count // 2
    total_out = weights.shape[3]
    points = data.shape[3]

    recip_rows = jnp.swapaxes(recip[:, 0], 1, 2).reshape(2 * NEAR, RECV)
    depth = points // 2
    parts = pl.pallas_call(
        main_product,
        grid=(points // depth,),
        out_shape=jax.ShapeDtypeStruct((pairs, 2, SLOT_ROWS, RECV), BF16),
        in_specs=[
            pl.BlockSpec((NEAR, RECV), lambda k: (0, 0)),
            pl.BlockSpec((2 * NEAR, RECV), lambda k: (0, 0)),
            pl.BlockSpec((2, 1, RECV, depth), lambda k: (0, 0, 0, k)),
            pl.BlockSpec((2, 1, depth, total_out), lambda k: (0, 0, k, 0)),
        ],
        out_specs=pl.BlockSpec((pairs, 2, SLOT_ROWS, RECV), lambda k: (0, 0, 0, 0)),
        scratch_shapes=[
            pltpu.VMEM((2, RECV, total_out), F32),
            pltpu.VMEM((RECV, RECV), BF16),
            pltpu.VMEM((pairs, NEAR, RECV), F32),
        ],
        cost_estimate=pl.CostEstimate(flops=8 * RECV * points * total_out, bytes_accessed=5000000, transcendentals=0),
    )(gap.T, recip_rows, data, weights)
    parts = parts.reshape(src_count, SLOT_ROWS, RECV)
    parts = lax.all_to_all(parts, ("pair", "half"), 0, 0, tiled=True)
    begin = freq_here * T_DEV - HALO
    first, last = start_row[0] - begin, end_row[0] - begin
    row = lax.broadcasted_iota(jnp.int32, (WROWS, RECV), 0)
    keep_rows = ((row >= first) & (row < last)).astype(F32)
    row = jnp.arange(AROWS, dtype=jnp.int32) // GROUP - LEAD
    keep = (row >= first) & (row < last)
    rows = lax.dynamic_index_in_dim(jnp.asarray(phase_rows()), freq_here, 0, keepdims=False)
    rows = jnp.where(keep[:, None], rows, jnp.zeros_like(rows))
    target = jnp.pad(recorded.reshape(WROWS, -1), ((0, 16), (0, 0)))

    copies = call(
        sum_and_fill,
        jax.ShapeDtypeStruct((NF, 2, 8, RECV), F32),
        (jnp.broadcast_to(owner[None], (8, src_count)), parts, keep_rows, rows, target),
        [VMEM, VMEM, ANY, ANY, ANY],
        [
            pltpu.VMEM((NEAR * src_count, RECV), BF16),
            pltpu.VMEM((NEAR * src_count, RECV), BF16),
            pltpu.VMEM((RECV, RECV), F32),
        ],
    )
    copies = copies.reshape(NF * 2, 8, RECV)
    spread = lax.all_to_all(copies, ("freq", "half"), 0, 0, tiled=True).reshape(NF * 16, RECV)

    trace_rows = 8 * (WROWS + 2 * LEAD)
    gram, trace = call(
        trace_and_gram,
        (jax.ShapeDtypeStruct((src_count, 8, RECV), F32), jax.ShapeDtypeStruct((trace_rows, RECV), F32)),
        (keep_rows, spread, rows, target),
        [VMEM] * 4,
        [pltpu.VMEM((8 * AROWS, RECV), F32), pltpu.VMEM((GROWS, GROWS), F32)],
    )
    gram = lax.all_to_all(gram, ("pair", "half"), 0, 0, tiled=True)
    damping = float(WROWS * total_out * RECV)
    primaries, filters = call(
        functools.partial(solve_and_filter, damping),
        (jax.ShapeDtypeStruct(recorded.shape, BF16), jax.ShapeDtypeStruct((1, UNKNOWNS), F32)),
        (keep_rows, gram, trace, recorded),
        [VMEM] * 4,
        [pltpu.VMEM((SIDE, RECV), F32)],
    )
    return primaries, filters


def solution(mesh):
    freq, src = mesh.devices.shape
    mesh = Mesh(mesh.devices.reshape(freq, src // 2, 2), ("freq", "pair", "half"))
    src = ("pair", "half")
    placed = (
        P(None, "freq", None, src),
        P(None, "freq", None, src),
        P(None, src),
        P(),
        P(None, "freq", src, None),
        P("freq"),
        P("freq"),
        P("freq", src, None),
    )
    return jax.shard_map(
        body,
        mesh=mesh,
        in_specs=placed,
        out_specs=(P("freq", src, None), P("freq", None)),
        check_vma=False,
    )
```
